128 devices in a mesh: dp: 16 (over y_lo, x, core), space: 8 (over z, y_hi).
Axes of the slice: x: 4, y: 4 (y_hi: 2, y_lo: 2; y = y_hi * 2 + y_lo), z: 4, core: 2. Of those that a mesh axis runs over, the one named last changes fastest.
Arguments:
- inputs: bfloat16 [16, 1, 64, 240, 320], P('dp', None, 'space'), may hold values from -6 to 6
- preacts: bfloat16 [1, 16, 1, 64, 240, 320], P(None, 'dp', None, 'space'), may hold values from -6 to 6
- cotangent: bfloat16 [16, 1, 64, 240, 320], P('dp', None, 'space'), may hold values from -0.01171875 to 0.01171875
- weights: bfloat16 [1, 2880, 320], replicated, may hold values from -0.109375 to 0.109375
- left_stats: float32 [2, 2880, 2880], P(None, 'space', 'dp'), as said below
- left_basis: float32 [2, 2880, 320], P(None, 'dp'), may hold values from -6 to 6
- right_stats: float32 [2, 320, 320], replicated, as said below
- right_basis: float32 [2, 320, 320], replicated, as said below
Outputs:
- left_out: float32 [2, 2880, 2880], P(None, 'space', 'dp')
- basis_out: float32 [2, 2880, 320], replicated
- right_out: float32 [2, 320, 320], replicated
- right_basis_out: float32 [2, 320, 320], replicated
The draws below stay inside these ranges and needn't reach their ends.
Inputs may be any that keep to these rules, and one draw needn't show every extreme that they name: `left_stats`: each matrix is symmetric positive definite. `right_stats`: each matrix is symmetric positive definite. `right_basis`: each matrix is invertible.
All inputs are finite; a program needn't handle non-finite values.
Results may differ from the reference program's by a relative error of at most 0.0014.
Values may be sent and summed in bfloat16 or wider, within the bound.
A program may use at most 128 MiB of HBM per device.

```python
import math
import jax
import jax.numpy as jnp
from jax import lax

CH = 320
KDIM = 2880
KB = 320
LAYERS = 2
FRAMES = 1
WID = 240
CLIPS = 16
HEIGHT = 64
CELLS_ALL = 245760


def definite_draw(key, order, base):
    noise_key, scale_key = jax.random.split(key)
    noise_draw = jax.random.normal(noise_key, (LAYERS, order, order), jnp.float32)
    mirror = (noise_draw + jnp.swapaxes(noise_draw, 1, 2)) * (0.25 / math.sqrt(2.0 * order))
    position_ramp = jnp.arange(order, dtype=jnp.float32) / order
    spread = jax.random.uniform(scale_key, (LAYERS, order), jnp.float32, 0.0, math.log(2.0))
    scales = base * jnp.exp(math.log(3.0) * position_ramp[None, :] + spread)
    root_scales = jnp.sqrt(scales)
    identity_mask = (jnp.arange(order)[:, None] == jnp.arange(order)[None, :]).astype(jnp.float32)
    return root_scales[:, :, None] * root_scales[:, None, :] * (identity_mask + mirror)


def draw_left_stats(key, part):
    return definite_draw(key, KDIM, 1.0)


def draw_right_stats(key, part):
    return definite_draw(key, CH, 20.0)


def draw_right_basis(key, part):
    perturb = jax.random.normal(key, (LAYERS, CH, CH), jnp.float32)
    identity_mask = (jnp.arange(CH)[:, None] == jnp.arange(CH)[None, :]).astype(jnp.float32)
    return math.sqrt(CH) * (identity_mask[None] + perturb * (0.25 / math.sqrt(CH)))


def block_scale(stream_key, dims, cuts, least, high):
    def one(axis_at, shards_of):
        heights = jax.random.uniform(jax.random.fold_in(jax.random.fold_in(stream_key, 6), axis_at), (shards_of,), jnp.float32, least / len(cuts), high / len(cuts))
        return jnp.repeat(jnp.exp(heights), dims[axis_at] // shards_of).reshape((-1,) + (1,) * (len(dims) - axis_at - 1))

    loudness = one(*cuts[0])
    for cut in cuts[1:]:
        loudness = loudness * one(*cut)
    return loudness


def scatter_about(key, extent, width, bound, pieces=(), kind=jnp.bfloat16):
    level = block_scale(key, extent, pieces, -0.22, 0.18) if pieces else 1.0
    drawn = jax.random.normal(key, extent, jnp.float32) * width * level
    return jnp.minimum(jnp.maximum(drawn, -bound), bound).astype(kind)


def setup_inputs(seed: int = 0) -> dict:
    key_of = jax.random.split(jax.random.key(seed), 9)
    inputs = scatter_about(key_of[0], (CLIPS, FRAMES, HEIGHT, WID, CH), 1.0, 6.0, ((0, 16), (2, 8)))
    preacts = scatter_about(key_of[1], (LAYERS - 1, CLIPS, FRAMES, HEIGHT, WID, CH), 1.0, 6.0, ((1, 16), (3, 8)))
    cotangent = scatter_about(key_of[2], (CLIPS, FRAMES, HEIGHT, WID, CH), CELLS_ALL ** -0.5, 0.01171875, ((0, 16), (2, 8)))
    weights = scatter_about(key_of[3], (LAYERS - 1, KDIM, CH), KDIM ** -0.5, 0.109375)
    left_stats = draw_left_stats(jax.random.fold_in(key_of[8], 71), 0)
    left_basis = scatter_about(key_of[5], (LAYERS, KDIM, KB), 1.0, 6.0, ((1, 16),), jnp.float32)
    right_stats = draw_right_stats(jax.random.fold_in(key_of[8], 71), 0)
    right_basis = draw_right_basis(jax.random.fold_in(key_of[8], 71), 0)
    return {"inputs": inputs, "preacts": preacts, "cotangent": cotangent, "weights": weights, "left_stats": left_stats, "left_basis": left_basis, "right_stats": right_stats, "right_basis": right_basis}


BETA = 0.95
HIGHEST = lax.Precision.HIGHEST
OFFSETS = (-1, 0, 1)
CONTRACT_ROWS = (((0,), (0,)), ((), ()))
CONTRACT_COLS = (((1,), (1,)), ((), ()))

def silu_slope(preact):
    argument = preact.astype(jnp.float32)
    logistic = jax.nn.sigmoid(argument)
    return logistic * (1.0 + argument * (1.0 - logistic))

def weight_grad(layer_input, layer_grad):
    row_count, col_count, channels = (layer_grad.shape[2], layer_grad.shape[3], layer_grad.shape[4])
    padded = jnp.pad(layer_input, ((0, 0), (0, 0), (1, 1), (1, 1), (0, 0)))
    flat_grad = layer_grad.reshape(-1, channels)
    blocks = []
    for row_step in OFFSETS:
        for col_step in OFFSETS:
            shifted = padded[:, :, 1 + row_step:1 + row_step + row_count, 1 + col_step:1 + col_step + col_count, :]
            blocks.append(lax.dot_general(shifted.reshape(-1, channels).astype(jnp.float32), flat_grad.astype(jnp.float32), CONTRACT_ROWS, preferred_element_type=jnp.float32))
    return jnp.concatenate(blocks, axis=0)

def input_grad(layer_grad, weight):
    row_count, col_count, channels = (layer_grad.shape[2], layer_grad.shape[3], layer_grad.shape[4])
    padded = jnp.pad(layer_grad, ((0, 0), (0, 0), (1, 1), (1, 1), (0, 0)))
    summed = jnp.zeros((layer_grad.size // channels, channels), jnp.float32)
    tap_number = 0
    for row_step in OFFSETS:
        for col_step in OFFSETS:
            shifted = padded[:, :, 1 - row_step:1 - row_step + row_count, 1 - col_step:1 - col_step + col_count, :]
            weight_tap = weight[tap_number * channels:(tap_number + 1) * channels]
            summed = summed + lax.dot_general(shifted.reshape(-1, channels).astype(jnp.float32), weight_tap.astype(jnp.float32), CONTRACT_COLS, preferred_element_type=jnp.float32)
            tap_number += 1
    return summed.reshape(layer_grad.shape)

def orthonormal(product_rows, gram_matrix, factor):
    lower_factor = jnp.linalg.cholesky(gram_matrix)
    solved = jax.scipy.linalg.solve_triangular(lower_factor, product_rows.T, lower=True)
    return solved.T * factor

def reference(inputs, preacts, cotangent, weights, left_stats, left_basis, right_stats, right_basis):
    layer_inputs = [inputs] + [jax.nn.silu(preacts[layer_num].astype(jnp.float32)).astype(jnp.bfloat16) for layer_num in range(LAYERS - 1)]
    left_outs = [None] * LAYERS
    basis_outs = [None] * LAYERS
    right_outs = [None] * LAYERS
    turned_outs = [None] * LAYERS
    current = cotangent
    for layer_num in range(LAYERS - 1, -1, -1):
        gradient = weight_grad(layer_inputs[layer_num], current)
        if layer_num > 0:
            backward = input_grad(current, weights[layer_num - 1])
            current = (backward * silu_slope(preacts[layer_num - 1])).astype(jnp.bfloat16)
        left_new = BETA * left_stats[layer_num] + (1.0 - BETA) * lax.dot_general(gradient, gradient, CONTRACT_COLS, precision=HIGHEST)
        right_new = BETA * right_stats[layer_num] + (1.0 - BETA) * lax.dot_general(gradient, gradient, CONTRACT_ROWS, precision=HIGHEST)
        product_rows = jnp.dot(left_new, left_basis[layer_num], precision=HIGHEST)
        gram_left = lax.dot_general(product_rows, product_rows, CONTRACT_ROWS, precision=HIGHEST)
        right_rows = jnp.dot(right_new, right_basis[layer_num], precision=HIGHEST)
        right_gram = lax.dot_general(right_rows, right_rows, CONTRACT_ROWS, precision=HIGHEST)
        left_outs[layer_num] = left_new
        basis_outs[layer_num] = orthonormal(product_rows, gram_left, math.sqrt(KDIM))
        right_outs[layer_num] = right_new
        turned_outs[layer_num] = orthonormal(right_rows, right_gram, math.sqrt(CH))
    return (jnp.stack(left_outs), jnp.stack(basis_outs), jnp.stack(right_outs), jnp.stack(turned_outs))
```

```python
import math

import jax
import jax.numpy as jnp
from jax import lax
from jax.experimental import pallas as pl
from jax.experimental.pallas import tpu as pltpu
from jax.sharding import PartitionSpec as P

BETA = 0.95
HIGHEST = lax.Precision.HIGHEST
OFFSETS = (-1, 0, 1)
CONTRACT_ROWS = (((0,), (0,)), ((), ()))
CONTRACT_COLS = (((1,), (1,)), ((), ()))


def padded_2(array, sides, width):
    for axis, dim in sides:
        size, length = (lax.axis_size(axis), array.shape[dim])
        up = [(i, (i + 1) % size) for i in range(size - 1)]
        down = [(j, i) for i, j in up]
        last = lax.slice_in_dim(array, length - width, length, axis=dim)
        first = lax.slice_in_dim(array, 0, width, axis=dim)
        before = lax.ppermute(last, axis, up)
        after = lax.ppermute(first, axis, down)
        array = jnp.concatenate([before, array, after], axis=dim)
    return array


def silu_slope(preact):
    argument = preact.astype(jnp.float32)
    logistic = jax.nn.sigmoid(argument)
    return logistic * (1.0 + argument * (1.0 - logistic))


def widen(with_rows):
    return jnp.pad(with_rows, ((0, 0), (0, 0), (0, 0), (1, 1), (0, 0)))


def weight_grad(input_rims, layer_grad):
    row_count, col_count, channels = (layer_grad.shape[2], layer_grad.shape[3], layer_grad.shape[4])
    padded = widen(input_rims)
    flat_grad = layer_grad.reshape(-1, channels)
    blocks = []
    for row_step in OFFSETS:
        for col_step in OFFSETS:
            shifted = padded[
                :,
                :,
                1 + row_step : 1 + row_step + row_count,
                1 + col_step : 1 + col_step + col_count,
                :,
            ]
            blocks.append(
                lax.dot_general(
                    shifted.reshape(-1, channels),
                    flat_grad,
                    CONTRACT_ROWS,
                    preferred_element_type=jnp.float32,
                )
            )
    return jnp.concatenate(blocks, axis=0)


def input_grad(grad_rims, weight):
    row_count = grad_rims.shape[2] - 2
    col_count, channels = (grad_rims.shape[3], grad_rims.shape[4])
    padded = widen(grad_rims)
    summed = jnp.zeros(
        (grad_rims.shape[0] * grad_rims.shape[1] * row_count * col_count, channels), jnp.float32
    )
    tap_number = 0
    for row_step in OFFSETS:
        for col_step in OFFSETS:
            shifted = padded[
                :,
                :,
                1 - row_step : 1 - row_step + row_count,
                1 - col_step : 1 - col_step + col_count,
                :,
            ]
            weight_tap = weight[tap_number * channels : (tap_number + 1) * channels]
            summed = summed + lax.dot_general(
                shifted.reshape(-1, channels),
                weight_tap,
                CONTRACT_COLS,
                preferred_element_type=jnp.float32,
            )
            tap_number += 1
    return summed.reshape(grad_rims.shape[0], grad_rims.shape[1], row_count, col_count, channels)


NB = 64

def diag_inverse(blocks):
    n = NB
    row = lax.broadcasted_iota(jnp.int32, (n, 2 * n), 0)
    col = lax.broadcasted_iota(jnp.int32, (n, 2 * n), 1)
    eye = jnp.where(row + n == col, 1.0, 0.0).astype(jnp.float32)
    tiles = []
    for b in blocks:
        x = jnp.concatenate([b, jnp.zeros((n, n), jnp.float32)], axis=1) + eye
        tiles.append([x[8 * t:8 * t + 8] for t in range(n // 8)])
    sub = lax.broadcasted_iota(jnp.int32, (8, 2 * n), 0)
    scales = [[None] * (n // 8) for _ in blocks]
    for j in range(n):
        tj, sj = j // 8, j % 8
        for m in range(len(blocks)):
            x = tiles[m]
            pivot_row = x[tj][sj:sj + 1, :]
            cb = jnp.broadcast_to(x[tj][:, j:j + 1], (8, 2 * n))
            d = cb[sj:sj + 1, :]
            rs = lax.rsqrt(d)
            scales[m][tj] = jnp.where(sub == sj, rs, scales[m][tj] if sj else 0.0)
            scaled = pivot_row * (rs * rs)
            if sj < 7:
                x[tj] = x[tj] - jnp.where(sub > sj, cb, 0.0) * scaled
            for t in range(tj + 1, n // 8):
                x[t] = x[t] - jnp.broadcast_to(x[t][:, j:j + 1], (8, 2 * n)) * scaled
    out = []
    for m in range(len(blocks)):
        w = jnp.concatenate([tiles[m][t] * scales[m][t] for t in range(n // 8)], axis=0)
        out.append(w[:, n:])
    return out

def chol_inv_kernel(g_ref, o_ref):
    nm, size, _ = g_ref.shape
    o_ref[...] = g_ref[...]
    nblk = size // NB
    for k in range(nblk):
        o = k * NB
        linv = diag_inverse([o_ref[m, o:o + NB, o:o + NB] for m in range(nm)])
        for m in range(nm):
            parts = []
            prow = o_ref[m, o:o + NB, :]
            r = jnp.dot(linv[m], prow, precision=HIGHEST, preferred_element_type=jnp.float32)
            pieces = []
            if k: pieces.append(r[:, :o])
            pieces.append(linv[m])
            if k < nblk - 1: pieces.append(r[:, o + NB:])
            rz = jnp.concatenate(pieces, axis=1)
            if k < nblk - 1:
                below = r[:, o + NB:]
                upd = lax.dot_general(below, rz, (((0,), (0,)), ((), ())), precision=HIGHEST, preferred_element_type=jnp.float32)
                old = o_ref[m, o + NB:, :]
                colid = lax.broadcasted_iota(jnp.int32, old.shape, 1)
                old = jnp.where((colid >= o) & (colid < o + NB), 0.0, old)
                o_ref[m, o + NB:, :] = old - upd
                colr = lax.broadcasted_iota(jnp.int32, rz.shape, 1)
                o_ref[m, o:o + NB, :] = jnp.where(colr < o + NB, rz, 0.0)
            else:
                o_ref[m, o:o + NB, :] = rz

def chol_inv(grams):
    return pl.pallas_call(chol_inv_kernel, out_shape=jax.ShapeDtypeStruct(grams.shape, jnp.float32),
        in_specs=[pl.BlockSpec(memory_space=pltpu.VMEM)], out_specs=pl.BlockSpec(memory_space=pltpu.VMEM),
        compiler_params=pltpu.CompilerParams(vmem_limit_bytes=48*1024*1024))(grams)


def with_rims(stacked):
    return padded_2(stacked, (("space", 3),), 1)


def local(inputs, preacts, cotangent, weights, left_stats, left_basis, right_stats, right_basis):
    layer_total = left_stats.shape[0]
    row_share = left_stats.shape[1]
    col_share = left_stats.shape[2]
    channels = inputs.shape[-1]
    full_rows = weights.shape[1]
    dp_index = lax.axis_index("dp")
    space_index = lax.axis_index("space")
    layer_inputs = [inputs] + [jax.nn.silu(preacts[0].astype(jnp.float32)).astype(jnp.bfloat16)]
    left_outs = [None] * layer_total
    basis_outs = [None] * layer_total
    right_outs = [None] * layer_total
    turned_outs = [None] * layer_total

    pieces = [None] * layer_total
    current = cotangent
    for layer_num in range(layer_total - 1, -1, -1):
        if layer_num > 0:
            extended = with_rims(jnp.stack([layer_inputs[layer_num], current]))
            backward = input_grad(extended[1], weights[layer_num - 1])
            following = (backward * silu_slope(preacts[layer_num - 1])).astype(jnp.bfloat16)
        else:
            extended = with_rims(layer_inputs[0][None])
            following = current
        gradient = weight_grad(extended[0], current)
        complete = lax.psum(gradient, ("dp", "space"))
        row_block = lax.dynamic_slice_in_dim(complete, space_index * row_share, row_share, 0)
        col_block = lax.dynamic_slice_in_dim(complete, dp_index * col_share, col_share, 0)
        gram_right = lax.dot_general(row_block, row_block, CONTRACT_ROWS, precision=HIGHEST)
        left_new = BETA * left_stats[layer_num] + (1.0 - BETA) * lax.dot_general(
            row_block, col_block, CONTRACT_COLS, precision=HIGHEST
        )
        left_outs[layer_num] = left_new
        product_rows = lax.psum(jnp.dot(left_new, left_basis[layer_num], precision=HIGHEST), "dp")
        gram_left = lax.dot_general(product_rows, product_rows, CONTRACT_ROWS, precision=HIGHEST)
        summed_left, summed_right = lax.psum((gram_left, gram_right), "space")
        right_new = BETA * right_stats[layer_num] + (1.0 - BETA) * summed_right
        right_rows = jnp.dot(right_new, right_basis[layer_num], precision=HIGHEST)
        right_gram = lax.dot_general(right_rows, right_rows, CONTRACT_ROWS, precision=HIGHEST)
        right_outs[layer_num] = right_new
        pieces[layer_num] = (product_rows, summed_left, right_rows, right_gram)
        current = following
    inverses = chol_inv(
        jnp.stack([p[1] for p in pieces] + [p[3] for p in pieces])
    )
    for i in range(layer_total):
        rows = math.sqrt(full_rows) * lax.dot_general(
            pieces[i][0], inverses[i], CONTRACT_COLS, precision=HIGHEST
        )
        basis_outs[i] = lax.all_gather(rows, "space", axis=0, tiled=True)
        turned_outs[i] = math.sqrt(channels) * lax.dot_general(
            pieces[i][2], inverses[layer_total + i], CONTRACT_COLS, precision=HIGHEST
        )
    return (
        jnp.stack(left_outs),
        jnp.stack(basis_outs),
        jnp.stack(right_outs),
        jnp.stack(turned_outs),
    )


def solution(mesh):
    placed = (
        P("dp", None, "space", None, None),
        P(None, "dp", None, "space", None, None),
        P("dp", None, "space", None, None),
        P(),
        P(None, "space", "dp"),
        P(None, "dp", None),
        P(),
        P(),
    )
    return jax.shard_map(
        local,
        mesh=mesh,
        in_specs=placed,
        out_specs=(P(None, "space", "dp"), P(), P(), P()),
        check_vma=False,
    )
```

```python
import functools
import math

import jax
import jax.numpy as jnp
from jax import lax
from jax.experimental import pallas as pl
from jax.experimental.pallas import tpu as pltpu
from jax.sharding import PartitionSpec as P

BETA = 0.95
HIGHEST = lax.Precision.HIGHEST
OFFSETS = (-1, 0, 1)
CONTRACT_ROWS = (((0,), (0,)), ((), ()))
CONTRACT_COLS = (((1,), (1,)), ((), ()))


def padded_2(array, sides, width):
    for axis, dim in sides:
        size, length = (lax.axis_size(axis), array.shape[dim])
        up = [(i, (i + 1) % size) for i in range(size - 1)]
        down = [(j, i) for i, j in up]
        last = lax.slice_in_dim(array, length - width, length, axis=dim)
        first = lax.slice_in_dim(array, 0, width, axis=dim)
        before = lax.ppermute(last, axis, up)
        after = lax.ppermute(first, axis, down)
        array = jnp.concatenate([before, array, after], axis=dim)
    return array


def silu_slope(preact):
    argument = preact.astype(jnp.float32)
    logistic = jax.nn.sigmoid(argument)
    return logistic * (1.0 + argument * (1.0 - logistic))


def widen(with_rows):
    return jnp.pad(with_rows, ((0, 0), (0, 0), (0, 0), (1, 1), (0, 0)))


def weight_grad(input_rims, layer_grad):
    row_count, col_count, channels = (layer_grad.shape[2], layer_grad.shape[3], layer_grad.shape[4])
    padded = widen(input_rims)
    flat_grad = layer_grad.reshape(-1, channels)
    blocks = []
    for row_step in OFFSETS:
        for col_step in OFFSETS:
            shifted = padded[
                :,
                :,
                1 + row_step : 1 + row_step + row_count,
                1 + col_step : 1 + col_step + col_count,
                :,
            ]
            blocks.append(
                lax.dot_general(
                    shifted.reshape(-1, channels),
                    flat_grad,
                    CONTRACT_ROWS,
                    preferred_element_type=jnp.float32,
                )
            )
    return jnp.concatenate(blocks, axis=0)


def input_grad(grad_rims, weight):
    row_count = grad_rims.shape[2] - 2
    col_count, channels = (grad_rims.shape[3], grad_rims.shape[4])
    padded = widen(grad_rims)
    summed = jnp.zeros(
        (grad_rims.shape[0] * grad_rims.shape[1] * row_count * col_count, channels), jnp.float32
    )
    tap_number = 0
    for row_step in OFFSETS:
        for col_step in OFFSETS:
            shifted = padded[
                :,
                :,
                1 - row_step : 1 - row_step + row_count,
                1 - col_step : 1 - col_step + col_count,
                :,
            ]
            weight_tap = weight[tap_number * channels : (tap_number + 1) * channels]
            summed = summed + lax.dot_general(
                shifted.reshape(-1, channels),
                weight_tap,
                CONTRACT_COLS,
                preferred_element_type=jnp.float32,
            )
            tap_number += 1
    return summed.reshape(grad_rims.shape[0], grad_rims.shape[1], row_count, col_count, channels)


NB = 64

def diag_inverse(blocks):
    n = NB
    row = lax.broadcasted_iota(jnp.int32, (n, 2 * n), 0)
    col = lax.broadcasted_iota(jnp.int32, (n, 2 * n), 1)
    eye = jnp.where(row + n == col, 1.0, 0.0).astype(jnp.float32)
    tiles = []
    for b in blocks:
        x = jnp.concatenate([b, jnp.zeros((n, n), jnp.float32)], axis=1) + eye
        tiles.append([x[8 * t:8 * t + 8] for t in range(n // 8)])
    sub = lax.broadcasted_iota(jnp.int32, (8, 2 * n), 0)
    scales = [[None] * (n // 8) for _ in blocks]
    for j in range(n):
        tj, sj = j // 8, j % 8
        for m in range(len(blocks)):
            x = tiles[m]
            pivot_row = x[tj][sj:sj + 1, :]
            cb = jnp.broadcast_to(x[tj][:, j:j + 1], (8, 2 * n))
            d = cb[sj:sj + 1, :]
            rs = lax.rsqrt(d)
            scales[m][tj] = jnp.where(sub == sj, rs, scales[m][tj] if sj else 0.0)
            scaled = pivot_row * (rs * rs)
            if sj < 7:
                x[tj] = x[tj] - jnp.where(sub > sj, cb, 0.0) * scaled
            for t in range(tj + 1, n // 8):
                x[t] = x[t] - jnp.broadcast_to(x[t][:, j:j + 1], (8, 2 * n)) * scaled
    out = []
    for m in range(len(blocks)):
        w = jnp.concatenate([tiles[m][t] * scales[m][t] for t in range(n // 8)], axis=0)
        out.append(w[:, n:])
    return out

def chol_inv_kernel(g_ref, o_ref):
    nm, size, _ = g_ref.shape
    o_ref[...] = g_ref[...]
    nblk = size // NB
    for k in range(nblk):
        o = k * NB
        linv = diag_inverse([o_ref[m, o:o + NB, o:o + NB] for m in range(nm)])
        for m in range(nm):
            parts = []
            prow = o_ref[m, o:o + NB, :]
            r = jnp.dot(linv[m], prow, precision=HIGHEST, preferred_element_type=jnp.float32)
            pieces = []
            if k: pieces.append(r[:, :o])
            pieces.append(linv[m])
            if k < nblk - 1: pieces.append(r[:, o + NB:])
            rz = jnp.concatenate(pieces, axis=1)
            if k < nblk - 1:
                below = r[:, o + NB:]
                upd = lax.dot_general(below, rz, (((0,), (0,)), ((), ())), precision=HIGHEST, preferred_element_type=jnp.float32)
                old = o_ref[m, o + NB:, :]
                colid = lax.broadcasted_iota(jnp.int32, old.shape, 1)
                old = jnp.where((colid >= o) & (colid < o + NB), 0.0, old)
                o_ref[m, o + NB:, :] = old - upd
                colr = lax.broadcasted_iota(jnp.int32, rz.shape, 1)
                o_ref[m, o:o + NB, :] = jnp.where(colr < o + NB, rz, 0.0)
            else:
                o_ref[m, o:o + NB, :] = rz

def chol_inv(grams):
    return pl.pallas_call(chol_inv_kernel, out_shape=jax.ShapeDtypeStruct(grams.shape, jnp.float32),
        in_specs=[pl.BlockSpec(memory_space=pltpu.VMEM)], out_specs=pl.BlockSpec(memory_space=pltpu.VMEM),
        compiler_params=pltpu.CompilerParams(vmem_limit_bytes=48*1024*1024))(grams)


def coords():
    dp, space = lax.axis_index("dp"), lax.axis_index("space")
    core, x, y = dp % 2, (dp // 2) % 4, (space % 2) * 2 + dp // 8
    return core, (x, y, space // 2)

def device_at(core, place):
    x, y, z = place
    return {"dp": ((y % 2) * 4 + x) * 2 + core, "space": z * 2 + y // 2}

def shifted_place(place, axis, step):
    moved = list(place)
    moved[axis] = (place[axis] + step) % 4
    return tuple(moved)

def greet(partners):
    barrier = pltpu.get_barrier_semaphore()
    for partner in partners:
        pl.semaphore_signal(barrier, inc=1, device_id=partner, device_id_type=pl.DeviceIdType.MESH)
    pl.semaphore_wait(barrier, len(partners))

def add_rows(dst, dst_row, terms, rows, step):
    def body(i, carry):
        total = None
        for ref, start in terms:
            first = pl.multiple_of(start + i * step, 8)
            value = ref[pl.ds(first, step), :]
            total = value if total is None else total + value
        dst[pl.ds(pl.multiple_of(dst_row + i * step, 8), step), :] = total
        return carry
    lax.fori_loop(0, rows // step, body, 0)

def reduce_kernel(g_ref, o_ref, r0, r1, b, r2, c, r3, f, send, recv):
    core, place = coords()
    orders = [(0, 1, 2), (1, 2, 0), (2, 0, 1)]
    sibling = device_at(1 - core, place)
    partners = [sibling]
    for axis in range(3):
        for step in (1, 2, 3):
            partners.append(device_at(core, shifted_place(place, axis, step)))
    greet(partners)
    copies = []
    def start(src, dst, to):
        n = len(copies)
        copy = pltpu.make_async_remote_copy(src_ref=src, dst_ref=dst, send_sem=send.at[n], recv_sem=recv.at[n],
            device_id=to, device_id_type=pl.DeviceIdType.MESH)
        copy.start()
        copies.append(copy)
        return copy
    part = 960
    first = [start(g_ref.at[1 - core, pl.ds(p * part, part)], r0.at[pl.ds(p * part, part)], sibling) for p in range(3)]
    level1, level2, level3 = [], [], []
    for p in range(3):
        first[p].wait_recv()
        add_rows(r0, p * part, [(r0, p * part), (g_ref.at[core], p * part)], part, 96)
        axis = orders[p][0]
        sends = []
        for step in (1, 2, 3):
            to = shifted_place(place, axis, step)
            src = pl.multiple_of(p * part + to[axis] * 240, 8)
            sends.append(start(r0.at[pl.ds(src, 240)], r1.at[p, step - 1], device_at(core, to)))
        level1.append(sends)
    for p in range(3):
        for copy in level1[p]:
            copy.wait_recv()
        mine = place[orders[p][0]]
        add_rows(b.at[p], 0, [(r0, p * part + mine * 240)] + [(r1.at[p, k], 0) for k in range(3)], 240, 48)
        b[p, 240:, :] = jnp.zeros((16, b.shape[2]), jnp.float32)
        axis = orders[p][1]
        sends = []
        for step in (1, 2, 3):
            to = shifted_place(place, axis, step)
            src = pl.multiple_of(to[axis] * 64, 8)
            sends.append(start(b.at[p, pl.ds(src, 64)], r2.at[p, step - 1], device_at(core, to)))
        level2.append(sends)
    for p in range(3):
        for copy in level2[p]:
            copy.wait_recv()
        mine = place[orders[p][1]]
        add_rows(c.at[p], 0, [(b.at[p], mine * 64)] + [(r2.at[p, k], 0) for k in range(3)], 64, 64)
        axis = orders[p][2]
        sends = []
        for step in (1, 2, 3):
            to = shifted_place(place, axis, step)
            src = pl.multiple_of(to[axis] * 16, 8)
            sends.append(start(c.at[p, pl.ds(src, 16)], r3.at[p, step - 1], device_at(core, to)))
        level3.append(sends)
    gather3, gather2, gather1, last = [], [], [], []
    for p in range(3):
        for copy in level3[p]:
            copy.wait_recv()
        axis = orders[p][2]
        row = pl.multiple_of(place[orders[p][1]] * 64 + place[axis] * 16, 8)
        add_rows(f.at[p], row, [(c.at[p], place[axis] * 16)] + [(r3.at[p, k], 0) for k in range(3)], 16, 16)
        here = f.at[p, pl.ds(row, 16)]
        gather3.append([start(here, here, device_at(core, shifted_place(place, axis, s))) for s in (1, 2, 3)])
    for p in range(3):
        for copy in gather3[p]:
            copy.wait_recv()
        axis = orders[p][1]
        here = f.at[p, pl.ds(pl.multiple_of(place[axis] * 64, 8), 64)]
        gather2.append([start(here, here, device_at(core, shifted_place(place, axis, s))) for s in (1, 2, 3)])
    for p in range(3):
        for copy in gather2[p]:
            copy.wait_recv()
        axis = orders[p][0]
        row = pl.multiple_of(p * part + place[axis] * 240, 8)
        src = f.at[p, pl.ds(0, 240)]
        gather1.append([start(src, o_ref.at[core, pl.ds(row, 240)], device_at(core, shifted_place(place, axis, s)))
                        for s in (1, 2, 3)])
        add_rows(o_ref.at[core], row, [(f.at[p], 0)], 240, 48)
    for p in range(3):
        for copy in gather1[p]:
            copy.wait_recv()
        here = o_ref.at[core, pl.ds(p * part, part)]
        last.append(start(here, here, sibling))
    for copy in last:
        copy.wait_recv()
    for copy in copies:
        copy.wait_send()

def reduce_all(g):
    n = g.shape[-1]
    vm = lambda *s: pltpu.VMEM(s + (n,), jnp.float32)
    count = 3 + 9 * 6 + 3
    return pl.pallas_call(reduce_kernel, out_shape=jax.ShapeDtypeStruct(g.shape, jnp.float32),
        in_specs=[pl.BlockSpec(memory_space=pltpu.VMEM)], out_specs=pl.BlockSpec(memory_space=pltpu.VMEM),
        scratch_shapes=[vm(2880), vm(3, 3, 240), vm(3, 256), vm(3, 3, 64), vm(3, 64), vm(3, 3, 16), vm(3, 256),
                        pltpu.SemaphoreType.DMA((count,)), pltpu.SemaphoreType.DMA((count,))],
        compiler_params=pltpu.CompilerParams(collective_id=0, has_side_effects=True, vmem_limit_bytes=50*1024*1024))(g)


def group_sum_kernel(axis, n, in_ref, o_ref, arrived, send, recv):
    me = lax.axis_index(axis)
    rows = in_ref.shape[0] // n
    others = [(me + k) % n for k in range(1, n)]
    greet([{axis: to} for to in others])
    copies = []
    def start(src, dst, to):
        i = len(copies)
        copy = pltpu.make_async_remote_copy(src_ref=src, dst_ref=dst, send_sem=send.at[i], recv_sem=recv.at[i],
            device_id={axis: to}, device_id_type=pl.DeviceIdType.MESH)
        copy.start()
        copies.append(copy)
    for k, to in enumerate(others):
        start(in_ref.at[pl.ds(pl.multiple_of(to * rows, 8), rows)], arrived.at[k], to)
    for copy in copies:
        copy.wait_recv()
    mine = pl.multiple_of(me * rows, 8)
    add_rows(o_ref, mine, [(in_ref, mine)] + [(arrived.at[k], 0) for k in range(n - 1)], rows, rows)
    here = o_ref.at[pl.ds(mine, rows)]
    for to in others:
        start(here, here, to)
    for copy in copies[n - 1:]:
        copy.wait_recv()
    for copy in copies:
        copy.wait_send()

def group_sum(value, axis, n, collective_id):
    rows, cols = value.shape
    return pl.pallas_call(functools.partial(group_sum_kernel, axis, n),
        out_shape=jax.ShapeDtypeStruct(value.shape, jnp.float32),
        in_specs=[pl.BlockSpec(memory_space=pltpu.VMEM)], out_specs=pl.BlockSpec(memory_space=pltpu.VMEM),
        scratch_shapes=[pltpu.VMEM((n - 1, rows // n, cols), jnp.float32),
                        pltpu.SemaphoreType.DMA((2 * n - 2,)), pltpu.SemaphoreType.DMA((2 * n - 2,))],
        compiler_params=pltpu.CompilerParams(collective_id=collective_id, has_side_effects=True))(value)

ORDERS = ((0, 1, 2), (1, 2, 0), (2, 0, 1))

def spread_kernel(in_ref, o_ref, send, recv):
    core, place = coords()
    sibling = device_at(1 - core, place)
    partners = [sibling]
    for axis in range(3):
        for step in (1, 2, 3):
            partners.append(device_at(core, shifted_place(place, axis, step)))
    greet(partners)
    copies = []
    def start(here, to):
        i = len(copies)
        copy = pltpu.make_async_remote_copy(src_ref=here, dst_ref=here, send_sem=send.at[i], recv_sem=recv.at[i],
            device_id=to, device_id_type=pl.DeviceIdType.MESH)
        copy.start()
        copies.append(copy)
        return copy
    pending = [[] for _ in range(3)]
    for level in (2, 1, 0):
        for p in range(3):
            for copy in pending[p]:
                copy.wait_recv()
            row, size = 0, 1024
            for axis in ORDERS[p][:level + 1]:
                size = size // 4
                row = row + place[axis] * size
            row = pl.multiple_of(row, 16)
            if level == 2:
                o_ref[core, p, pl.ds(row, 16), :] = in_ref[pl.ds(16 * p, 16), :]
            here = o_ref.at[core, p, pl.ds(row, size)]
            pending[p] = [start(here, device_at(core, shifted_place(place, ORDERS[p][level], s))) for s in (1, 2, 3)]
    last = []
    for p in range(3):
        for copy in pending[p]:
            copy.wait_recv()
        last.append(start(o_ref.at[core, p], sibling))
    for copy in last:
        copy.wait_recv()
    for copy in copies:
        copy.wait_send()

def spread(rows, collective_id):
    return pl.pallas_call(spread_kernel, out_shape=jax.ShapeDtypeStruct((2, 3, 1024, rows.shape[1]), jnp.float32),
        in_specs=[pl.BlockSpec(memory_space=pltpu.VMEM)], out_specs=pl.BlockSpec(memory_space=pltpu.VMEM),
        scratch_shapes=[pltpu.SemaphoreType.DMA((30,)), pltpu.SemaphoreType.DMA((30,))],
        compiler_params=pltpu.CompilerParams(collective_id=collective_id, has_side_effects=True, vmem_limit_bytes=40*1024*1024))(rows)

def assemble(spread_out, full_rows):
    n = spread_out.shape[-1]
    parts = []
    for p in range(3):
        block = spread_out[:, p]
        shape, names = [], []
        for axis in ORDERS[p]:
            shape += [2, 2] if axis == 1 else [4]
            names += ["yh", "yl"] if axis == 1 else [["x", None, "z"][axis]]
        block = block.reshape([2] + shape + [16, n])
        perm = [1 + names.index(w) for w in ("z", "yh", "x", "yl")]
        parts.append(block.transpose([0] + perm + [5, 6]))
    both = jnp.stack(parts, axis=5)
    both = both.reshape(2, 8, 384, n)[:, :, :full_rows // 8]
    return both.reshape(2, full_rows, n)


def with_rims(stacked):
    return padded_2(stacked, (("space", 3),), 1)


def local(inputs, preacts, cotangent, weights, left_stats, left_basis, right_stats, right_basis):
    row_share = left_stats.shape[1]
    col_share = left_stats.shape[2]
    channels = inputs.shape[-1]
    full_rows = weights.shape[1]
    dp_index = lax.axis_index("dp")
    space_index = lax.axis_index("space")
    stat_rows = lax.psum(
        lax.dot_general(left_stats, left_basis, (((2,), (1,)), ((0,), (0,))), precision=HIGHEST), "dp"
    )
    full_basis = lax.all_gather(left_basis, "dp", axis=1, tiled=True)

    activation = jax.nn.silu(preacts[0].astype(jnp.float32)).astype(jnp.bfloat16)
    extended = with_rims(jnp.stack([activation, cotangent]))
    backward = input_grad(extended[1], weights[0])
    following = (backward * silu_slope(preacts[0])).astype(jnp.bfloat16)
    first = with_rims(inputs[None])
    gradient = jnp.stack([weight_grad(first[0], following), weight_grad(extended[0], cotangent)])
    complete = reduce_all(gradient)

    row_block = lax.dynamic_slice_in_dim(complete, space_index * row_share, row_share, 1)
    col_block = lax.dynamic_slice_in_dim(complete, dp_index * col_share, col_share, 1)
    left_new = BETA * left_stats + (1.0 - BETA) * lax.dot_general(
        row_block, col_block, (((2,), (2,)), ((0,), (0,))), precision=HIGHEST
    )
    inner = (((1,), (1,)), ((0,), (0,)))
    gram_right = lax.dot_general(complete, complete, inner, precision=HIGHEST)
    turned = lax.dot_general(complete, full_basis, inner, precision=HIGHEST)
    product_rows = BETA * stat_rows + (1.0 - BETA) * jnp.matmul(row_block, turned, precision=HIGHEST)
    gram_left = lax.dot_general(product_rows, product_rows, inner, precision=HIGHEST)
    gram_left = group_sum(gram_left.reshape(2 * channels, channels), "space", 8, 1)
    right_new = BETA * right_stats + (1.0 - BETA) * gram_right
    right_rows = jnp.matmul(right_new, right_basis, precision=HIGHEST)
    right_gram = lax.dot_general(right_rows, right_rows, inner, precision=HIGHEST)
    inverses = chol_inv(jnp.concatenate([gram_left.reshape(2, channels, channels), right_gram]))

    core = dp_index % 2
    place = ((dp_index // 2) % 4) * 2 + dp_index // 8
    padded = jnp.pad(product_rows, ((0, 0), (0, 384 - row_share), (0, 0)))
    own = lax.dynamic_slice(padded, (core, place * 48, 0), (1, 48, channels))[0]
    own_inverse = lax.dynamic_index_in_dim(inverses[:2], core, 0, keepdims=False)
    basis_rows = math.sqrt(full_rows) * lax.dot_general(
        own, own_inverse, CONTRACT_COLS, precision=HIGHEST
    )
    basis_out = assemble(spread(basis_rows, 2), full_rows)
    turned_out = math.sqrt(channels) * jnp.matmul(
        right_rows, jnp.swapaxes(inverses[2:], 1, 2), precision=HIGHEST
    )
    return left_new, basis_out, right_new, turned_out


def solution(mesh):
    placed = (
        P("dp", None, "space", None, None),
        P(None, "dp", None, "space", None, None),
        P("dp", None, "space", None, None),
        P(),
        P(None, "space", "dp"),
        P(None, "dp", None),
        P(),
        P(),
    )
    return jax.shard_map(
        local,
        mesh=mesh,
        in_specs=placed,
        out_specs=(P(None, "space", "dp"), P(), P(), P()),
        check_vma=False,
    )
```

```python
import functools
import math

import jax
import jax.numpy as jnp
from jax import lax
from jax.experimental import pallas as pl
from jax.experimental.pallas import tpu as pltpu
from jax.sharding import PartitionSpec as P

BETA = 0.95
HIGHEST = lax.Precision.HIGHEST
CONTRACT_ROWS = (((0,), (0,)), ((), ()))
CONTRACT_COLS = (((1,), (1,)), ((), ()))
MESH = pl.DeviceIdType.MESH
ORDERS = ((0, 1, 2), (1, 2, 0), (2, 0, 1))
PADDED = 384


def kernel_params(collective_id=None):
    extra = {} if collective_id is None else {"collective_id": collective_id, "has_side_effects": True}
    return pltpu.CompilerParams(vmem_limit_bytes=50 * 1024 * 1024, **extra)

def coords():
    dp, space = lax.axis_index("dp"), lax.axis_index("space")
    core, x, y = dp % 2, (dp // 2) % 4, (space % 2) * 2 + dp // 8
    return core, (x, y, space // 2)

def device_at(core, place):
    x, y, z = place
    return {"dp": ((y % 2) * 4 + x) * 2 + core, "space": z * 2 + y // 2}

def shifted_place(place, axis, step):
    moved = list(place)
    moved[axis] = (place[axis] + step) % 4
    return tuple(moved)

def greet(partners):
    barrier = pltpu.get_barrier_semaphore()
    for partner in partners:
        pl.semaphore_signal(barrier, inc=1, device_id=partner, device_id_type=pl.DeviceIdType.MESH)
    pl.semaphore_wait(barrier, len(partners))

def add_rows(dst, dst_row, terms, rows, step):
    def body(i, carry):
        total = None
        for ref, start in terms:
            first = pl.multiple_of(start + i * step, 8)
            value = ref[pl.ds(first, step), :]
            total = value if total is None else total + value
        dst[pl.ds(pl.multiple_of(dst_row + i * step, 8), step), :] = total
        return carry
    lax.fori_loop(0, rows // step, body, 0)


class Sender:
    def __init__(self, send, recv):
        self.send, self.recv, self.copies = send, recv, []

    def start(self, src, dst, to):
        n = len(self.copies)
        copy = pltpu.make_async_remote_copy(
            src_ref=src, dst_ref=dst, send_sem=self.send.at[n], recv_sem=self.recv.at[n],
            device_id=to, device_id_type=MESH,
        )
        copy.start()
        self.copies.append(copy)
        return copy

    def finish(self):
        for copy in self.copies:
            copy.wait_send()


def arrived(copies):
    for copy in copies:
        copy.wait_recv()


def all_partners(core, place):
    partners = [device_at(1 - core, place)]
    for axis in range(3):
        for step in (1, 2, 3):
            partners.append(device_at(core, shifted_place(place, axis, step)))
    return partners


def moved_to(place, axis, value):
    moved = list(place)
    moved[axis] = value
    return tuple(moved)


def ring_pairs(half):
    near = lambda x: x + 1 - 2 * (x % 2)
    far = lambda x: 3 - x
    return (near, far) if half == 0 else (far, near)


def peers(place, axis):
    return [shifted_place(place, axis, step) for step in (1, 2, 3)]


def reduce_kernel(g_ref, o_ref, r0, r1, s1, b, r2, c, r3, f, send, recv):
    core, place = coords()
    greet(all_partners(core, place))
    sibling = device_at(1 - core, place)
    out = Sender(send, recv)
    part, chunk, half_rows = 960, 240, 120
    first = [out.start(g_ref.at[1 - core, pl.ds(p * part, part)], r0.at[pl.ds(p * part, part)], sibling) for p in range(3)]
    level1a, level1b, level2, level3 = {}, {}, [], []

    def rows_at(p, j, half):
        return pl.multiple_of(p * part + j * chunk + half * half_rows, 8)

    for p in range(3):
        first[p].wait_recv()
        add_rows(r0, p * part, [(r0, p * part), (g_ref.at[core], p * part)], part, 96)
        axis = ORDERS[p][0]
        for half in range(2):
            near, far = ring_pairs(half)
            to = near(place[axis])
            device = device_at(core, moved_to(place, axis, to))
            level1a[p, half] = [
                out.start(r0.at[pl.ds(rows_at(p, j, half), half_rows)], r1.at[p, half, slot], device)
                for slot, j in ((1, far(to)), (0, to))
            ]
    for p in range(3):
        axis = ORDERS[p][0]
        for half in range(2):
            near, far = ring_pairs(half)
            to = far(place[axis])
            level1a[p, half][0].wait_recv()
            add_rows(s1.at[p, half], 0, [(r0, rows_at(p, to, half)), (r1.at[p, half, 1], 0)], half_rows, 40)
            level1b[p, half] = out.start(s1.at[p, half], r1.at[p, half, 2], device_at(core, moved_to(place, axis, to)))
    for p in range(3):
        mine = place[ORDERS[p][0]]
        for half in range(2):
            level1a[p, half][1].wait_recv()
            level1b[p, half].wait_recv()
            add_rows(b.at[p], half * half_rows,
                     [(r0, rows_at(p, mine, half)), (r1.at[p, half, 0], 0), (r1.at[p, half, 2], 0)], half_rows, 40)
        b[p, chunk:, :] = jnp.zeros((16, b.shape[2]), jnp.float32)
        axis = ORDERS[p][1]
        level2.append([
            out.start(b.at[p, pl.ds(pl.multiple_of(to[axis] * 64, 8), 64)], r2.at[p, k], device_at(core, to))
            for k, to in enumerate(peers(place, axis))
        ])
    for p in range(3):
        arrived(level2[p])
        mine = place[ORDERS[p][1]]
        add_rows(c.at[p], 0, [(b.at[p], mine * 64)] + [(r2.at[p, k], 0) for k in range(3)], 64, 64)
        axis = ORDERS[p][2]
        level3.append([
            out.start(c.at[p, pl.ds(pl.multiple_of(to[axis] * 16, 8), 16)], r3.at[p, k], device_at(core, to))
            for k, to in enumerate(peers(place, axis))
        ])
    gather3, gather2, gather1a, gather1b, last = [], [], {}, {}, []
    for p in range(3):
        arrived(level3[p])
        axis = ORDERS[p][2]
        row = pl.multiple_of(place[ORDERS[p][1]] * 64 + place[axis] * 16, 8)
        add_rows(f.at[p], row, [(c.at[p], place[axis] * 16)] + [(r3.at[p, k], 0) for k in range(3)], 16, 16)
        here = f.at[p, pl.ds(row, 16)]
        gather3.append([out.start(here, here, device_at(core, to)) for to in peers(place, axis)])
    for p in range(3):
        arrived(gather3[p])
        axis = ORDERS[p][1]
        here = f.at[p, pl.ds(pl.multiple_of(place[axis] * 64, 8), 64)]
        gather2.append([out.start(here, here, device_at(core, to)) for to in peers(place, axis)])

    def gathered(p, j, half):
        return o_ref.at[core, pl.ds(rows_at(p, j, half), half_rows)]

    for p in range(3):
        arrived(gather2[p])
        axis = ORDERS[p][0]
        x = place[axis]
        add_rows(o_ref.at[core], rows_at(p, x, 0), [(f.at[p], 0)], chunk, 48)
        for half in range(2):
            near, far = ring_pairs(half)
            here = gathered(p, x, half)
            gather1a[p, half] = out.start(here, here, device_at(core, moved_to(place, axis, far(x))))
            gather1b[p, half] = [out.start(here, here, device_at(core, moved_to(place, axis, near(x))))]
    for p in range(3):
        axis = ORDERS[p][0]
        x = place[axis]
        for half in range(2):
            near, far = ring_pairs(half)
            gather1a[p, half].wait_recv()
            here = gathered(p, far(x), half)
            gather1b[p, half].append(out.start(here, here, device_at(core, moved_to(place, axis, near(x)))))
    for p in range(3):
        for half in range(2):
            arrived(gather1b[p, half])
        here = o_ref.at[core, pl.ds(p * part, part)]
        last.append(out.start(here, here, sibling))
    arrived(last)
    out.finish()


def reduce_all(g):
    n = g.shape[-1]
    vm = lambda *s: pltpu.VMEM(s + (n,), jnp.float32)
    count = 3 + 18 + 9 * 4 + 18 + 3
    return pl.pallas_call(
        reduce_kernel,
        out_shape=jax.ShapeDtypeStruct(g.shape, jnp.float32),
        in_specs=[pl.BlockSpec(memory_space=pltpu.VMEM)],
        out_specs=pl.BlockSpec(memory_space=pltpu.VMEM),
        scratch_shapes=[vm(2880), vm(3, 2, 3, 120), vm(3, 2, 120), vm(3, 256), vm(3, 3, 64), vm(3, 64), vm(3, 3, 16),
                        vm(3, 256), pltpu.SemaphoreType.DMA((count,)), pltpu.SemaphoreType.DMA((count,))],
        compiler_params=kernel_params(0),
    )(g)


def gram_kernel(p_ref, own_ref, gram_ref, r0, r1, a, b, r2, c, r3, f, r4, send, recv):
    core, place = coords()
    x, y, z = place
    quads = []
    for step in range(1, 8):
        quads.append(((x + step // 2) % 4, (y // 2) * 2 + (y + step % 2) % 2, z))
    partners = all_partners(core, place)
    partners += [device_at(core, to) for step, to in enumerate(quads, 1) if step // 2 and step % 2]
    greet(partners)
    out = Sender(send, recv)
    out.start(p_ref.at[1 - core], r0, device_at(1 - core, place)).wait_recv()
    add_rows(a, 0, [(r0, 0), (p_ref.at[core], 0)], PADDED, 96)
    block = lambda to: pl.multiple_of((to[0] * 2 + to[1] % 2) * 48, 16)
    arrived([out.start(a.at[pl.ds(block(to), 48)], r1.at[k], device_at(core, to)) for k, to in enumerate(quads)])
    add_rows(own_ref, 0, [(a, block(place))] + [(r1.at[k], 0) for k in range(7)], 48, 48)
    own = own_ref[...]
    n = own.shape[1]
    gram = lax.dot_general(own, own, CONTRACT_ROWS, precision=HIGHEST, preferred_element_type=jnp.float32)
    b[0, :, :] = gram[:128]
    b[1, :, :] = gram[128:256]
    b[2, :n - 256, :] = gram[256:]
    b[2, n - 256:, :] = jnp.zeros((PADDED - n, n), jnp.float32)
    level1, level2, level3, gather2, gather1 = [], [], [], [], []
    for p in range(3):
        axis = ORDERS[p][0]
        level1.append([
            out.start(b.at[p, pl.ds(pl.multiple_of(to[axis] * 32, 8), 32)], r2.at[p, k], device_at(core, to))
            for k, to in enumerate(peers(place, axis))
        ])
    for p in range(3):
        arrived(level1[p])
        add_rows(c.at[p], 0, [(b.at[p], place[ORDERS[p][0]] * 32)] + [(r2.at[p, k], 0) for k in range(3)], 32, 32)
        axis = ORDERS[p][1]
        level2.append([
            out.start(c.at[p, pl.ds(pl.multiple_of(to[axis] * 8, 8), 8)], r3.at[p, k], device_at(core, to))
            for k, to in enumerate(peers(place, axis))
        ])
    for p in range(3):
        arrived(level2[p])
        add_rows(f.at[p], 0, [(c.at[p], place[ORDERS[p][1]] * 8)] + [(r3.at[p, k], 0) for k in range(3)], 8, 8)
        axis = ORDERS[p][2]
        level3.append([
            out.start(f.at[p], r4.at[p, k], device_at(core, to)) for k, to in enumerate(peers(place, axis))
        ])
    for p in range(3):
        arrived(level3[p])
        axis = ORDERS[p][1]
        row = pl.multiple_of(p * 128 + place[ORDERS[p][0]] * 32 + place[axis] * 8, 8)
        add_rows(gram_ref, row, [(f.at[p], 0)] + [(r4.at[p, k], 0) for k in range(3)], 8, 8)
        here = gram_ref.at[pl.ds(row, 8)]
        gather2.append([out.start(here, here, device_at(core, to)) for to in peers(place, axis)])
    for p in range(3):
        arrived(gather2[p])
        axis = ORDERS[p][0]
        here = gram_ref.at[pl.ds(pl.multiple_of(p * 128 + place[axis] * 32, 8), 32)]
        gather1.append([out.start(here, here, device_at(core, to)) for to in peers(place, axis)])
    for p in range(3):
        arrived(gather1[p])
    out.finish()


def gram_of_rows(partial):
    n = partial.shape[-1]
    vm = lambda *s: pltpu.VMEM(s + (n,), jnp.float32)
    return pl.pallas_call(
        gram_kernel,
        out_shape=(jax.ShapeDtypeStruct((48, n), jnp.float32), jax.ShapeDtypeStruct((PADDED, n), jnp.float32)),
        in_specs=[pl.BlockSpec(memory_space=pltpu.VMEM)],
        out_specs=(pl.BlockSpec(memory_space=pltpu.VMEM),) * 2,
        scratch_shapes=[vm(PADDED), vm(7, 48), vm(PADDED), vm(3, 128), vm(3, 3, 32), vm(3, 32), vm(3, 3, 8), vm(3, 8),
                        vm(3, 3, 8), pltpu.SemaphoreType.DMA((53,)), pltpu.SemaphoreType.DMA((53,))],
        compiler_params=kernel_params(1),
    )(partial)


def spread_kernel(in_ref, x_ref, o_ref, y_ref, send, recv):
    core, place = coords()
    greet(all_partners(core, place))
    sibling = device_at(1 - core, place)
    out = Sender(send, recv)
    last = [out.start(x_ref, y_ref.at[core], sibling)]
    y_ref[core] = x_ref[...]

    def view(p, places, half=None):
        row, size = 0, 1024
        for c in places:
            size = size // 4
            row = row + c * size
        if half is not None:
            size = size // 2
            row = row + half * size
        return o_ref.at[core, p, pl.ds(pl.multiple_of(row, 16), size)]

    pending, gather1a, gather1b = [], {}, {}
    for p in range(3):
        a1, a2, a3 = ORDERS[p]
        here = view(p, (place[a1], place[a2], place[a3]))
        here[...] = in_ref[pl.ds(16 * p, 16), :]
        pending.append([out.start(here, here, device_at(core, to)) for to in peers(place, a3)])
    for p in range(3):
        arrived(pending[p])
        a1, a2, a3 = ORDERS[p]
        here = view(p, (place[a1], place[a2]))
        pending[p] = [out.start(here, here, device_at(core, to)) for to in peers(place, a2)]
    for p in range(3):
        arrived(pending[p])
        axis = ORDERS[p][0]
        x = place[axis]
        for half in range(2):
            near, far = ring_pairs(half)
            here = view(p, (x,), half)
            gather1a[p, half] = out.start(here, here, device_at(core, moved_to(place, axis, far(x))))
            gather1b[p, half] = [out.start(here, here, device_at(core, moved_to(place, axis, near(x))))]
    for p in range(3):
        axis = ORDERS[p][0]
        x = place[axis]
        for half in range(2):
            near, far = ring_pairs(half)
            gather1a[p, half].wait_recv()
            here = view(p, (far(x),), half)
            gather1b[p, half].append(out.start(here, here, device_at(core, moved_to(place, axis, near(x)))))
    for p in range(3):
        for half in range(2):
            arrived(gather1b[p, half])
        last.append(out.start(o_ref.at[core, p], o_ref.at[core, p], sibling))
    arrived(last)
    out.finish()


def spread(rows, extra):
    n = rows.shape[1]
    return pl.pallas_call(
        spread_kernel,
        out_shape=(jax.ShapeDtypeStruct((2, 3, 1024, n), jnp.float32),
                   jax.ShapeDtypeStruct((2,) + extra.shape, jnp.float32)),
        in_specs=[pl.BlockSpec(memory_space=pltpu.VMEM)] * 2,
        out_specs=(pl.BlockSpec(memory_space=pltpu.VMEM),) * 2,
        scratch_shapes=[pltpu.SemaphoreType.DMA((40,)), pltpu.SemaphoreType.DMA((40,))],
        compiler_params=kernel_params(2),
    )(rows, extra)


def assemble_kernel(in_ref, o_ref):
    layer, block = pl.program_id(0), pl.program_id(1)
    z, y_high = block // 2, block % 2
    for q in range(8):
        place = (q // 2, y_high * 2 + q % 2, z)
        for p in range(3):
            row = 48 * q + 16 * p
            size = min(16, o_ref.shape[1] - row)
            if size <= 0:
                continue
            a1, a2, a3 = ORDERS[p]
            src = pl.multiple_of(((place[a1] * 4 + place[a2]) * 4 + place[a3]) * 16, 16)
            o_ref[0, row:row + size, :] = in_ref[layer, p, pl.ds(src, size), :]


def assemble(spread_out, full_rows):
    n = spread_out.shape[-1]
    share = full_rows // 8
    return pl.pallas_call(
        assemble_kernel,
        grid=(2, 8),
        out_shape=jax.ShapeDtypeStruct((2, full_rows, n), jnp.float32),
        in_specs=[pl.BlockSpec(memory_space=pltpu.VMEM)],
        out_specs=pl.BlockSpec((1, share, n), lambda i, j: (i, j, 0)),
        compiler_params=kernel_params(),
    )(spread_out)


def three_wide(x):
    cols = x.shape[0]
    col = lax.broadcasted_iota(jnp.int32, x.shape, 0)
    before = jnp.where(col == 0, 0.0, pltpu.roll(x, 1, 0))
    after = jnp.where(col == cols - 1, 0.0, pltpu.roll(x, cols - 1, 0))
    return jnp.concatenate([v.astype(jnp.bfloat16) for v in (before, x, after)], axis=1)

def grads_kernel(remote, rows, cols, a_ref, v_ref, g_ref, w_ref, o_ref, rims, wide, wide_g, back, g_t, w_t, send, recv):
    n = a_ref.shape[1]
    copies = []
    if remote:
        me = lax.axis_index("space")
        up, down = (me + 7) % 8, (me + 1) % 8
        greet([{"space": up}, {"space": down}])
        for i, ref in enumerate((g_ref, v_ref, a_ref)):
            for side, (first, to) in enumerate((((rows - 1) * cols, down), (0, up))):
                copy = pltpu.make_async_remote_copy(src_ref=ref.at[pl.ds(first, cols)], dst_ref=rims.at[i, side],
                    send_sem=send.at[2 * i + side], recv_sem=recv.at[2 * i + side],
                    device_id={"space": to}, device_id_type=pl.DeviceIdType.MESH)
                copy.start()
                copies.append(copy)
        has = (me > 0, me < 7)
    else:
        has = (True, True)
    same = lambda x: x
    silu = lambda x: (x * jax.nn.sigmoid(x)).astype(jnp.bfloat16).astype(jnp.float32)
    def widen_rows(ref, dst, change):
        def body(r, carry):
            x = change(ref[pl.ds(pl.multiple_of(r * cols, 16), cols), :].astype(jnp.float32))
            dst[pl.ds(pl.multiple_of((r + 1) * cols, 16), cols), :] = three_wide(x)
            return carry
        lax.fori_loop(0, rows, body, 0)
    def widen_rims(i, dst, change):
        for side in range(2):
            if remote:
                copies[2 * i + side].wait_recv()
            x = change(rims[i, side].astype(jnp.float32))
            x = jnp.where(has[side], x, 0.0)
            dst[pl.ds(side * (rows + 1) * cols, cols), :] = three_wide(x)
    cells = rows * cols
    def gradient(layer):
        def body(dr, carry):
            start = pl.multiple_of(dr * cols, 16)
            for lane in range(0, 3 * n, 256):
                size = min(256, 3 * n - lane)
                part = jnp.dot(g_t[...], wide[pl.ds(start, cells), pl.ds(lane, size)],
                               preferred_element_type=jnp.float32)
                o_ref[layer, pl.ds(pl.multiple_of(dr * 3 * n + lane, 8), size), :] = part.T
            return carry
        lax.fori_loop(0, 3, body, 0)
    for dr in range(3):
        for seg in range(3):
            tap = w_ref[pl.ds((3 * dr + 2 - seg) * n, n), :]
            w_t[dr, pl.ds(seg * n, n), :] = tap.T
    widen_rows(v_ref, wide, silu)
    widen_rows(g_ref, wide_g, same)
    g_t[...] = g_ref[...].T
    widen_rims(0, wide_g, same)
    widen_rims(1, wide, silu)
    gradient(1)
    half = cells // 2
    def back_body(i, carry):
        first = pl.multiple_of(i * half, 16)
        total = None
        for dr in range(3):
            x = wide_g[pl.ds(pl.multiple_of(first + (2 - dr) * cols, 16), half), :]
            y = jnp.dot(x, w_t[dr], preferred_element_type=jnp.float32)
            total = y if total is None else total + y
        v = v_ref[pl.ds(first, half), :].astype(jnp.float32)
        s = jax.nn.sigmoid(v)
        back[pl.ds(first, half), :] = (total * (s * (1.0 + v * (1.0 - s)))).astype(jnp.bfloat16)
        return carry
    lax.fori_loop(0, 2, back_body, 0)
    g_t[...] = back[...].T
    widen_rows(a_ref, wide, same)
    widen_rims(2, wide, same)
    gradient(0)
    for copy in copies:
        copy.wait_send()

def gradients(inputs, preacts, cotangent, weights, remote=True, collective_id=3):
    rows, cols, n = inputs.shape
    flat = [x.reshape(rows * cols, n) for x in (inputs, preacts, cotangent)]
    b16 = jnp.bfloat16
    return pl.pallas_call(functools.partial(grads_kernel, remote, rows, cols),
        out_shape=jax.ShapeDtypeStruct((2, 9 * n, n), jnp.float32),
        in_specs=[pl.BlockSpec(memory_space=pltpu.VMEM)] * 4, out_specs=pl.BlockSpec(memory_space=pltpu.VMEM),
        scratch_shapes=[pltpu.VMEM((3, 2, cols, n), b16), pltpu.VMEM(((rows + 2) * cols, 3 * n), b16),
                        pltpu.VMEM(((rows + 2) * cols, 3 * n), b16), pltpu.VMEM((rows * cols, n), b16),
                        pltpu.VMEM((n, rows * cols), b16), pltpu.VMEM((3, 3 * n, n), b16),
                        pltpu.SemaphoreType.DMA((6,)), pltpu.SemaphoreType.DMA((6,))],
        compiler_params=kernel_params(collective_id if remote else None))(*flat, weights)


NB = 64

def diag_inverse(blocks):
    n = NB
    row = lax.broadcasted_iota(jnp.int32, (n, 2 * n), 0)
    col = lax.broadcasted_iota(jnp.int32, (n, 2 * n), 1)
    eye = jnp.where(row + n == col, 1.0, 0.0).astype(jnp.float32)
    tiles = []
    for b in blocks:
        x = jnp.concatenate([b, jnp.zeros((n, n), jnp.float32)], axis=1) + eye
        tiles.append([x[8 * t:8 * t + 8] for t in range(n // 8)])
    sub = lax.broadcasted_iota(jnp.int32, (8, 2 * n), 0)
    scales = [[None] * (n // 8) for _ in blocks]
    for j in range(n):
        tj, sj = j // 8, j % 8
        for m in range(len(blocks)):
            x = tiles[m]
            pivot_row = x[tj][sj:sj + 1, :]
            cb = jnp.broadcast_to(x[tj][:, j:j + 1], (8, 2 * n))
            d = cb[sj:sj + 1, :]
            rs = lax.rsqrt(d)
            scales[m][tj] = jnp.where(sub == sj, rs, scales[m][tj] if sj else 0.0)
            scaled = pivot_row * (rs * rs)
            if sj < 7:
                x[tj] = x[tj] - jnp.where(sub > sj, cb, 0.0) * scaled
            for t in range(tj + 1, n // 8):
                x[t] = x[t] - jnp.broadcast_to(x[t][:, j:j + 1], (8, 2 * n)) * scaled
    out = []
    for m in range(len(blocks)):
        w = jnp.concatenate([tiles[m][t] * scales[m][t] for t in range(n // 8)], axis=0)
        out.append(w[:, n:])
    return out

def chol_inv_kernel(g_ref, o_ref):
    nm, size, _ = g_ref.shape
    o_ref[...] = g_ref[...]
    nblk = size // NB
    for k in range(nblk):
        o = k * NB
        linv = diag_inverse([o_ref[m, o:o + NB, o:o + NB] for m in range(nm)])
        for m in range(nm):
            parts = []
            prow = o_ref[m, o:o + NB, :]
            r = jnp.dot(linv[m], prow, precision=HIGHEST, preferred_element_type=jnp.float32)
            pieces = []
            if k: pieces.append(r[:, :o])
            pieces.append(linv[m])
            if k < nblk - 1: pieces.append(r[:, o + NB:])
            rz = jnp.concatenate(pieces, axis=1)
            if k < nblk - 1:
                below = r[:, o + NB:]
                upd = lax.dot_general(below, rz, (((0,), (0,)), ((), ())), precision=HIGHEST, preferred_element_type=jnp.float32)
                old = o_ref[m, o + NB:, :]
                colid = lax.broadcasted_iota(jnp.int32, old.shape, 1)
                old = jnp.where((colid >= o) & (colid < o + NB), 0.0, old)
                o_ref[m, o + NB:, :] = old - upd
                colr = lax.broadcasted_iota(jnp.int32, rz.shape, 1)
                o_ref[m, o:o + NB, :] = jnp.where(colr < o + NB, rz, 0.0)
            else:
                o_ref[m, o:o + NB, :] = rz

def chol_inv(grams):
    return pl.pallas_call(chol_inv_kernel, out_shape=jax.ShapeDtypeStruct(grams.shape, jnp.float32),
        in_specs=[pl.BlockSpec(memory_space=pltpu.VMEM)], out_specs=pl.BlockSpec(memory_space=pltpu.VMEM),
        compiler_params=pltpu.CompilerParams(vmem_limit_bytes=48*1024*1024))(grams)


def local(inputs, preacts, cotangent, weights, left_stats, left_basis, right_stats, right_basis):
    row_share = left_stats.shape[1]
    col_share = left_stats.shape[2]
    full_rows, channels = weights.shape[1:]
    dp_index = lax.axis_index("dp")
    space_index = lax.axis_index("space")
    core = dp_index % 2
    complete = reduce_all(gradients(inputs[0, 0], preacts[0, 0, 0], cotangent[0, 0], weights[0]))

    row_block = lax.dynamic_slice_in_dim(complete, space_index * row_share, row_share, 1)
    col_block = lax.dynamic_slice_in_dim(complete, dp_index * col_share, col_share, 1)
    left_new = BETA * left_stats + (1.0 - BETA) * lax.dot_general(
        row_block, col_block, (((2,), (2,)), ((0,), (0,))), precision=HIGHEST
    )
    partial = lax.dot_general(left_new, left_basis, (((2,), (1,)), ((0,), (0,))), precision=HIGHEST)
    own, gram_left = gram_of_rows(jnp.pad(partial, ((0, 0), (0, PADDED - row_share), (0, 0))))

    pick = lambda x: lax.dynamic_index_in_dim(x, core, 0, keepdims=False)
    mine = pick(complete)
    gram_right = lax.dot_general(mine, mine, CONTRACT_ROWS, precision=HIGHEST)
    right_new = BETA * pick(right_stats) + (1.0 - BETA) * gram_right
    right_rows = jnp.dot(right_new, pick(right_basis), precision=HIGHEST)
    right_gram = lax.dot_general(right_rows, right_rows, CONTRACT_ROWS, precision=HIGHEST)
    inverses = chol_inv(jnp.stack([gram_left[:channels], right_gram]))
    basis_rows = math.sqrt(full_rows) * lax.dot_general(own, inverses[0], CONTRACT_COLS, precision=HIGHEST)
    turned = math.sqrt(channels) * lax.dot_general(right_rows, inverses[1], CONTRACT_COLS, precision=HIGHEST)
    spread_rows, right_both = spread(basis_rows, jnp.stack([right_new, turned]))
    return left_new, assemble(spread_rows, full_rows), right_both[:, 0], right_both[:, 1]


def solution(mesh):
    placed = (
        P("dp", None, "space", None, None),
        P(None, "dp", None, "space", None, None),
        P("dp", None, "space", None, None),
        P(),
        P(None, "space", "dp"),
        P(None, "dp", None),
        P(),
        P(),
    )
    return jax.shard_map(
        local,
        mesh=mesh,
        in_specs=placed,
        out_specs=(P(None, "space", "dp"), P(), P(), P()),
        check_vma=False,
    )
```

```python
import functools
import math

import jax
import jax.numpy as jnp
from jax import lax
from jax.experimental import pallas as pl
from jax.experimental.pallas import tpu as pltpu
from jax.sharding import PartitionSpec as P

BETA = 0.95
HIGHEST = lax.Precision.HIGHEST
CONTRACT_ROWS = (((0,), (0,)), ((), ()))
CONTRACT_COLS = (((1,), (1,)), ((), ()))
MESH = pl.DeviceIdType.MESH
ORDERS = ((0, 1, 2), (1, 2, 0), (2, 0, 1))
PADDED = 384


def kernel_params(collective_id=None):
    extra = {} if collective_id is None else {"collective_id": collective_id, "has_side_effects": True}
    return pltpu.CompilerParams(vmem_limit_bytes=50 * 1024 * 1024, **extra)

def coords():
    dp, space = lax.axis_index("dp"), lax.axis_index("space")
    core, x, y = dp % 2, (dp // 2) % 4, (space % 2) * 2 + dp // 8
    return core, (x, y, space // 2)

def device_at(core, place):
    x, y, z = place
    return {"dp": ((y % 2) * 4 + x) * 2 + core, "space": z * 2 + y // 2}

def shifted_place(place, axis, step):
    moved = list(place)
    moved[axis] = (place[axis] + step) % 4
    return tuple(moved)

def greet(partners):
    barrier = pltpu.get_barrier_semaphore()
    for partner in partners:
        pl.semaphore_signal(barrier, inc=1, device_id=partner, device_id_type=pl.DeviceIdType.MESH)
    pl.semaphore_wait(barrier, len(partners))

def add_rows(dst, dst_row, terms, rows, step):
    def body(i, carry):
        total = None
        for ref, start in terms:
            first = pl.multiple_of(start + i * step, 8)
            value = ref[pl.ds(first, step), :]
            total = value if total is None else total + value
        dst[pl.ds(pl.multiple_of(dst_row + i * step, 8), step), :] = total
        return carry
    lax.fori_loop(0, rows // step, body, 0)


class Sender:
    def __init__(self, send, recv):
        self.send, self.recv, self.copies = send, recv, []

    def start(self, src, dst, to):
        n = len(self.copies)
        copy = pltpu.make_async_remote_copy(
            src_ref=src, dst_ref=dst, send_sem=self.send.at[n], recv_sem=self.recv.at[n],
            device_id=to, device_id_type=MESH,
        )
        copy.start()
        self.copies.append(copy)
        return copy

    def finish(self):
        for copy in self.copies:
            copy.wait_send()


def arrived(copies):
    for copy in copies:
        copy.wait_recv()


def all_partners(core, place):
    partners = [device_at(1 - core, place)]
    for axis in range(3):
        for step in (1, 2, 3):
            partners.append(device_at(core, shifted_place(place, axis, step)))
    return partners


def moved_to(place, axis, value):
    moved = list(place)
    moved[axis] = value
    return tuple(moved)


def ring_pairs(half):
    near = lambda x: x + 1 - 2 * (x % 2)
    far = lambda x: 3 - x
    return (near, far) if half == 0 else (far, near)


def peers(place, axis):
    return [shifted_place(place, axis, step) for step in (1, 2, 3)]


def reduce_kernel(g_ref, o_ref, r0, r1, s1, b, r2, c, r3, f, send, recv):
    core, place = coords()
    greet(all_partners(core, place))
    sibling = device_at(1 - core, place)
    out = Sender(send, recv)
    part, chunk, half_rows = 960, 240, 120
    first = [out.start(g_ref.at[1 - core, pl.ds(p * part, part)], r0.at[pl.ds(p * part, part)], sibling) for p in range(3)]
    level1a, level1b, level2, level3 = {}, {}, [], []

    def rows_at(p, j, half):
        return pl.multiple_of(p * part + j * chunk + half * half_rows, 8)

    for p in range(3):
        first[p].wait_recv()
        add_rows(r0, p * part, [(r0, p * part), (g_ref.at[core], p * part)], part, 96)
        axis = ORDERS[p][0]
        for half in range(2):
            near, far = ring_pairs(half)
            to = near(place[axis])
            device = device_at(core, moved_to(place, axis, to))
            level1a[p, half] = [
                out.start(r0.at[pl.ds(rows_at(p, j, half), half_rows)], r1.at[p, half, slot], device)
                for slot, j in ((1, far(to)), (0, to))
            ]
    for p in range(3):
        axis = ORDERS[p][0]
        for half in range(2):
            near, far = ring_pairs(half)
            to = far(place[axis])
            level1a[p, half][0].wait_recv()
            add_rows(s1.at[p, half], 0, [(r0, rows_at(p, to, half)), (r1.at[p, half, 1], 0)], half_rows, 40)
            level1b[p, half] = out.start(s1.at[p, half], r1.at[p, half, 2], device_at(core, moved_to(place, axis, to)))
    for p in range(3):
        mine = place[ORDERS[p][0]]
        for half in range(2):
            level1a[p, half][1].wait_recv()
            level1b[p, half].wait_recv()
            add_rows(b.at[p], half * half_rows,
                     [(r0, rows_at(p, mine, half)), (r1.at[p, half, 0], 0), (r1.at[p, half, 2], 0)], half_rows, 40)
        b[p, chunk:, :] = jnp.zeros((16, b.shape[2]), jnp.float32)
        axis = ORDERS[p][1]
        level2.append([
            out.start(b.at[p, pl.ds(pl.multiple_of(to[axis] * 64, 8), 64)], r2.at[p, k], device_at(core, to))
            for k, to in enumerate(peers(place, axis))
        ])
    for p in range(3):
        arrived(level2[p])
        mine = place[ORDERS[p][1]]
        add_rows(c.at[p], 0, [(b.at[p], mine * 64)] + [(r2.at[p, k], 0) for k in range(3)], 64, 64)
        axis = ORDERS[p][2]
        level3.append([
            out.start(c.at[p, pl.ds(pl.multiple_of(to[axis] * 16, 8), 16)], r3.at[p, k], device_at(core, to))
            for k, to in enumerate(peers(place, axis))
        ])
    gather3, gather2, gather1a, gather1b, last = [], [], {}, {}, []
    for p in range(3):
        arrived(level3[p])
        axis = ORDERS[p][2]
        row = pl.multiple_of(place[ORDERS[p][1]] * 64 + place[axis] * 16, 8)
        add_rows(f.at[p], row, [(c.at[p], place[axis] * 16)] + [(r3.at[p, k], 0) for k in range(3)], 16, 16)
        here = f.at[p, pl.ds(row, 16)]
        gather3.append([out.start(here, here, device_at(core, to)) for to in peers(place, axis)])
    for p in range(3):
        arrived(gather3[p])
        axis = ORDERS[p][1]
        here = f.at[p, pl.ds(pl.multiple_of(place[axis] * 64, 8), 64)]
        gather2.append([out.start(here, here, device_at(core, to)) for to in peers(place, axis)])

    def gathered(p, j, half):
        return o_ref.at[core, pl.ds(rows_at(p, j, half), half_rows)]

    for p in range(3):
        arrived(gather2[p])
        axis = ORDERS[p][0]
        x = place[axis]
        add_rows(o_ref.at[core], rows_at(p, x, 0), [(f.at[p], 0)], chunk, 48)
        for half in range(2):
            near, far = ring_pairs(half)
            here = gathered(p, x, half)
            gather1a[p, half] = out.start(here, here, device_at(core, moved_to(place, axis, far(x))))
            gather1b[p, half] = [out.start(here, here, device_at(core, moved_to(place, axis, near(x))))]
    for p in range(3):
        axis = ORDERS[p][0]
        x = place[axis]
        for half in range(2):
            near, far = ring_pairs(half)
            gather1a[p, half].wait_recv()
            here = gathered(p, far(x), half)
            gather1b[p, half].append(out.start(here, here, device_at(core, moved_to(place, axis, near(x)))))
    for p in range(3):
        for half in range(2):
            arrived(gather1b[p, half])
        here = o_ref.at[core, pl.ds(p * part, part)]
        last.append(out.start(here, here, sibling))
    arrived(last)
    out.finish()


def reduce_all(g):
    n = g.shape[-1]
    vm = lambda *s: pltpu.VMEM(s + (n,), jnp.float32)
    count = 3 + 18 + 9 * 4 + 18 + 3
    return pl.pallas_call(
        reduce_kernel,
        out_shape=jax.ShapeDtypeStruct(g.shape, jnp.float32),
        in_specs=[pl.BlockSpec(memory_space=pltpu.VMEM)],
        out_specs=pl.BlockSpec(memory_space=pltpu.VMEM),
        scratch_shapes=[vm(2880), vm(3, 2, 3, 120), vm(3, 2, 120), vm(3, 256), vm(3, 3, 64), vm(3, 64), vm(3, 3, 16),
                        vm(3, 256), pltpu.SemaphoreType.DMA((count,)), pltpu.SemaphoreType.DMA((count,))],
        compiler_params=kernel_params(0),
    )(g)


def view(ref, p, places, half=None):
    row, size = 0, 1024
    for c in places:
        size = size // 4
        row = row + c * size
    if half is not None:
        size = size // 2
        row = row + half * size
    return ref.at[p, pl.ds(pl.multiple_of(row, 16), size)]


def gram_kernel(p_ref, g_ref, rs_ref, rb_ref, spread_ref, gram_ref, right_ref, rows_ref, rgram_ref,
                r0, r1, a, own_ref, b, r2, c, r3, f, r4, acc, send, recv):
    core, place = coords()
    x, y, z = place
    quads = []
    for step in range(1, 8):
        quads.append(((x + step // 2) % 4, (y // 2) * 2 + (y + step % 2) % 2, z))
    partners = all_partners(core, place)
    partners += [device_at(core, to) for step, to in enumerate(quads, 1) if step // 2 and step % 2]
    greet(partners)
    out = Sender(send, recv)
    first = out.start(p_ref.at[1 - core], r0, device_at(1 - core, place))
    acc[...] = jnp.zeros_like(acc)

    def right_body(i, carry):
        x = g_ref[core, pl.ds(pl.multiple_of(i * 480, 16), 480), :]
        high = x.astype(jnp.bfloat16)
        low = (x - high.astype(jnp.float32)).astype(jnp.bfloat16)
        acc[0] += lax.dot_general(high, high, CONTRACT_ROWS, preferred_element_type=jnp.float32)
        acc[1] += lax.dot_general(high, low, CONTRACT_ROWS, preferred_element_type=jnp.float32)
        return carry

    lax.fori_loop(0, 6, right_body, 0)
    cross = acc[1]
    right = BETA * rs_ref[core] + (1.0 - BETA) * (acc[0] + (cross + cross.T))
    right_ref[...] = right
    first.wait_recv()
    add_rows(a, 0, [(r0, 0), (p_ref.at[core], 0)], PADDED, 96)
    block = lambda to: pl.multiple_of((to[0] * 2 + to[1] % 2) * 48, 16)
    quarter = [out.start(a.at[pl.ds(block(to), 48)], r1.at[k], device_at(core, to)) for k, to in enumerate(quads)]
    right_rows = jnp.dot(right_ref[...], rb_ref[core], precision=HIGHEST, preferred_element_type=jnp.float32)
    rows_ref[...] = right_rows
    rgram_ref[...] = lax.dot_general(right_rows, right_rows, CONTRACT_ROWS, precision=HIGHEST,
                                     preferred_element_type=jnp.float32)
    arrived(quarter)
    add_rows(own_ref, 0, [(a, block(place))] + [(r1.at[k], 0) for k in range(7)], 48, 48)
    own = own_ref[...]
    n = own.shape[1]
    spread3, spread2 = [], []
    for p in range(3):
        a1, a2, a3 = ORDERS[p]
        row = pl.multiple_of((place[a2] * 4 + place[a3]) * 16, 16)
        spread_ref[p, pl.ds(row, 16), :] = own_ref[pl.ds(16 * p, 16), :]
        here = spread_ref.at[p, pl.ds(row, 16)]
        spread3.append([out.start(here, here, device_at(core, to)) for to in peers(place, a3)])
    gram = lax.dot_general(own, own, CONTRACT_ROWS, precision=HIGHEST, preferred_element_type=jnp.float32)
    b[0, :, :] = gram[:128]
    b[1, :, :] = gram[128:256]
    b[2, :n - 256, :] = gram[256:]
    b[2, n - 256:, :] = jnp.zeros((PADDED - n, n), jnp.float32)
    level1, level2, level3, gather2, gather1 = [], [], [], [], []
    for p in range(3):
        axis = ORDERS[p][0]
        level1.append([
            out.start(b.at[p, pl.ds(pl.multiple_of(to[axis] * 32, 8), 32)], r2.at[p, k], device_at(core, to))
            for k, to in enumerate(peers(place, axis))
        ])
    for p in range(3):
        arrived(level1[p])
        add_rows(c.at[p], 0, [(b.at[p], place[ORDERS[p][0]] * 32)] + [(r2.at[p, k], 0) for k in range(3)], 32, 32)
        axis = ORDERS[p][1]
        level2.append([
            out.start(c.at[p, pl.ds(pl.multiple_of(to[axis] * 8, 8), 8)], r3.at[p, k], device_at(core, to))
            for k, to in enumerate(peers(place, axis))
        ])
    for p in range(3):
        arrived(spread3[p])
        a2 = ORDERS[p][1]
        here = spread_ref.at[p, pl.ds(pl.multiple_of(place[a2] * 64, 16), 64)]
        spread2.append([out.start(here, here, device_at(core, to)) for to in peers(place, a2)])
    for p in range(3):
        arrived(level2[p])
        add_rows(f.at[p], 0, [(c.at[p], place[ORDERS[p][1]] * 8)] + [(r3.at[p, k], 0) for k in range(3)], 8, 8)
        axis = ORDERS[p][2]
        level3.append([
            out.start(f.at[p], r4.at[p, k], device_at(core, to)) for k, to in enumerate(peers(place, axis))
        ])
    for p in range(3):
        arrived(level3[p])
        axis = ORDERS[p][1]
        row = pl.multiple_of(p * 128 + place[ORDERS[p][0]] * 32 + place[axis] * 8, 8)
        add_rows(gram_ref, row, [(f.at[p], 0)] + [(r4.at[p, k], 0) for k in range(3)], 8, 8)
        here = gram_ref.at[pl.ds(row, 8)]
        gather2.append([out.start(here, here, device_at(core, to)) for to in peers(place, axis)])
    for p in range(3):
        arrived(gather2[p])
        axis = ORDERS[p][0]
        here = gram_ref.at[pl.ds(pl.multiple_of(p * 128 + place[axis] * 32, 8), 32)]
        gather1.append([out.start(here, here, device_at(core, to)) for to in peers(place, axis)])
    for p in range(3):
        arrived(gather1[p])
        arrived(spread2[p])
    out.finish()


def gram_of_rows(partial, complete, right_stats, right_basis):
    n = partial.shape[-1]
    vm = lambda *s: pltpu.VMEM(s + (n,), jnp.float32)
    square = jax.ShapeDtypeStruct((n, n), jnp.float32)
    return pl.pallas_call(
        gram_kernel,
        out_shape=(jax.ShapeDtypeStruct((3, 256, n), jnp.float32), jax.ShapeDtypeStruct((PADDED, n), jnp.float32),
                   square, square, square),
        in_specs=[pl.BlockSpec(memory_space=pltpu.VMEM)] * 4,
        out_specs=(pl.BlockSpec(memory_space=pltpu.VMEM),) * 5,
        scratch_shapes=[vm(PADDED), vm(7, 48), vm(PADDED), vm(48), vm(3, 128), vm(3, 3, 32), vm(3, 32), vm(3, 3, 8),
                        vm(3, 8), vm(3, 3, 8), vm(2, n), pltpu.SemaphoreType.DMA((71,)), pltpu.SemaphoreType.DMA((71,))],
        compiler_params=kernel_params(1),
    )(partial, complete, right_stats, right_basis)


def three_wide(x):
    cols = x.shape[0]
    col = lax.broadcasted_iota(jnp.int32, x.shape, 0)
    before = jnp.where(col == 0, 0.0, pltpu.roll(x, 1, 0))
    after = jnp.where(col == cols - 1, 0.0, pltpu.roll(x, cols - 1, 0))
    return jnp.concatenate([v.astype(jnp.bfloat16) for v in (before, x, after)], axis=1)

def grads_kernel(remote, rows, cols, a_ref, v_ref, g_ref, w_ref, o_ref, rims, wide, wide_g, back, g_t, w_t, send, recv):
    n = a_ref.shape[1]
    copies = []
    if remote:
        me = lax.axis_index("space")
        up, down = (me + 7) % 8, (me + 1) % 8
        greet([{"space": up}, {"space": down}])
        for i, ref in enumerate((g_ref, v_ref, a_ref)):
            for side, (first, to) in enumerate((((rows - 1) * cols, down), (0, up))):
                copy = pltpu.make_async_remote_copy(src_ref=ref.at[pl.ds(first, cols)], dst_ref=rims.at[i, side],
                    send_sem=send.at[2 * i + side], recv_sem=recv.at[2 * i + side],
                    device_id={"space": to}, device_id_type=pl.DeviceIdType.MESH)
                copy.start()
                copies.append(copy)
        has = (me > 0, me < 7)
    else:
        has = (True, True)
    same = lambda x: x
    silu = lambda x: (x * jax.nn.sigmoid(x)).astype(jnp.bfloat16).astype(jnp.float32)
    def widen_rows(ref, dst, change):
        def body(r, carry):
            x = change(ref[pl.ds(pl.multiple_of(r * cols, 16), cols), :].astype(jnp.float32))
            dst[pl.ds(pl.multiple_of((r + 1) * cols, 16), cols), :] = three_wide(x)
            return carry
        lax.fori_loop(0, rows, body, 0)
    def widen_rims(i, dst, change):
        for side in range(2):
            if remote:
                copies[2 * i + side].wait_recv()
            x = change(rims[i, side].astype(jnp.float32))
            x = jnp.where(has[side], x, 0.0)
            dst[pl.ds(side * (rows + 1) * cols, cols), :] = three_wide(x)
    cells = rows * cols
    def gradient(layer):
        def body(dr, carry):
            start = pl.multiple_of(dr * cols, 16)
            for lane in range(0, 3 * n, 256):
                size = min(256, 3 * n - lane)
                part = jnp.dot(g_t[...], wide[pl.ds(start, cells), pl.ds(lane, size)],
                               preferred_element_type=jnp.float32)
                o_ref[layer, pl.ds(pl.multiple_of(dr * 3 * n + lane, 8), size), :] = part.T
            return carry
        lax.fori_loop(0, 3, body, 0)
    for dr in range(3):
        for seg in range(3):
            tap = w_ref[pl.ds((3 * dr + 2 - seg) * n, n), :]
            w_t[dr, pl.ds(seg * n, n), :] = tap.T
    widen_rows(v_ref, wide, silu)
    widen_rows(g_ref, wide_g, same)
    g_t[...] = g_ref[...].T
    widen_rims(0, wide_g, same)
    widen_rims(1, wide, silu)
    gradient(1)
    half = cells // 2
    def back_body(i, carry):
        first = pl.multiple_of(i * half, 16)
        total = None
        for dr in range(3):
            x = wide_g[pl.ds(pl.multiple_of(first + (2 - dr) * cols, 16), half), :]
            y = jnp.dot(x, w_t[dr], preferred_element_type=jnp.float32)
            total = y if total is None else total + y
        v = v_ref[pl.ds(first, half), :].astype(jnp.float32)
        s = jax.nn.sigmoid(v)
        back[pl.ds(first, half), :] = (total * (s * (1.0 + v * (1.0 - s)))).astype(jnp.bfloat16)
        return carry
    lax.fori_loop(0, 2, back_body, 0)
    g_t[...] = back[...].T
    widen_rows(a_ref, wide, same)
    widen_rims(2, wide, same)
    gradient(0)
    for copy in copies:
        copy.wait_send()

def gradients(inputs, preacts, cotangent, weights, remote=True, collective_id=3):
    rows, cols, n = inputs.shape
    flat = [x.reshape(rows * cols, n) for x in (inputs, preacts, cotangent)]
    b16 = jnp.bfloat16
    return pl.pallas_call(functools.partial(grads_kernel, remote, rows, cols),
        out_shape=jax.ShapeDtypeStruct((2, 9 * n, n), jnp.float32),
        in_specs=[pl.BlockSpec(memory_space=pltpu.VMEM)] * 4, out_specs=pl.BlockSpec(memory_space=pltpu.VMEM),
        scratch_shapes=[pltpu.VMEM((3, 2, cols, n), b16), pltpu.VMEM(((rows + 2) * cols, 3 * n), b16),
                        pltpu.VMEM(((rows + 2) * cols, 3 * n), b16), pltpu.VMEM((rows * cols, n), b16),
                        pltpu.VMEM((n, rows * cols), b16), pltpu.VMEM((3, 3 * n, n), b16),
                        pltpu.SemaphoreType.DMA((6,)), pltpu.SemaphoreType.DMA((6,))],
        compiler_params=kernel_params(collective_id if remote else None))(*flat, weights)


NB = 64


def diag_inverse(blocks):
    n = NB
    shape = (8, 2 * n)
    row = lax.broadcasted_iota(jnp.int32, (n, 2 * n), 0)
    col = lax.broadcasted_iota(jnp.int32, (n, 2 * n), 1)
    eye = jnp.where(row + n == col, 1.0, 0.0).astype(jnp.float32)
    sub = lax.broadcasted_iota(jnp.int32, shape, 0)
    tiles = []
    for b in blocks:
        x = jnp.concatenate([b, jnp.zeros((n, n), jnp.float32)], axis=1) + eye
        tiles.append([x[8 * t:8 * t + 8] for t in range(n // 8)])
    scales = [[None] * (n // 8) for _ in blocks]
    for tj in range(n // 8):
        steps = [[] for _ in blocks]
        for m in range(len(blocks)):
            x = tiles[m][tj]
            c = [jnp.broadcast_to(x[:, 8 * tj + k:8 * tj + k + 1], shape) for k in range(8)]
            scale = jnp.zeros(shape, jnp.float32)
            for k in range(8):
                rs = lax.rsqrt(jnp.broadcast_to(c[k][k:k + 1, :], shape))
                inv = rs * rs
                scale = jnp.where(sub == k, rs, scale)
                scaled = jnp.broadcast_to(x[k:k + 1, :], shape) * inv
                factors = []
                for kk in range(k + 1, 8):
                    factor = jnp.broadcast_to(c[kk][k:k + 1, :], shape) * inv
                    c[kk] = c[kk] - c[k] * factor
                    factors.append(factor)
                if k < 7:
                    x = x - jnp.where(sub > k, c[k], 0.0) * scaled
                steps[m].append((scaled, factors))
            tiles[m][tj] = x
            scales[m][tj] = scale
        for m in range(len(blocks)):
            for t in range(tj + 1, n // 8):
                x = tiles[m][t]
                c = [jnp.broadcast_to(x[:, 8 * tj + k:8 * tj + k + 1], shape) for k in range(8)]
                for k in range(8):
                    scaled, factors = steps[m][k]
                    for kk in range(k + 1, 8):
                        c[kk] = c[kk] - c[k] * factors[kk - k - 1]
                    x = x - c[k] * scaled
                tiles[m][t] = x
    out = []
    for m in range(len(blocks)):
        w = jnp.concatenate([tiles[m][t] * scales[m][t] for t in range(n // 8)], axis=0)
        out.append(w[:, n:])
    return out


def factor_step(m_ref, k):
    count, size, _ = m_ref.shape
    o = k * NB
    linv = diag_inverse([m_ref[m, o:o + NB, o:o + NB] for m in range(count)])
    for m in range(count):
        r = jnp.dot(linv[m], m_ref[m, o:o + NB, :], precision=HIGHEST, preferred_element_type=jnp.float32)
        pieces = ([r[:, :o]] if k else []) + [linv[m]] + ([r[:, o + NB:]] if o + NB < size else [])
        rz = jnp.concatenate(pieces, axis=1)
        if o + NB == size:
            m_ref[m, o:, :] = rz
            continue
        change = lax.dot_general(r[:, o + NB:], rz, CONTRACT_ROWS, precision=HIGHEST, preferred_element_type=jnp.float32)
        old = m_ref[m, o + NB:, :]
        col = lax.broadcasted_iota(jnp.int32, old.shape, 1)
        m_ref[m, o + NB:, :] = jnp.where((col >= o) & (col < o + NB), 0.0, old) - change
        col = lax.broadcasted_iota(jnp.int32, rz.shape, 1)
        m_ref[m, o:o + NB, :] = jnp.where(col < o + NB, rz, 0.0)


def factor_kernel(s_ref, gram_ref, right_ref, rows_ref, rgram_ref, o_ref, y_ref, m_ref, send, recv):
    core, place = coords()
    n = rgram_ref.shape[0]
    greet(all_partners(core, place))
    sibling = device_at(1 - core, place)
    out = Sender(send, recv)
    mine = o_ref.at[core]
    y_ref[core, 0] = right_ref[...]
    last = [out.start(y_ref.at[core, 0], y_ref.at[core, 0], sibling)]
    gather1a, gather1b = {}, {}
    for p in range(3):
        axis = ORDERS[p][0]
        x = place[axis]
        mine[p, pl.ds(pl.multiple_of(x * 256, 16), 256), :] = s_ref[p]
        for half in range(2):
            near, far = ring_pairs(half)
            here = view(mine, p, (x,), half)
            gather1a[p, half] = out.start(here, here, device_at(core, moved_to(place, axis, far(x))))
            gather1b[p, half] = [out.start(here, here, device_at(core, moved_to(place, axis, near(x))))]
    m_ref[0] = gram_ref[:n, :]
    m_ref[1] = rgram_ref[...]
    steps = n // NB
    for k in range(2):
        factor_step(m_ref, k)
    for p in range(3):
        axis = ORDERS[p][0]
        x = place[axis]
        for half in range(2):
            near, far = ring_pairs(half)
            gather1a[p, half].wait_recv()
            here = view(mine, p, (far(x),), half)
            gather1b[p, half].append(out.start(here, here, device_at(core, moved_to(place, axis, near(x)))))
    for k in range(2, steps - 1):
        factor_step(m_ref, k)
    for p in range(3):
        for half in range(2):
            arrived(gather1b[p, half])
        last.append(out.start(mine.at[p], mine.at[p], sibling))
    factor_step(m_ref, steps - 1)
    y_ref[core, 1] = m_ref[0]
    last.append(out.start(y_ref.at[core, 1], y_ref.at[core, 1], sibling))
    y_ref[core, 2] = math.sqrt(n) * lax.dot_general(
        rows_ref[...], m_ref[1], CONTRACT_COLS, precision=HIGHEST, preferred_element_type=jnp.float32
    )
    last.append(out.start(y_ref.at[core, 2], y_ref.at[core, 2], sibling))
    arrived(last)
    out.finish()


def factor(*pieces):
    n = pieces[0].shape[-1]
    return pl.pallas_call(
        factor_kernel,
        out_shape=(jax.ShapeDtypeStruct((2, 3, 1024, n), jnp.float32), jax.ShapeDtypeStruct((2, 3, n, n), jnp.float32)),
        in_specs=[pl.BlockSpec(memory_space=pltpu.VMEM)] * 5,
        out_specs=(pl.BlockSpec(memory_space=pltpu.VMEM),) * 2,
        scratch_shapes=[pltpu.VMEM((2, n, n), jnp.float32), pltpu.SemaphoreType.DMA((24,)), pltpu.SemaphoreType.DMA((24,))],
        compiler_params=kernel_params(2),
    )(*pieces)


def basis_kernel(full_rows, in_ref, y_ref, o_ref, dense):
    layer = pl.program_id(0)
    share = full_rows // 8

    def place_rows(block, carry):
        z, y_high = block // 2, block % 2
        for q in range(8):
            place = (q // 2, y_high * 2 + q % 2, z)
            for p in range(3):
                row = 48 * q + 16 * p
                size = min(16, share - row)
                if size <= 0:
                    continue
                a1, a2, a3 = ORDERS[p]
                src = pl.multiple_of(((place[a1] * 4 + place[a2]) * 4 + place[a3]) * 16, 16)
                dense[pl.ds(pl.multiple_of(block * share + row, 8), size), :] = in_ref[layer, p, pl.ds(src, size), :]
        return carry

    lax.fori_loop(0, 8, place_rows, 0)

    def halves(x):
        high = x.astype(jnp.bfloat16)
        return high, (x - high.astype(jnp.float32)).astype(jnp.bfloat16)

    times = lambda x, y: lax.dot_general(x, y, CONTRACT_COLS, preferred_element_type=jnp.float32)
    l_high, l_low = halves(y_ref[layer, 1] * math.sqrt(full_rows))
    for start in range(0, full_rows, 768):
        size = min(768, full_rows - start)
        high, low = halves(dense[start:start + size, :])
        o_ref[0, :, start:start + size] = times(l_high, high) + (times(l_high, low) + times(l_low, high))


def basis_of(spread_rows, both, full_rows):
    n = spread_rows.shape[-1]
    return pl.pallas_call(
        functools.partial(basis_kernel, full_rows),
        grid=(2,),
        out_shape=jax.ShapeDtypeStruct((2, n, full_rows), jnp.float32),
        in_specs=[pl.BlockSpec(memory_space=pltpu.VMEM)] * 2,
        out_specs=pl.BlockSpec((1, n, full_rows), lambda i: (i, 0, 0)),
        scratch_shapes=[pltpu.VMEM((full_rows, n), jnp.float32)],
        compiler_params=kernel_params(),
    )(spread_rows, both)


def local(inputs, preacts, cotangent, weights, left_stats, left_basis, right_stats, right_basis):
    row_share = left_stats.shape[1]
    col_share = left_stats.shape[2]
    full_rows, channels = weights.shape[1:]
    dp_index = lax.axis_index("dp")
    space_index = lax.axis_index("space")
    complete = reduce_all(gradients(inputs[0, 0], preacts[0, 0, 0], cotangent[0, 0], weights[0]))

    row_block = lax.dynamic_slice_in_dim(complete, space_index * row_share, row_share, 1)
    col_block = lax.dynamic_slice_in_dim(complete, dp_index * col_share, col_share, 1)
    left_new = BETA * left_stats + (1.0 - BETA) * lax.dot_general(
        row_block, col_block, (((2,), (2,)), ((0,), (0,))), precision=HIGHEST
    )
    partial = lax.dot_general(left_new, left_basis, (((2,), (1,)), ((0,), (0,))), precision=HIGHEST)
    padded = jnp.pad(partial, ((0, 0), (0, PADDED - row_share), (0, 0)))
    spread_rows, both = factor(*gram_of_rows(padded, complete, right_stats, right_basis))
    basis_out = jnp.swapaxes(basis_of(spread_rows, both, full_rows), 1, 2)
    return left_new, basis_out, both[:, 0], both[:, 2]


def solution(mesh):
    placed = (
        P("dp", None, "space", None, None),
        P(None, "dp", None, "space", None, None),
        P("dp", None, "space", None, None),
        P(),
        P(None, "space", "dp"),
        P(None, "dp", None),
        P(),
        P(),
    )
    return jax.shard_map(
        local,
        mesh=mesh,
        in_specs=placed,
        out_specs=(P(None, "space", "dp"), P(), P(), P()),
        check_vma=False,
    )
```

```python
import functools
import math

import jax
import jax.numpy as jnp
from jax import lax
from jax.experimental import pallas as pl
from jax.experimental.pallas import tpu as pltpu
from jax.sharding import PartitionSpec as P

BETA = 0.95
HIGHEST = lax.Precision.HIGHEST
CONTRACT_ROWS = (((0,), (0,)), ((), ()))
CONTRACT_COLS = (((1,), (1,)), ((), ()))
MESH = pl.DeviceIdType.MESH
ORDERS = ((0, 1, 2), (1, 2, 0), (2, 0, 1))
PADDED = 384


def kernel_params(collective_id=None):
    extra = {} if collective_id is None else {"collective_id": collective_id, "has_side_effects": True}
    return pltpu.CompilerParams(vmem_limit_bytes=50 * 1024 * 1024, **extra)

def coords():
    dp, space = lax.axis_index("dp"), lax.axis_index("space")
    core, x, y = dp % 2, (dp // 2) % 4, (space % 2) * 2 + dp // 8
    return core, (x, y, space // 2)

def device_at(core, place):
    x, y, z = place
    return {"dp": ((y % 2) * 4 + x) * 2 + core, "space": z * 2 + y // 2}

def shifted_place(place, axis, step):
    moved = list(place)
    moved[axis] = (place[axis] + step) % 4
    return tuple(moved)

def greet(partners):
    barrier = pltpu.get_barrier_semaphore()
    for partner in partners:
        pl.semaphore_signal(barrier, inc=1, device_id=partner, device_id_type=pl.DeviceIdType.MESH)
    pl.semaphore_wait(barrier, len(partners))

def add_rows(dst, dst_row, terms, rows, step):
    def body(i, carry):
        total = None
        for ref, start in terms:
            first = pl.multiple_of(start + i * step, 8)
            value = ref[pl.ds(first, step), :]
            total = value if total is None else total + value
        dst[pl.ds(pl.multiple_of(dst_row + i * step, 8), step), :] = total
        return carry
    lax.fori_loop(0, rows // step, body, 0)


class Sender:
    def __init__(self, send, recv):
        self.send, self.recv, self.copies = send, recv, []

    def start(self, src, dst, to):
        n = len(self.copies)
        copy = pltpu.make_async_remote_copy(
            src_ref=src, dst_ref=dst, send_sem=self.send.at[n], recv_sem=self.recv.at[n],
            device_id=to, device_id_type=MESH,
        )
        copy.start()
        self.copies.append(copy)
        return copy

    def finish(self):
        for copy in self.copies:
            copy.wait_send()


def arrived(copies):
    for copy in copies:
        copy.wait_recv()


def all_partners(core, place):
    partners = [device_at(1 - core, place)]
    for axis in range(3):
        for step in (1, 2, 3):
            partners.append(device_at(core, shifted_place(place, axis, step)))
    return partners


def moved_to(place, axis, value):
    moved = list(place)
    moved[axis] = value
    return tuple(moved)


def ring_pairs(half):
    near = lambda x: x + 1 - 2 * (x % 2)
    far = lambda x: 3 - x
    return (near, far) if half == 0 else (far, near)


def peers(place, axis):
    return [shifted_place(place, axis, step) for step in (1, 2, 3)]


def reduce_kernel(g_ref, o_ref, r0, r1, s1, b, r2, c, r3, f, send, recv):
    core, place = coords()
    greet(all_partners(core, place))
    sibling = device_at(1 - core, place)
    out = Sender(send, recv)
    part, chunk, half_rows = 960, 240, 120
    first = [out.start(g_ref.at[1 - core, pl.ds(p * part, part)], r0.at[pl.ds(p * part, part)], sibling) for p in range(3)]
    level1a, level1b, level2, level3 = {}, {}, [], []

    def rows_at(p, j, half):
        return pl.multiple_of(p * part + j * chunk + half * half_rows, 8)

    for p in range(3):
        first[p].wait_recv()
        add_rows(r0, p * part, [(r0, p * part), (g_ref.at[core], p * part)], part, 96)
        axis = ORDERS[p][0]
        for half in range(2):
            near, far = ring_pairs(half)
            to = near(place[axis])
            device = device_at(core, moved_to(place, axis, to))
            level1a[p, half] = [
                out.start(r0.at[pl.ds(rows_at(p, j, half), half_rows)], r1.at[p, half, slot], device)
                for slot, j in ((1, far(to)), (0, to))
            ]
    for p in range(3):
        axis = ORDERS[p][0]
        for half in range(2):
            near, far = ring_pairs(half)
            to = far(place[axis])
            level1a[p, half][0].wait_recv()
            add_rows(s1.at[p, half], 0, [(r0, rows_at(p, to, half)), (r1.at[p, half, 1], 0)], half_rows, 40)
            level1b[p, half] = out.start(s1.at[p, half], r1.at[p, half, 2], device_at(core, moved_to(place, axis, to)))
    for p in range(3):
        mine = place[ORDERS[p][0]]
        for half in range(2):
            level1a[p, half][1].wait_recv()
            level1b[p, half].wait_recv()
            add_rows(b.at[p], half * half_rows,
                     [(r0, rows_at(p, mine, half)), (r1.at[p, half, 0], 0), (r1.at[p, half, 2], 0)], half_rows, 40)
        b[p, chunk:, :] = jnp.zeros((16, b.shape[2]), jnp.float32)
        axis = ORDERS[p][1]
        level2.append([
            out.start(b.at[p, pl.ds(pl.multiple_of(to[axis] * 64, 8), 64)], r2.at[p, k], device_at(core, to))
            for k, to in enumerate(peers(place, axis))
        ])
    for p in range(3):
        arrived(level2[p])
        mine = place[ORDERS[p][1]]
        add_rows(c.at[p], 0, [(b.at[p], mine * 64)] + [(r2.at[p, k], 0) for k in range(3)], 64, 64)
        axis = ORDERS[p][2]
        level3.append([
            out.start(c.at[p, pl.ds(pl.multiple_of(to[axis] * 16, 8), 16)], r3.at[p, k], device_at(core, to))
            for k, to in enumerate(peers(place, axis))
        ])
    gather3, gather2, gather1a, gather1b, last = [], [], {}, {}, []
    for p in range(3):
        arrived(level3[p])
        axis = ORDERS[p][2]
        row = pl.multiple_of(place[ORDERS[p][1]] * 64 + place[axis] * 16, 8)
        add_rows(f.at[p], row, [(c.at[p], place[axis] * 16)] + [(r3.at[p, k], 0) for k in range(3)], 16, 16)
        here = f.at[p, pl.ds(row, 16)]
        gather3.append([out.start(here, here, device_at(core, to)) for to in peers(place, axis)])
    for p in range(3):
        arrived(gather3[p])
        axis = ORDERS[p][1]
        here = f.at[p, pl.ds(pl.multiple_of(place[axis] * 64, 8), 64)]
        gather2.append([out.start(here, here, device_at(core, to)) for to in peers(place, axis)])

    def gathered(p, j, half):
        return o_ref.at[core, pl.ds(rows_at(p, j, half), half_rows)]

    for p in range(3):
        arrived(gather2[p])
        axis = ORDERS[p][0]
        x = place[axis]
        add_rows(o_ref.at[core], rows_at(p, x, 0), [(f.at[p], 0)], chunk, 48)
        for half in range(2):
            near, far = ring_pairs(half)
            here = gathered(p, x, half)
            gather1a[p, half] = out.start(here, here, device_at(core, moved_to(place, axis, far(x))))
            gather1b[p, half] = [out.start(here, here, device_at(core, moved_to(place, axis, near(x))))]
    for p in range(3):
        axis = ORDERS[p][0]
        x = place[axis]
        for half in range(2):
            near, far = ring_pairs(half)
            gather1a[p, half].wait_recv()
            here = gathered(p, far(x), half)
            gather1b[p, half].append(out.start(here, here, device_at(core, moved_to(place, axis, near(x)))))
    for p in range(3):
        for half in range(2):
            arrived(gather1b[p, half])
        here = o_ref.at[core, pl.ds(p * part, part)]
        last.append(out.start(here, here, sibling))
    arrived(last)
    out.finish()


def reduce_all(g):
    n = g.shape[-1]
    vm = lambda *s: pltpu.VMEM(s + (n,), jnp.float32)
    count = 3 + 18 + 9 * 4 + 18 + 3
    return pl.pallas_call(
        reduce_kernel,
        out_shape=jax.ShapeDtypeStruct(g.shape, jnp.float32),
        in_specs=[pl.BlockSpec(memory_space=pltpu.VMEM)],
        out_specs=pl.BlockSpec(memory_space=pltpu.VMEM),
        scratch_shapes=[vm(2880), vm(3, 2, 3, 120), vm(3, 2, 120), vm(3, 256), vm(3, 3, 64), vm(3, 64), vm(3, 3, 16),
                        vm(3, 256), pltpu.SemaphoreType.DMA((count,)), pltpu.SemaphoreType.DMA((count,))],
        compiler_params=kernel_params(0),
    )(g)


def view(ref, p, places, half=None):
    row, size = 0, 1024
    for c in places:
        size = size // 4
        row = row + c * size
    if half is not None:
        size = size // 2
        row = row + half * size
    return ref.at[p, pl.ds(pl.multiple_of(row, 16), size)]


def gram_kernel(p_ref, g_ref, rs_ref, rb_ref, spread_ref, gram_ref, right_ref, rows_ref, rgram_ref,
                r0, r1, a, own_ref, b, r2, c, r3, f, r4, acc, send, recv):
    core, place = coords()
    x, y, z = place
    quads = []
    for step in range(1, 8):
        quads.append(((x + step // 2) % 4, (y // 2) * 2 + (y + step % 2) % 2, z))
    partners = all_partners(core, place)
    partners += [device_at(core, to) for step, to in enumerate(quads, 1) if step // 2 and step % 2]
    greet(partners)
    out = Sender(send, recv)
    first = out.start(p_ref.at[1 - core], r0, device_at(1 - core, place))
    acc[...] = jnp.zeros_like(acc)

    def right_body(i, carry):
        x = g_ref[core, pl.ds(pl.multiple_of(i * 480, 16), 480), :]
        high = x.astype(jnp.bfloat16)
        low = (x - high.astype(jnp.float32)).astype(jnp.bfloat16)
        acc[0] += lax.dot_general(high, high, CONTRACT_ROWS, preferred_element_type=jnp.float32)
        acc[1] += lax.dot_general(high, low, CONTRACT_ROWS, preferred_element_type=jnp.float32)
        return carry

    lax.fori_loop(0, 2, right_body, 0)
    first.wait_recv()
    add_rows(a, 0, [(r0, 0), (p_ref.at[core], 0)], PADDED, 96)
    block = lambda to: pl.multiple_of((to[0] * 2 + to[1] % 2) * 48, 16)
    quarter = [out.start(a.at[pl.ds(block(to), 48)], r1.at[k], device_at(core, to)) for k, to in enumerate(quads)]
    lax.fori_loop(2, 4, right_body, 0)
    arrived(quarter)
    add_rows(own_ref, 0, [(a, block(place))] + [(r1.at[k], 0) for k in range(7)], 48, 48)
    own = own_ref[...]
    n = own.shape[1]
    spread3, spread2 = [], []
    for p in range(3):
        a1, a2, a3 = ORDERS[p]
        row = pl.multiple_of((place[a2] * 4 + place[a3]) * 16, 16)
        spread_ref[p, pl.ds(row, 16), :] = own_ref[pl.ds(16 * p, 16), :]
        here = spread_ref.at[p, pl.ds(row, 16)]
        spread3.append([out.start(here, here, device_at(core, to)) for to in peers(place, a3)])
    gram = lax.dot_general(own, own, CONTRACT_ROWS, precision=HIGHEST, preferred_element_type=jnp.float32)
    b[0, :, :] = gram[:128]
    b[1, :, :] = gram[128:256]
    b[2, :n - 256, :] = gram[256:]
    b[2, n - 256:, :] = jnp.zeros((PADDED - n, n), jnp.float32)
    level1, level2, level3, gather2, gather1 = [], [], [], [], []
    for p in range(3):
        axis = ORDERS[p][0]
        level1.append([
            out.start(b.at[p, pl.ds(pl.multiple_of(to[axis] * 32, 8), 32)], r2.at[p, k], device_at(core, to))
            for k, to in enumerate(peers(place, axis))
        ])
    lax.fori_loop(4, 5, right_body, 0)
    for p in range(3):
        arrived(level1[p])
        add_rows(c.at[p], 0, [(b.at[p], place[ORDERS[p][0]] * 32)] + [(r2.at[p, k], 0) for k in range(3)], 32, 32)
        axis = ORDERS[p][1]
        level2.append([
            out.start(c.at[p, pl.ds(pl.multiple_of(to[axis] * 8, 8), 8)], r3.at[p, k], device_at(core, to))
            for k, to in enumerate(peers(place, axis))
        ])
    for p in range(3):
        arrived(spread3[p])
        a2 = ORDERS[p][1]
        here = spread_ref.at[p, pl.ds(pl.multiple_of(place[a2] * 64, 16), 64)]
        spread2.append([out.start(here, here, device_at(core, to)) for to in peers(place, a2)])
    lax.fori_loop(5, 6, right_body, 0)
    cross = acc[1]
    right_ref[...] = BETA * rs_ref[core] + (1.0 - BETA) * (acc[0] + (cross + cross.T))
    for p in range(3):
        arrived(level2[p])
        add_rows(f.at[p], 0, [(c.at[p], place[ORDERS[p][1]] * 8)] + [(r3.at[p, k], 0) for k in range(3)], 8, 8)
        axis = ORDERS[p][2]
        level3.append([
            out.start(f.at[p], r4.at[p, k], device_at(core, to)) for k, to in enumerate(peers(place, axis))
        ])
    right_rows = jnp.dot(right_ref[...], rb_ref[core], precision=HIGHEST, preferred_element_type=jnp.float32)
    rows_ref[...] = right_rows
    for p in range(3):
        arrived(level3[p])
        axis = ORDERS[p][1]
        row = pl.multiple_of(p * 128 + place[ORDERS[p][0]] * 32 + place[axis] * 8, 8)
        add_rows(gram_ref, row, [(f.at[p], 0)] + [(r4.at[p, k], 0) for k in range(3)], 8, 8)
        here = gram_ref.at[pl.ds(row, 8)]
        gather2.append([out.start(here, here, device_at(core, to)) for to in peers(place, axis)])
    rgram_ref[...] = lax.dot_general(right_rows, right_rows, CONTRACT_ROWS, precision=HIGHEST,
                                     preferred_element_type=jnp.float32)
    for p in range(3):
        arrived(gather2[p])
        axis = ORDERS[p][0]
        here = gram_ref.at[pl.ds(pl.multiple_of(p * 128 + place[axis] * 32, 8), 32)]
        gather1.append([out.start(here, here, device_at(core, to)) for to in peers(place, axis)])
    for p in range(3):
        arrived(gather1[p])
        arrived(spread2[p])
    out.finish()


def gram_of_rows(partial, complete, right_stats, right_basis):
    n = partial.shape[-1]
    vm = lambda *s: pltpu.VMEM(s + (n,), jnp.float32)
    square = jax.ShapeDtypeStruct((n, n), jnp.float32)
    return pl.pallas_call(
        gram_kernel,
        out_shape=(jax.ShapeDtypeStruct((3, 256, n), jnp.float32), jax.ShapeDtypeStruct((PADDED, n), jnp.float32),
                   square, square, square),
        in_specs=[pl.BlockSpec(memory_space=pltpu.VMEM)] * 4,
        out_specs=(pl.BlockSpec(memory_space=pltpu.VMEM),) * 5,
        scratch_shapes=[vm(PADDED), vm(7, 48), vm(PADDED), vm(48), vm(3, 128), vm(3, 3, 32), vm(3, 32), vm(3, 3, 8),
                        vm(3, 8), vm(3, 3, 8), vm(2, n), pltpu.SemaphoreType.DMA((71,)), pltpu.SemaphoreType.DMA((71,))],
        compiler_params=kernel_params(1),
    )(partial, complete, right_stats, right_basis)


LANES = 256

def widened(x):
    return jnp.concatenate([x, jnp.zeros((x.shape[0], LANES - x.shape[1]), x.dtype)], axis=1)

def put_taps(x, dst, r):
    n = x.shape[0]
    x = widened(x)
    lanes = pl.ds(pl.multiple_of(r * LANES, LANES), LANES)
    for i, v in enumerate((pltpu.roll(x, 1, 1), x, pltpu.roll(x, LANES - 1, 1))):
        dst[pl.ds(i * n, n), lanes] = v.astype(jnp.bfloat16)

def grads_kernel(remote, a_ref, v_ref, g_ref, w_ref, o_ref, rims, wide_v, wide_a, wide_g, back, g_n, w_l, send, recv):
    rows, n, cols = a_ref.shape
    span = rows * LANES
    copies = []
    if remote:
        me = lax.axis_index("space")
        up, down = (me + 7) % 8, (me + 1) % 8
        greet([{"space": up}, {"space": down}])
        for i, ref in enumerate((g_ref, a_ref)):
            for side, (first, to) in enumerate(((rows - 1, down), (0, up))):
                copy = pltpu.make_async_remote_copy(
                    src_ref=ref.at[first], dst_ref=rims.at[i, side],
                    send_sem=send.at[2 * i + side], recv_sem=recv.at[2 * i + side],
                    device_id={"space": to}, device_id_type=pl.DeviceIdType.MESH,
                )
                copy.start()
                copies.append(copy)
        has = (me > 0, me < 7)
    else:
        has = (False, False)
    same = lambda x: x
    silu = lambda x: (x * jax.nn.sigmoid(x)).astype(jnp.bfloat16).astype(jnp.float32)

    def widen_rows(ref, dst, change, offset):
        def body(r, carry):
            put_taps(change(ref[r].astype(jnp.float32)), dst, r + offset)
            return carry

        lax.fori_loop(0, rows, body, 0)

    def widen_rims(i, dst):
        for side in range(2):
            if remote:
                copies[2 * i + side].wait_recv()
            put_taps(jnp.where(has[side], rims[i, side].astype(jnp.float32), 0.0), dst, side * (rows + 1))

    def tap_rows(layer, d, cells, first):
        o_ref[layer, pl.ds(pl.multiple_of(d * 3 * n, 8), 3 * n), :] = jnp.dot(
            cells, g_n[pl.ds(pl.multiple_of(first, LANES), span), :], preferred_element_type=jnp.float32
        )

    widen_rows(g_ref, wide_g, same, 1)
    g_n[pl.ds(LANES, span), :] = wide_g[n:2 * n, LANES:LANES + span].T
    widen_rows(v_ref, wide_v, silu, 0)
    tap_rows(1, 1, wide_v[...], LANES)
    widen_rows(a_ref, wide_a, same, 1)
    for d in range(3):
        for s in range(3):
            t = 3 * d + 2 - s
            w_l[d, :, s * n:(s + 1) * n] = w_ref[:, t * n:(t + 1) * n].T
    widen_rims(0, wide_g)
    for row in (0, rows + 1):
        g_n[pl.ds(row * LANES, LANES), :] = wide_g[n:2 * n, row * LANES:(row + 1) * LANES].T

    def outer_taps(i, carry):
        tap_rows(1, 2 * i, wide_v[...], (2 - 2 * i) * LANES)
        return carry

    lax.fori_loop(0, 2, outer_taps, 0)
    half = span // 2

    def back_body(i, carry):
        total = None
        for d in range(3):
            lanes = pl.ds(pl.multiple_of(i * half + (2 - d) * LANES, LANES), half)
            y = jnp.dot(w_l[d], wide_g[:, lanes], preferred_element_type=jnp.float32)
            total = y if total is None else total + y
        back[:, pl.ds(pl.multiple_of(i * half, LANES), half)] = total
        return carry

    lax.fori_loop(0, 2, back_body, 0)

    def slope_body(r, carry):
        v = v_ref[r].astype(jnp.float32)
        s = jax.nn.sigmoid(v)
        start = pl.multiple_of(r * LANES, LANES)
        g0 = back[:, pl.ds(start, LANES)] * widened(s * (1.0 + v * (1.0 - s)))
        g_n[pl.ds(pl.multiple_of(start + LANES, LANES), LANES), :] = g0.astype(jnp.bfloat16).T
        return carry

    lax.fori_loop(0, rows, slope_body, 0)
    widen_rims(1, wide_a)

    def first_taps(d, carry):
        tap_rows(0, d, wide_a[:, pl.ds(pl.multiple_of(d * LANES, LANES), span)], LANES)
        return carry

    lax.fori_loop(0, 3, first_taps, 0)
    for copy in copies:
        copy.wait_send()

def gradients(inputs, preacts, cotangent, weights, remote=True, collective_id=3):
    rows, cols, n = inputs.shape
    turned = [jnp.swapaxes(x, -1, -2) for x in (inputs, preacts, cotangent, weights)]
    b16 = jnp.bfloat16
    return pl.pallas_call(functools.partial(grads_kernel, remote),
        out_shape=jax.ShapeDtypeStruct((2, 9 * n, n), jnp.float32),
        in_specs=[pl.BlockSpec(memory_space=pltpu.VMEM)] * 4, out_specs=pl.BlockSpec(memory_space=pltpu.VMEM),
        scratch_shapes=[pltpu.VMEM((2, 2, n, cols), b16), pltpu.VMEM((3 * n, rows * LANES), b16),
                        pltpu.VMEM((3 * n, (rows + 2) * LANES), b16), pltpu.VMEM((3 * n, (rows + 2) * LANES), b16),
                        pltpu.VMEM((n, rows * LANES), jnp.float32), pltpu.VMEM(((rows + 2) * LANES, n), b16),
                        pltpu.VMEM((3, n, 3 * n), b16), pltpu.SemaphoreType.DMA((4,)), pltpu.SemaphoreType.DMA((4,))],
        compiler_params=kernel_params(collective_id if remote else None))(*turned)


NB = 64


def diag_inverse(blocks):
    n = NB
    shape = (8, 2 * n)
    row = lax.broadcasted_iota(jnp.int32, (n, 2 * n), 0)
    col = lax.broadcasted_iota(jnp.int32, (n, 2 * n), 1)
    eye = jnp.where(row + n == col, 1.0, 0.0).astype(jnp.float32)
    sub = lax.broadcasted_iota(jnp.int32, shape, 0)
    tiles = []
    for b in blocks:
        x = jnp.concatenate([b, jnp.zeros((n, n), jnp.float32)], axis=1) + eye
        tiles.append([x[8 * t:8 * t + 8] for t in range(n // 8)])
    scales = [[None] * (n // 8) for _ in blocks]
    for tj in range(n // 8):
        steps = [[] for _ in blocks]
        for m in range(len(blocks)):
            x = tiles[m][tj]
            c = [jnp.broadcast_to(x[:, 8 * tj + k:8 * tj + k + 1], shape) for k in range(8)]
            scale = jnp.zeros(shape, jnp.float32)
            for k in range(8):
                rs = lax.rsqrt(jnp.broadcast_to(c[k][k:k + 1, :], shape))
                inv = rs * rs
                scale = jnp.where(sub == k, rs, scale)
                scaled = jnp.broadcast_to(x[k:k + 1, :], shape) * inv
                factors = []
                for kk in range(k + 1, 8):
                    factor = jnp.broadcast_to(c[kk][k:k + 1, :], shape) * inv
                    c[kk] = c[kk] - c[k] * factor
                    factors.append(factor)
                if k < 7:
                    x = x - jnp.where(sub > k, c[k], 0.0) * scaled
                steps[m].append((scaled, factors))
            tiles[m][tj] = x
            scales[m][tj] = scale
        for m in range(len(blocks)):
            for t in range(tj + 1, n // 8):
                x = tiles[m][t]
                c = [jnp.broadcast_to(x[:, 8 * tj + k:8 * tj + k + 1], shape) for k in range(8)]
                for k in range(8):
                    scaled, factors = steps[m][k]
                    for kk in range(k + 1, 8):
                        c[kk] = c[kk] - c[k] * factors[kk - k - 1]
                    x = x - c[k] * scaled
                tiles[m][t] = x
    out = []
    for m in range(len(blocks)):
        w = jnp.concatenate([tiles[m][t] * scales[m][t] for t in range(n // 8)], axis=0)
        out.append(w[:, n:])
    return out


def factor_step(m_ref, k):
    count, size, _ = m_ref.shape
    o = k * NB
    linv = diag_inverse([m_ref[m, o:o + NB, o:o + NB] for m in range(count)])
    for m in range(count):
        r = jnp.dot(linv[m], m_ref[m, o:o + NB, :], precision=HIGHEST, preferred_element_type=jnp.float32)
        pieces = ([r[:, :o]] if k else []) + [linv[m]] + ([r[:, o + NB:]] if o + NB < size else [])
        rz = jnp.concatenate(pieces, axis=1)
        if o + NB == size:
            m_ref[m, o:, :] = rz
            continue
        change = lax.dot_general(r[:, o + NB:], rz, CONTRACT_ROWS, precision=HIGHEST, preferred_element_type=jnp.float32)
        old = m_ref[m, o + NB:, :]
        col = lax.broadcasted_iota(jnp.int32, old.shape, 1)
        m_ref[m, o + NB:, :] = jnp.where((col >= o) & (col < o + NB), 0.0, old) - change
        col = lax.broadcasted_iota(jnp.int32, rz.shape, 1)
        m_ref[m, o:o + NB, :] = jnp.where(col < o + NB, rz, 0.0)


def factor_kernel(s_ref, gram_ref, right_ref, rows_ref, rgram_ref, o_ref, y_ref, m_ref, send, recv):
    core, place = coords()
    n = rgram_ref.shape[0]
    greet(all_partners(core, place))
    sibling = device_at(1 - core, place)
    out = Sender(send, recv)
    mine = o_ref.at[core]
    y_ref[core, 0] = right_ref[...]
    last = [out.start(y_ref.at[core, 0], y_ref.at[core, 0], sibling)]
    gather1a, gather1b = {}, {}
    for p in range(3):
        axis = ORDERS[p][0]
        x = place[axis]
        mine[p, pl.ds(pl.multiple_of(x * 256, 16), 256), :] = s_ref[p]
        for half in range(2):
            near, far = ring_pairs(half)
            here = view(mine, p, (x,), half)
            gather1a[p, half] = out.start(here, here, device_at(core, moved_to(place, axis, far(x))))
            gather1b[p, half] = [out.start(here, here, device_at(core, moved_to(place, axis, near(x))))]
    m_ref[0] = gram_ref[:n, :]
    m_ref[1] = rgram_ref[...]
    steps = n // NB
    for k in range(2):
        factor_step(m_ref, k)
    for p in range(3):
        axis = ORDERS[p][0]
        x = place[axis]
        for half in range(2):
            near, far = ring_pairs(half)
            gather1a[p, half].wait_recv()
            here = view(mine, p, (far(x),), half)
            gather1b[p, half].append(out.start(here, here, device_at(core, moved_to(place, axis, near(x)))))
    for k in range(2, steps - 1):
        factor_step(m_ref, k)
    for p in range(3):
        for half in range(2):
            arrived(gather1b[p, half])
        last.append(out.start(mine.at[p], mine.at[p], sibling))
    factor_step(m_ref, steps - 1)
    y_ref[core, 1] = m_ref[0]
    last.append(out.start(y_ref.at[core, 1], y_ref.at[core, 1], sibling))
    y_ref[core, 2] = math.sqrt(n) * lax.dot_general(
        rows_ref[...], m_ref[1], CONTRACT_COLS, precision=HIGHEST, preferred_element_type=jnp.float32
    )
    last.append(out.start(y_ref.at[core, 2], y_ref.at[core, 2], sibling))
    arrived(last)
    out.finish()


def factor(*pieces):
    n = pieces[0].shape[-1]
    return pl.pallas_call(
        factor_kernel,
        out_shape=(jax.ShapeDtypeStruct((2, 3, 1024, n), jnp.float32), jax.ShapeDtypeStruct((2, 3, n, n), jnp.float32)),
        in_specs=[pl.BlockSpec(memory_space=pltpu.VMEM)] * 5,
        out_specs=(pl.BlockSpec(memory_space=pltpu.VMEM),) * 2,
        scratch_shapes=[pltpu.VMEM((2, n, n), jnp.float32), pltpu.SemaphoreType.DMA((24,)), pltpu.SemaphoreType.DMA((24,))],
        compiler_params=kernel_params(2),
    )(*pieces)


def basis_kernel(full_rows, in_ref, y_ref, o_ref, dense):
    layer = pl.program_id(0)
    share = full_rows // 8

    def place_rows(block, carry):
        z, y_high = block // 2, block % 2
        for pair in range(4):
            loaded = []
            for q in (2 * pair, 2 * pair + 1):
                place = (q // 2, y_high * 2 + q % 2, z)
                for p in range(3):
                    row = 48 * q + 16 * p
                    size = min(16, share - row)
                    if size <= 0:
                        continue
                    a1, a2, a3 = ORDERS[p]
                    src = pl.multiple_of(((place[a1] * 4 + place[a2]) * 4 + place[a3]) * 16, 16)
                    loaded.append((row, size, in_ref[layer, p, pl.ds(src, size), :]))
            for row, size, value in loaded:
                dense[pl.ds(pl.multiple_of(block * share + row, 8), size), :] = value
        return carry

    lax.fori_loop(0, 8, place_rows, 0)

    def halves(x):
        high = x.astype(jnp.bfloat16)
        return high, (x - high.astype(jnp.float32)).astype(jnp.bfloat16)

    times = lambda x, y: lax.dot_general(x, y, CONTRACT_COLS, preferred_element_type=jnp.float32)
    l_high, l_low = halves(y_ref[layer, 1] * math.sqrt(full_rows))
    for start in range(0, full_rows, 768):
        size = min(768, full_rows - start)
        high, low = halves(dense[start:start + size, :])
        o_ref[0, :, start:start + size] = times(l_high, high) + (times(l_high, low) + times(l_low, high))


def basis_of(spread_rows, both, full_rows):
    n = spread_rows.shape[-1]
    return pl.pallas_call(
        functools.partial(basis_kernel, full_rows),
        grid=(2,),
        out_shape=jax.ShapeDtypeStruct((2, n, full_rows), jnp.float32),
        in_specs=[pl.BlockSpec(memory_space=pltpu.VMEM)] * 2,
        out_specs=pl.BlockSpec((1, n, full_rows), lambda i: (i, 0, 0)),
        scratch_shapes=[pltpu.VMEM((full_rows, n), jnp.float32)],
        compiler_params=kernel_params(),
    )(spread_rows, both)


def local(inputs, preacts, cotangent, weights, left_stats, left_basis, right_stats, right_basis):
    row_share = left_stats.shape[1]
    col_share = left_stats.shape[2]
    full_rows, channels = weights.shape[1:]
    dp_index = lax.axis_index("dp")
    space_index = lax.axis_index("space")
    complete = reduce_all(gradients(inputs[0, 0], preacts[0, 0, 0], cotangent[0, 0], weights[0]))

    row_block = lax.dynamic_slice_in_dim(complete, space_index * row_share, row_share, 1)
    col_block = lax.dynamic_slice_in_dim(complete, dp_index * col_share, col_share, 1)
    left_new = BETA * left_stats + (1.0 - BETA) * lax.dot_general(
        row_block, col_block, (((2,), (2,)), ((0,), (0,))), precision=HIGHEST
    )
    partial = lax.dot_general(left_new, left_basis, (((2,), (1,)), ((0,), (0,))), precision=HIGHEST)
    padded = jnp.pad(partial, ((0, 0), (0, PADDED - row_share), (0, 0)))
    spread_rows, both = factor(*gram_of_rows(padded, complete, right_stats, right_basis))
    basis_out = jnp.swapaxes(basis_of(spread_rows, both, full_rows), 1, 2)
    return left_new, basis_out, both[:, 0], both[:, 2]


def solution(mesh):
    placed = (
        P("dp", None, "space", None, None),
        P(None, "dp", None, "space", None, None),
        P("dp", None, "space", None, None),
        P(),
        P(None, "space", "dp"),
        P(None, "dp", None),
        P(),
        P(),
    )
    return jax.shard_map(
        local,
        mesh=mesh,
        in_specs=placed,
        out_specs=(P(None, "space", "dp"), P(), P(), P()),
        check_vma=False,
    )
```

```python
import functools
import math

import jax
import jax.numpy as jnp
from jax import lax
from jax.experimental import pallas as pl
from jax.experimental.pallas import tpu as pltpu
from jax.sharding import PartitionSpec as P

BETA = 0.95
HIGHEST = lax.Precision.HIGHEST
CONTRACT_ROWS = (((0,), (0,)), ((), ()))
CONTRACT_COLS = (((1,), (1,)), ((), ()))
MESH = pl.DeviceIdType.MESH
ORDERS = ((0, 1, 2), (1, 2, 0), (2, 0, 1))
PADDED = 384


def kernel_params(collective_id=None):
    extra = {} if collective_id is None else {"collective_id": collective_id, "has_side_effects": True}
    return pltpu.CompilerParams(vmem_limit_bytes=50 * 1024 * 1024, **extra)

def coords():
    dp, space = lax.axis_index("dp"), lax.axis_index("space")
    core, x, y = dp % 2, (dp // 2) % 4, (space % 2) * 2 + dp // 8
    return core, (x, y, space // 2)

def device_at(core, place):
    x, y, z = place
    return {"dp": ((y % 2) * 4 + x) * 2 + core, "space": z * 2 + y // 2}

def shifted_place(place, axis, step):
    moved = list(place)
    moved[axis] = (place[axis] + step) % 4
    return tuple(moved)

def greet(partners):
    barrier = pltpu.get_barrier_semaphore()
    for partner in partners:
        pl.semaphore_signal(barrier, inc=1, device_id=partner, device_id_type=pl.DeviceIdType.MESH)
    pl.semaphore_wait(barrier, len(partners))

def add_rows(dst, dst_row, terms, rows, step):
    def body(i, carry):
        total = None
        for ref, start in terms:
            first = pl.multiple_of(start + i * step, 8)
            value = ref[pl.ds(first, step), :]
            total = value if total is None else total + value
        dst[pl.ds(pl.multiple_of(dst_row + i * step, 8), step), :] = total
        return carry
    lax.fori_loop(0, rows // step, body, 0)


class Sender:
    def __init__(self, send, recv):
        self.send, self.recv, self.copies = send, recv, []

    def start(self, src, dst, to):
        n = len(self.copies)
        copy = pltpu.make_async_remote_copy(
            src_ref=src, dst_ref=dst, send_sem=self.send.at[n], recv_sem=self.recv.at[n],
            device_id=to, device_id_type=MESH,
        )
        copy.start()
        self.copies.append(copy)
        return copy

    def finish(self):
        for copy in self.copies:
            copy.wait_send()


def arrived(copies):
    for copy in copies:
        copy.wait_recv()


def all_partners(core, place):
    partners = [device_at(1 - core, place)]
    for axis in range(3):
        for step in (1, 2, 3):
            partners.append(device_at(core, shifted_place(place, axis, step)))
    return partners


def moved_to(place, axis, value):
    moved = list(place)
    moved[axis] = value
    return tuple(moved)


def ring_pairs(half):
    near = lambda x: x + 1 - 2 * (x % 2)
    far = lambda x: 3 - x
    return (near, far) if half == 0 else (far, near)


def peers(place, axis):
    return [shifted_place(place, axis, step) for step in (1, 2, 3)]


def reduce_layer(out, core, place, part_ref, o_ref, r0, r1, s1, b, r2, c, r3, f):
    part, chunk = 480, 120
    halves = ((0, 64), (64, 56))
    mine = core * 3 * part
    sibling = device_at(1 - core, place)
    theirs = (1 - core) * 3 * part
    first = [
        out.start(part_ref.at[pl.ds(pl.multiple_of(theirs + p * part, 8), part)], r0.at[pl.ds(p * part, part)], sibling)
        for p in range(3)
    ]
    yield
    level1a, level1b, level2, level3 = {}, {}, [], []

    def rows_at(p, j, half):
        return pl.multiple_of(p * part + j * chunk + halves[half][0], 8)

    for p in range(3):
        first[p].wait_recv()
        add_rows(r0, p * part, [(r0, p * part), (part_ref, mine + p * part)], part, 96)
        axis = ORDERS[p][0]
        for half in range(2):
            near, far = ring_pairs(half)
            to = near(place[axis])
            size = halves[half][1]
            level1a[p, half] = [
                out.start(r0.at[pl.ds(rows_at(p, j, half), size)], r1.at[p, half, slot, pl.ds(0, size)],
                          device_at(core, moved_to(place, axis, to)))
                for slot, j in ((1, far(to)), (0, to))
            ]
    yield
    for p in range(3):
        axis = ORDERS[p][0]
        for half in range(2):
            near, far = ring_pairs(half)
            to = far(place[axis])
            size = halves[half][1]
            level1a[p, half][0].wait_recv()
            add_rows(s1.at[p, half], 0, [(r0, rows_at(p, to, half)), (r1.at[p, half, 1], 0)], size, size)
            level1b[p, half] = out.start(s1.at[p, half, pl.ds(0, size)], r1.at[p, half, 2, pl.ds(0, size)],
                                         device_at(core, moved_to(place, axis, to)))
    yield
    for p in range(3):
        x = place[ORDERS[p][0]]
        for half in range(2):
            level1a[p, half][1].wait_recv()
            level1b[p, half].wait_recv()
            add_rows(b.at[p], halves[half][0],
                     [(r0, rows_at(p, x, half)), (r1.at[p, half, 0], 0), (r1.at[p, half, 2], 0)],
                     halves[half][1], halves[half][1])
        b[p, chunk:, :] = jnp.zeros((8, b.shape[2]), jnp.float32)
        axis = ORDERS[p][1]
        level2.append([
            out.start(b.at[p, pl.ds(pl.multiple_of(to[axis] * 32, 8), 32)], r2.at[p, k], device_at(core, to))
            for k, to in enumerate(peers(place, axis))
        ])
    yield
    for p in range(3):
        arrived(level2[p])
        add_rows(c.at[p], 0, [(b.at[p], place[ORDERS[p][1]] * 32)] + [(r2.at[p, k], 0) for k in range(3)], 32, 32)
        axis = ORDERS[p][2]
        level3.append([
            out.start(c.at[p, pl.ds(pl.multiple_of(to[axis] * 8, 8), 8)], r3.at[p, k], device_at(core, to))
            for k, to in enumerate(peers(place, axis))
        ])
    yield
    gather3, gather2, gather1a, gather1b, last = [], [], {}, {}, []
    for p in range(3):
        arrived(level3[p])
        axis = ORDERS[p][2]
        row = pl.multiple_of(place[ORDERS[p][1]] * 32 + place[axis] * 8, 8)
        add_rows(f.at[p], row, [(c.at[p], place[axis] * 8)] + [(r3.at[p, k], 0) for k in range(3)], 8, 8)
        here = f.at[p, pl.ds(row, 8)]
        gather3.append([out.start(here, here, device_at(core, to)) for to in peers(place, axis)])
    yield
    for p in range(3):
        arrived(gather3[p])
        axis = ORDERS[p][1]
        here = f.at[p, pl.ds(pl.multiple_of(place[axis] * 32, 8), 32)]
        gather2.append([out.start(here, here, device_at(core, to)) for to in peers(place, axis)])
    yield

    def gathered(p, j, half):
        return o_ref.at[pl.ds(pl.multiple_of(mine + rows_at(p, j, half), 8), halves[half][1])]

    for p in range(3):
        arrived(gather2[p])
        axis = ORDERS[p][0]
        x = place[axis]
        add_rows(o_ref, mine + rows_at(p, x, 0), [(f.at[p], 0)], chunk, 40)
        for half in range(2):
            near, far = ring_pairs(half)
            here = gathered(p, x, half)
            gather1a[p, half] = out.start(here, here, device_at(core, moved_to(place, axis, far(x))))
            gather1b[p, half] = [out.start(here, here, device_at(core, moved_to(place, axis, near(x))))]
    yield
    for p in range(3):
        axis = ORDERS[p][0]
        x = place[axis]
        for half in range(2):
            near, far = ring_pairs(half)
            gather1a[p, half].wait_recv()
            here = gathered(p, far(x), half)
            gather1b[p, half].append(out.start(here, here, device_at(core, moved_to(place, axis, near(x)))))
    yield
    for p in range(3):
        for half in range(2):
            arrived(gather1b[p, half])
        here = o_ref.at[pl.ds(pl.multiple_of(mine + p * part, 8), part)]
        last.append(out.start(here, here, sibling))
    yield
    arrived(last)


def reduce_scratch(n):
    vm = lambda *shape: pltpu.VMEM((2,) + shape + (n,), jnp.float32)
    return [vm(1440), vm(3, 2, 3, 64), vm(3, 2, 64), vm(3, 128), vm(3, 3, 32), vm(3, 32), vm(3, 3, 8), vm(3, 128)]


def view(ref, p, places, half=None):
    row, size = 0, 1024
    for c in places:
        size = size // 4
        row = row + c * size
    if half is not None:
        size = size // 2
        row = row + half * size
    return ref.at[p, pl.ds(pl.multiple_of(row, 16), size)]


def gram_kernel(p_ref, g_ref, rs_ref, rb_ref, spread_ref, gram_ref, right_ref, rows_ref, rgram_ref,
                r0, r1, a, own_ref, b, r2, c, r3, f, r4, acc, send, recv):
    core, place = coords()
    x, y, z = place
    quads = []
    for step in range(1, 8):
        quads.append(((x + step // 2) % 4, (y // 2) * 2 + (y + step % 2) % 2, z))
    partners = all_partners(core, place)
    partners += [device_at(core, to) for step, to in enumerate(quads, 1) if step // 2 and step % 2]
    greet(partners)
    out = Sender(send, recv)
    first = out.start(p_ref.at[1 - core], r0, device_at(1 - core, place))
    acc[...] = jnp.zeros_like(acc)

    def right_body(i, carry):
        x = g_ref[core, pl.ds(pl.multiple_of(i * 480, 16), 480), :]
        high = x.astype(jnp.bfloat16)
        low = (x - high.astype(jnp.float32)).astype(jnp.bfloat16)
        acc[0] += lax.dot_general(high, high, CONTRACT_ROWS, preferred_element_type=jnp.float32)
        acc[1] += lax.dot_general(high, low, CONTRACT_ROWS, preferred_element_type=jnp.float32)
        return carry

    lax.fori_loop(0, 2, right_body, 0)
    first.wait_recv()
    add_rows(a, 0, [(r0, 0), (p_ref.at[core], 0)], PADDED, 96)
    block = lambda to: pl.multiple_of((to[0] * 2 + to[1] % 2) * 48, 16)
    quarter = [out.start(a.at[pl.ds(block(to), 48)], r1.at[k], device_at(core, to)) for k, to in enumerate(quads)]
    lax.fori_loop(2, 4, right_body, 0)
    arrived(quarter)
    add_rows(own_ref, 0, [(a, block(place))] + [(r1.at[k], 0) for k in range(7)], 48, 48)
    own = own_ref[...]
    n = own.shape[1]
    spread3, spread2 = [], []
    for p in range(3):
        a1, a2, a3 = ORDERS[p]
        row = pl.multiple_of((place[a2] * 4 + place[a3]) * 16, 16)
        spread_ref[p, pl.ds(row, 16), :] = own_ref[pl.ds(16 * p, 16), :]
        here = spread_ref.at[p, pl.ds(row, 16)]
        spread3.append([out.start(here, here, device_at(core, to)) for to in peers(place, a3)])
    gram = lax.dot_general(own, own, CONTRACT_ROWS, precision=HIGHEST, preferred_element_type=jnp.float32)
    b[0, :, :] = gram[:128]
    b[1, :, :] = gram[128:256]
    b[2, :n - 256, :] = gram[256:]
    b[2, n - 256:, :] = jnp.zeros((PADDED - n, n), jnp.float32)
    level1, level2, level3, gather2, gather1 = [], [], [], [], []
    for p in range(3):
        axis = ORDERS[p][0]
        level1.append([
            out.start(b.at[p, pl.ds(pl.multiple_of(to[axis] * 32, 8), 32)], r2.at[p, k], device_at(core, to))
            for k, to in enumerate(peers(place, axis))
        ])
    lax.fori_loop(4, 5, right_body, 0)
    for p in range(3):
        arrived(level1[p])
        add_rows(c.at[p], 0, [(b.at[p], place[ORDERS[p][0]] * 32)] + [(r2.at[p, k], 0) for k in range(3)], 32, 32)
        axis = ORDERS[p][1]
        level2.append([
            out.start(c.at[p, pl.ds(pl.multiple_of(to[axis] * 8, 8), 8)], r3.at[p, k], device_at(core, to))
            for k, to in enumerate(peers(place, axis))
        ])
    for p in range(3):
        arrived(spread3[p])
        a2 = ORDERS[p][1]
        here = spread_ref.at[p, pl.ds(pl.multiple_of(place[a2] * 64, 16), 64)]
        spread2.append([out.start(here, here, device_at(core, to)) for to in peers(place, a2)])
    lax.fori_loop(5, 6, right_body, 0)
    cross = acc[1]
    right_ref[...] = BETA * rs_ref[core] + (1.0 - BETA) * (acc[0] + (cross + cross.T))
    for p in range(3):
        arrived(level2[p])
        add_rows(f.at[p], 0, [(c.at[p], place[ORDERS[p][1]] * 8)] + [(r3.at[p, k], 0) for k in range(3)], 8, 8)
        axis = ORDERS[p][2]
        level3.append([
            out.start(f.at[p], r4.at[p, k], device_at(core, to)) for k, to in enumerate(peers(place, axis))
        ])
    right_rows = jnp.dot(right_ref[...], rb_ref[core], precision=HIGHEST, preferred_element_type=jnp.float32)
    rows_ref[...] = right_rows
    for p in range(3):
        arrived(level3[p])
        axis = ORDERS[p][1]
        row = pl.multiple_of(p * 128 + place[ORDERS[p][0]] * 32 + place[axis] * 8, 8)
        add_rows(gram_ref, row, [(f.at[p], 0)] + [(r4.at[p, k], 0) for k in range(3)], 8, 8)
        here = gram_ref.at[pl.ds(row, 8)]
        gather2.append([out.start(here, here, device_at(core, to)) for to in peers(place, axis)])
    rgram_ref[...] = lax.dot_general(right_rows, right_rows, CONTRACT_ROWS, precision=HIGHEST,
                                     preferred_element_type=jnp.float32)
    for p in range(3):
        arrived(gather2[p])
        axis = ORDERS[p][0]
        here = gram_ref.at[pl.ds(pl.multiple_of(p * 128 + place[axis] * 32, 8), 32)]
        gather1.append([out.start(here, here, device_at(core, to)) for to in peers(place, axis)])
    for p in range(3):
        arrived(gather1[p])
        arrived(spread2[p])
    out.finish()


def gram_of_rows(partial, complete, right_stats, right_basis):
    n = partial.shape[-1]
    vm = lambda *s: pltpu.VMEM(s + (n,), jnp.float32)
    square = jax.ShapeDtypeStruct((n, n), jnp.float32)
    return pl.pallas_call(
        gram_kernel,
        out_shape=(jax.ShapeDtypeStruct((3, 256, n), jnp.float32), jax.ShapeDtypeStruct((PADDED, n), jnp.float32),
                   square, square, square),
        in_specs=[pl.BlockSpec(memory_space=pltpu.VMEM)] * 4,
        out_specs=(pl.BlockSpec(memory_space=pltpu.VMEM),) * 5,
        scratch_shapes=[vm(PADDED), vm(7, 48), vm(PADDED), vm(48), vm(3, 128), vm(3, 3, 32), vm(3, 32), vm(3, 3, 8),
                        vm(3, 8), vm(3, 3, 8), vm(2, n), pltpu.SemaphoreType.DMA((71,)), pltpu.SemaphoreType.DMA((71,))],
        compiler_params=kernel_params(1),
    )(partial, complete, right_stats, right_basis)


LANES = 256

def widened(x):
    return jnp.concatenate([x, jnp.zeros((x.shape[0], LANES - x.shape[1]), x.dtype)], axis=1)

def put_taps(x, dst, r):
    n = x.shape[0]
    x = widened(x)
    lanes = pl.ds(pl.multiple_of(r * LANES, LANES), LANES)
    for i, v in enumerate((pltpu.roll(x, 1, 1), x, pltpu.roll(x, LANES - 1, 1))):
        dst[pl.ds(i * n, n), lanes] = v.astype(jnp.bfloat16)

def grads_kernel(a_ref, v_ref, g_ref, w_ref, total_ref, o_ref, rims, wide_v, wide_a, wide_g, back, g_n, w_l, *rest):
    rows, n, cols = a_ref.shape
    span = rows * LANES
    scratch, (send, recv) = rest[:-2], rest[-2:]
    core, place = coords()
    me = lax.axis_index("space")
    up, down = (me + 7) % 8, (me + 1) % 8
    x, y, z = place
    greet(all_partners(core, place)
          + [device_at(core, (x, (y + 2) % 4, (z + 1 - 2 * (1 - y // 2)) % 4))])
    out = Sender(send, recv)
    copies = []
    for i, ref in enumerate((g_ref, a_ref)):
        for side, (first, to) in enumerate(((rows - 1, down), (0, up))):
            copies.append(out.start(ref.at[first], rims.at[i, side], {"dp": lax.axis_index("dp"), "space": to}))
    has = (me > 0, me < 7)
    stages = [
        reduce_layer(out, core, place, o_ref.at[layer], total_ref.at[layer], *[ref.at[layer] for ref in scratch])
        for layer in range(2)
    ]
    go = lambda layer: next(stages[layer], None)
    same = lambda x: x
    silu = lambda x: (x * jax.nn.sigmoid(x)).astype(jnp.bfloat16).astype(jnp.float32)

    def widen_rows(ref, dst, change, offset):
        def body(r, carry):
            put_taps(change(ref[r].astype(jnp.float32)), dst, r + offset)
            return carry

        lax.fori_loop(0, rows, body, 0)

    def widen_rims(i, dst):
        for side in range(2):
            copies[2 * i + side].wait_recv()
            put_taps(jnp.where(has[side], rims[i, side].astype(jnp.float32), 0.0), dst, side * (rows + 1))

    def tap_rows(layer, d, cells, first):
        o_ref[layer, pl.ds(pl.multiple_of(d * 3 * n, 8), 3 * n), :] = jnp.dot(
            cells, g_n[pl.ds(pl.multiple_of(first, LANES), span), :], preferred_element_type=jnp.float32
        )

    widen_rows(g_ref, wide_g, same, 1)
    g_n[pl.ds(LANES, span), :] = wide_g[n:2 * n, LANES:LANES + span].T
    widen_rows(v_ref, wide_v, silu, 0)
    tap_rows(1, 1, wide_v[...], LANES)
    widen_rows(a_ref, wide_a, same, 1)
    for d in range(3):
        for s in range(3):
            t = 3 * d + 2 - s
            w_l[d, :, s * n:(s + 1) * n] = w_ref[:, t * n:(t + 1) * n].T
    widen_rims(0, wide_g)
    for row in (0, rows + 1):
        g_n[pl.ds(row * LANES, LANES), :] = wide_g[n:2 * n, row * LANES:(row + 1) * LANES].T

    def outer_taps(i, carry):
        tap_rows(1, 2 * i, wide_v[...], (2 - 2 * i) * LANES)
        return carry

    lax.fori_loop(0, 2, outer_taps, 0)
    go(1)
    half = span // 2

    def back_body(i, carry):
        total = None
        for d in range(3):
            lanes = pl.ds(pl.multiple_of(i * half + (2 - d) * LANES, LANES), half)
            y = jnp.dot(w_l[d], wide_g[:, lanes], preferred_element_type=jnp.float32)
            total = y if total is None else total + y
        back[:, pl.ds(pl.multiple_of(i * half, LANES), half)] = total
        return carry

    lax.fori_loop(0, 2, back_body, 0)
    go(1)

    def slope_body(r, carry):
        v = v_ref[r].astype(jnp.float32)
        s = jax.nn.sigmoid(v)
        start = pl.multiple_of(r * LANES, LANES)
        g0 = back[:, pl.ds(start, LANES)] * widened(s * (1.0 + v * (1.0 - s)))
        g_n[pl.ds(pl.multiple_of(start + LANES, LANES), LANES), :] = g0.astype(jnp.bfloat16).T
        return carry

    lax.fori_loop(0, rows, slope_body, 0)
    widen_rims(1, wide_a)

    def first_taps(d, carry):
        tap_rows(0, d, wide_a[:, pl.ds(pl.multiple_of(d * LANES, LANES), span)], LANES)
        return carry

    for d in range(3):
        go(1)
        lax.fori_loop(d, d + 1, first_taps, 0)
    for _ in range(12):
        go(0)
        go(1)
    out.finish()


def gradients(inputs, preacts, cotangent, weights):
    rows, cols, n = inputs.shape
    turned = [jnp.swapaxes(x, -1, -2) for x in (inputs, preacts, cotangent, weights)]
    b16 = jnp.bfloat16
    count = 4 + 2 * (3 + 18 + 9 * 4 + 18 + 3)
    return pl.pallas_call(
        grads_kernel,
        out_shape=jax.ShapeDtypeStruct((2, 9 * n, n), jnp.float32),
        in_specs=[pl.BlockSpec(memory_space=pltpu.VMEM)] * 4,
        out_specs=pl.BlockSpec(memory_space=pltpu.VMEM),
        scratch_shapes=[pltpu.VMEM((2, 9 * n, n), jnp.float32), pltpu.VMEM((2, 2, n, cols), b16),
                        pltpu.VMEM((3 * n, rows * LANES), b16), pltpu.VMEM((3 * n, (rows + 2) * LANES), b16),
                        pltpu.VMEM((3 * n, (rows + 2) * LANES), b16), pltpu.VMEM((n, rows * LANES), jnp.float32),
                        pltpu.VMEM(((rows + 2) * LANES, n), b16), pltpu.VMEM((3, n, 3 * n), b16),
                        *reduce_scratch(n), pltpu.SemaphoreType.DMA((count,)), pltpu.SemaphoreType.DMA((count,))],
        compiler_params=pltpu.CompilerParams(vmem_limit_bytes=60 * 1000 * 1000, collective_id=0, has_side_effects=True),
    )(*turned)


NB = 64


def diag_inverse(blocks):
    n = NB
    shape = (8, 2 * n)
    row = lax.broadcasted_iota(jnp.int32, (n, 2 * n), 0)
    col = lax.broadcasted_iota(jnp.int32, (n, 2 * n), 1)
    eye = jnp.where(row + n == col, 1.0, 0.0).astype(jnp.float32)
    sub = lax.broadcasted_iota(jnp.int32, shape, 0)
    tiles = []
    for b in blocks:
        x = jnp.concatenate([b, jnp.zeros((n, n), jnp.float32)], axis=1) + eye
        tiles.append([x[8 * t:8 * t + 8] for t in range(n // 8)])
    scales = [[None] * (n // 8) for _ in blocks]
    for tj in range(n // 8):
        steps = [[] for _ in blocks]
        for m in range(len(blocks)):
            x = tiles[m][tj]
            c = [jnp.broadcast_to(x[:, 8 * tj + k:8 * tj + k + 1], shape) for k in range(8)]
            scale = jnp.zeros(shape, jnp.float32)
            for k in range(8):
                rs = lax.rsqrt(jnp.broadcast_to(c[k][k:k + 1, :], shape))
                inv = rs * rs
                scale = jnp.where(sub == k, rs, scale)
                scaled = jnp.broadcast_to(x[k:k + 1, :], shape) * inv
                factors = []
                for kk in range(k + 1, 8):
                    factor = jnp.broadcast_to(c[kk][k:k + 1, :], shape) * inv
                    c[kk] = c[kk] - c[k] * factor
                    factors.append(factor)
                if k < 7:
                    x = x - jnp.where(sub > k, c[k], 0.0) * scaled
                steps[m].append((scaled, factors))
            tiles[m][tj] = x
            scales[m][tj] = scale
        for m in range(len(blocks)):
            for t in range(tj + 1, n // 8):
                x = tiles[m][t]
                c = [jnp.broadcast_to(x[:, 8 * tj + k:8 * tj + k + 1], shape) for k in range(8)]
                for k in range(8):
                    scaled, factors = steps[m][k]
                    for kk in range(k + 1, 8):
                        c[kk] = c[kk] - c[k] * factors[kk - k - 1]
                    x = x - c[k] * scaled
                tiles[m][t] = x
    out = []
    for m in range(len(blocks)):
        w = jnp.concatenate([tiles[m][t] * scales[m][t] for t in range(n // 8)], axis=0)
        out.append(w[:, n:])
    return out


def factor_step(m_ref, k):
    count, size, _ = m_ref.shape
    o = k * NB
    linv = diag_inverse([m_ref[m, o:o + NB, o:o + NB] for m in range(count)])
    for m in range(count):
        r = jnp.dot(linv[m], m_ref[m, o:o + NB, :], precision=HIGHEST, preferred_element_type=jnp.float32)
        pieces = ([r[:, :o]] if k else []) + [linv[m]] + ([r[:, o + NB:]] if o + NB < size else [])
        rz = jnp.concatenate(pieces, axis=1)
        if o + NB == size:
            m_ref[m, o:, :] = rz
            continue
        change = lax.dot_general(r[:, o + NB:], rz, CONTRACT_ROWS, precision=HIGHEST, preferred_element_type=jnp.float32)
        old = m_ref[m, o + NB:, :]
        col = lax.broadcasted_iota(jnp.int32, old.shape, 1)
        m_ref[m, o + NB:, :] = jnp.where((col >= o) & (col < o + NB), 0.0, old) - change
        col = lax.broadcasted_iota(jnp.int32, rz.shape, 1)
        m_ref[m, o:o + NB, :] = jnp.where(col < o + NB, rz, 0.0)


def factor_kernel(s_ref, gram_ref, right_ref, rows_ref, rgram_ref, o_ref, y_ref, m_ref, send, recv):
    core, place = coords()
    n = rgram_ref.shape[0]
    greet(all_partners(core, place))
    sibling = device_at(1 - core, place)
    out = Sender(send, recv)
    mine = o_ref.at[core]
    y_ref[core, 0] = right_ref[...]
    last = [out.start(y_ref.at[core, 0], y_ref.at[core, 0], sibling)]
    gather1a, gather1b = {}, {}
    for p in range(3):
        axis = ORDERS[p][0]
        x = place[axis]
        mine[p, pl.ds(pl.multiple_of(x * 256, 16), 256), :] = s_ref[p]
        for half in range(2):
            near, far = ring_pairs(half)
            here = view(mine, p, (x,), half)
            gather1a[p, half] = out.start(here, here, device_at(core, moved_to(place, axis, far(x))))
            gather1b[p, half] = [out.start(here, here, device_at(core, moved_to(place, axis, near(x))))]
    m_ref[0] = gram_ref[:n, :]
    m_ref[1] = rgram_ref[...]
    steps = n // NB
    for k in range(2):
        factor_step(m_ref, k)
    for p in range(3):
        axis = ORDERS[p][0]
        x = place[axis]
        for half in range(2):
            near, far = ring_pairs(half)
            gather1a[p, half].wait_recv()
            here = view(mine, p, (far(x),), half)
            gather1b[p, half].append(out.start(here, here, device_at(core, moved_to(place, axis, near(x)))))
    for k in range(2, steps - 1):
        factor_step(m_ref, k)
    for p in range(3):
        for half in range(2):
            arrived(gather1b[p, half])
        last.append(out.start(mine.at[p], mine.at[p], sibling))
    factor_step(m_ref, steps - 1)
    y_ref[core, 1] = m_ref[0]
    last.append(out.start(y_ref.at[core, 1], y_ref.at[core, 1], sibling))
    y_ref[core, 2] = math.sqrt(n) * lax.dot_general(
        rows_ref[...], m_ref[1], CONTRACT_COLS, precision=HIGHEST, preferred_element_type=jnp.float32
    )
    last.append(out.start(y_ref.at[core, 2], y_ref.at[core, 2], sibling))
    arrived(last)
    out.finish()


def factor(*pieces):
    n = pieces[0].shape[-1]
    return pl.pallas_call(
        factor_kernel,
        out_shape=(jax.ShapeDtypeStruct((2, 3, 1024, n), jnp.float32), jax.ShapeDtypeStruct((2, 3, n, n), jnp.float32)),
        in_specs=[pl.BlockSpec(memory_space=pltpu.VMEM)] * 5,
        out_specs=(pl.BlockSpec(memory_space=pltpu.VMEM),) * 2,
        scratch_shapes=[pltpu.VMEM((2, n, n), jnp.float32), pltpu.SemaphoreType.DMA((24,)), pltpu.SemaphoreType.DMA((24,))],
        compiler_params=kernel_params(2),
    )(*pieces)


def basis_kernel(full_rows, in_ref, y_ref, o_ref, dense):
    layer = pl.program_id(0)
    share = full_rows // 8

    def place_rows(block, carry):
        z, y_high = block // 2, block % 2
        for pair in range(4):
            loaded = []
            for q in (2 * pair, 2 * pair + 1):
                place = (q // 2, y_high * 2 + q % 2, z)
                for p in range(3):
                    row = 48 * q + 16 * p
                    size = min(16, share - row)
                    if size <= 0:
                        continue
                    a1, a2, a3 = ORDERS[p]
                    src = pl.multiple_of(((place[a1] * 4 + place[a2]) * 4 + place[a3]) * 16, 16)
                    loaded.append((row, size, in_ref[layer, p, pl.ds(src, size), :]))
            for row, size, value in loaded:
                dense[pl.ds(pl.multiple_of(block * share + row, 8), size), :] = value
        return carry

    lax.fori_loop(0, 8, place_rows, 0)

    def halves(x):
        high = x.astype(jnp.bfloat16)
        return high, (x - high.astype(jnp.float32)).astype(jnp.bfloat16)

    times = lambda x, y: lax.dot_general(x, y, CONTRACT_COLS, preferred_element_type=jnp.float32)
    l_high, l_low = halves(y_ref[layer, 1] * math.sqrt(full_rows))
    for start in range(0, full_rows, 768):
        size = min(768, full_rows - start)
        high, low = halves(dense[start:start + size, :])
        o_ref[0, :, start:start + size] = times(l_high, high) + (times(l_high, low) + times(l_low, high))


def basis_of(spread_rows, both, full_rows):
    n = spread_rows.shape[-1]
    return pl.pallas_call(
        functools.partial(basis_kernel, full_rows),
        grid=(2,),
        out_shape=jax.ShapeDtypeStruct((2, n, full_rows), jnp.float32),
        in_specs=[pl.BlockSpec(memory_space=pltpu.VMEM)] * 2,
        out_specs=pl.BlockSpec((1, n, full_rows), lambda i: (i, 0, 0)),
        scratch_shapes=[pltpu.VMEM((full_rows, n), jnp.float32)],
        compiler_params=kernel_params(),
    )(spread_rows, both)


def local(inputs, preacts, cotangent, weights, left_stats, left_basis, right_stats, right_basis):
    row_share = left_stats.shape[1]
    col_share = left_stats.shape[2]
    full_rows, channels = weights.shape[1:]
    dp_index = lax.axis_index("dp")
    space_index = lax.axis_index("space")
    complete = gradients(inputs[0, 0], preacts[0, 0, 0], cotangent[0, 0], weights[0])

    row_block = lax.dynamic_slice_in_dim(complete, space_index * row_share, row_share, 1)
    col_block = lax.dynamic_slice_in_dim(complete, dp_index * col_share, col_share, 1)
    left_new = BETA * left_stats + (1.0 - BETA) * lax.dot_general(
        row_block, col_block, (((2,), (2,)), ((0,), (0,))), precision=HIGHEST
    )
    partial = lax.dot_general(left_new, left_basis, (((2,), (1,)), ((0,), (0,))), precision=HIGHEST)
    padded = jnp.pad(partial, ((0, 0), (0, PADDED - row_share), (0, 0)))
    spread_rows, both = factor(*gram_of_rows(padded, complete, right_stats, right_basis))
    basis_out = jnp.swapaxes(basis_of(spread_rows, both, full_rows), 1, 2)
    return left_new, basis_out, both[:, 0], both[:, 2]


def solution(mesh):
    placed = (
        P("dp", None, "space", None, None),
        P(None, "dp", None, "space", None, None),
        P("dp", None, "space", None, None),
        P(),
        P(None, "space", "dp"),
        P(None, "dp", None),
        P(),
        P(),
    )
    return jax.shard_map(
        local,
        mesh=mesh,
        in_specs=placed,
        out_specs=(P(None, "space", "dp"), P(), P(), P()),
        check_vma=False,
    )
```

```python
import functools
import math

import jax
import jax.numpy as jnp
from jax import lax
from jax.experimental import pallas as pl
from jax.experimental.pallas import tpu as pltpu
from jax.sharding import PartitionSpec as P

BETA = 0.95
HIGHEST = lax.Precision.HIGHEST
CONTRACT_ROWS = (((0,), (0,)), ((), ()))
CONTRACT_COLS = (((1,), (1,)), ((), ()))
MESH = pl.DeviceIdType.MESH
ORDERS = ((0, 1, 2), (1, 2, 0), (2, 0, 1))
PADDED = 384


def kernel_params(collective_id=None):
    extra = {} if collective_id is None else {"collective_id": collective_id, "has_side_effects": True}
    return pltpu.CompilerParams(vmem_limit_bytes=50 * 1024 * 1024, **extra)

def coords():
    dp, space = lax.axis_index("dp"), lax.axis_index("space")
    core, x, y = dp % 2, (dp // 2) % 4, (space % 2) * 2 + dp // 8
    return core, (x, y, space // 2)

def device_at(core, place):
    x, y, z = place
    return {"dp": ((y % 2) * 4 + x) * 2 + core, "space": z * 2 + y // 2}

def shifted_place(place, axis, step):
    moved = list(place)
    moved[axis] = (place[axis] + step) % 4
    return tuple(moved)

def greet(partners):
    barrier = pltpu.get_barrier_semaphore()
    for partner in partners:
        pl.semaphore_signal(barrier, inc=1, device_id=partner, device_id_type=pl.DeviceIdType.MESH)
    pl.semaphore_wait(barrier, len(partners))

def add_rows(dst, dst_row, terms, rows, step):
    def body(i, carry):
        total = None
        for ref, start in terms:
            first = pl.multiple_of(start + i * step, 8)
            value = ref[pl.ds(first, step), :]
            total = value if total is None else total + value
        dst[pl.ds(pl.multiple_of(dst_row + i * step, 8), step), :] = total
        return carry
    lax.fori_loop(0, rows // step, body, 0)


class Sender:
    def __init__(self, send, recv):
        self.send, self.recv, self.copies = send, recv, []

    def start(self, src, dst, to):
        n = len(self.copies)
        copy = pltpu.make_async_remote_copy(
            src_ref=src, dst_ref=dst, send_sem=self.send.at[n], recv_sem=self.recv.at[n],
            device_id=to, device_id_type=MESH,
        )
        copy.start()
        self.copies.append(copy)
        return copy

    def finish(self):
        for copy in self.copies:
            copy.wait_send()


def arrived(copies):
    for copy in copies:
        copy.wait_recv()


def all_partners(core, place):
    partners = [device_at(1 - core, place)]
    for axis in range(3):
        for step in (1, 2, 3):
            partners.append(device_at(core, shifted_place(place, axis, step)))
    return partners


def moved_to(place, axis, value):
    moved = list(place)
    moved[axis] = value
    return tuple(moved)


def ring_pairs(half):
    near = lambda x: x + 1 - 2 * (x % 2)
    far = lambda x: 3 - x
    return (near, far) if half == 0 else (far, near)


def peers(place, axis):
    return [shifted_place(place, axis, step) for step in (1, 2, 3)]


def reduce_layer(out, core, place, part_ref, o_ref, r0, r1, s1, b, r2, c, r3, f):
    part, chunk = 480, 120
    halves = ((0, 64), (64, 56))
    mine = core * 3 * part
    sibling = device_at(1 - core, place)
    theirs = (1 - core) * 3 * part
    first = [
        out.start(part_ref.at[pl.ds(pl.multiple_of(theirs + p * part, 8), part)], r0.at[pl.ds(p * part, part)], sibling)
        for p in range(3)
    ]
    yield
    level1a, level1b, level2, level3 = {}, {}, [], []

    def rows_at(p, j, half):
        return pl.multiple_of(p * part + j * chunk + halves[half][0], 8)

    for p in range(3):
        first[p].wait_recv()
        add_rows(r0, p * part, [(r0, p * part), (part_ref, mine + p * part)], part, 96)
        axis = ORDERS[p][0]
        for half in range(2):
            near, far = ring_pairs(half)
            to = near(place[axis])
            size = halves[half][1]
            level1a[p, half] = [
                out.start(r0.at[pl.ds(rows_at(p, j, half), size)], r1.at[p, half, slot, pl.ds(0, size)],
                          device_at(core, moved_to(place, axis, to)))
                for slot, j in ((1, far(to)), (0, to))
            ]
    yield
    for p in range(3):
        axis = ORDERS[p][0]
        for half in range(2):
            near, far = ring_pairs(half)
            to = far(place[axis])
            size = halves[half][1]
            level1a[p, half][0].wait_recv()
            add_rows(s1.at[p, half], 0, [(r0, rows_at(p, to, half)), (r1.at[p, half, 1], 0)], size, size)
            level1b[p, half] = out.start(s1.at[p, half, pl.ds(0, size)], r1.at[p, half, 2, pl.ds(0, size)],
                                         device_at(core, moved_to(place, axis, to)))
    yield
    for p in range(3):
        x = place[ORDERS[p][0]]
        for half in range(2):
            level1a[p, half][1].wait_recv()
            level1b[p, half].wait_recv()
            add_rows(b.at[p], halves[half][0],
                     [(r0, rows_at(p, x, half)), (r1.at[p, half, 0], 0), (r1.at[p, half, 2], 0)],
                     halves[half][1], halves[half][1])
        b[p, chunk:, :] = jnp.zeros((8, b.shape[2]), jnp.float32)
        axis = ORDERS[p][1]
        level2.append([
            out.start(b.at[p, pl.ds(pl.multiple_of(to[axis] * 32, 8), 32)], r2.at[p, k], device_at(core, to))
            for k, to in enumerate(peers(place, axis))
        ])
    yield
    for p in range(3):
        arrived(level2[p])
        add_rows(c.at[p], 0, [(b.at[p], place[ORDERS[p][1]] * 32)] + [(r2.at[p, k], 0) for k in range(3)], 32, 32)
        axis = ORDERS[p][2]
        level3.append([
            out.start(c.at[p, pl.ds(pl.multiple_of(to[axis] * 8, 8), 8)], r3.at[p, k], device_at(core, to))
            for k, to in enumerate(peers(place, axis))
        ])
    yield
    gather3, gather2, gather1a, gather1b, last = [], [], {}, {}, []
    for p in range(3):
        arrived(level3[p])
        axis = ORDERS[p][2]
        row = pl.multiple_of(place[ORDERS[p][1]] * 32 + place[axis] * 8, 8)
        add_rows(f.at[p], row, [(c.at[p], place[axis] * 8)] + [(r3.at[p, k], 0) for k in range(3)], 8, 8)
        here = f.at[p, pl.ds(row, 8)]
        gather3.append([out.start(here, here, device_at(core, to)) for to in peers(place, axis)])
    yield
    for p in range(3):
        arrived(gather3[p])
        axis = ORDERS[p][1]
        here = f.at[p, pl.ds(pl.multiple_of(place[axis] * 32, 8), 32)]
        gather2.append([out.start(here, here, device_at(core, to)) for to in peers(place, axis)])
    yield

    def gathered(p, j, half):
        return o_ref.at[pl.ds(pl.multiple_of(mine + rows_at(p, j, half), 8), halves[half][1])]

    for p in range(3):
        arrived(gather2[p])
        axis = ORDERS[p][0]
        x = place[axis]
        add_rows(o_ref, mine + rows_at(p, x, 0), [(f.at[p], 0)], chunk, 40)
        for half in range(2):
            near, far = ring_pairs(half)
            here = gathered(p, x, half)
            gather1a[p, half] = out.start(here, here, device_at(core, moved_to(place, axis, far(x))))
            gather1b[p, half] = [out.start(here, here, device_at(core, moved_to(place, axis, near(x))))]
    yield
    for p in range(3):
        axis = ORDERS[p][0]
        x = place[axis]
        for half in range(2):
            near, far = ring_pairs(half)
            gather1a[p, half].wait_recv()
            here = gathered(p, far(x), half)
            gather1b[p, half].append(out.start(here, here, device_at(core, moved_to(place, axis, near(x)))))
    yield
    for p in range(3):
        for half in range(2):
            arrived(gather1b[p, half])
        here = o_ref.at[pl.ds(pl.multiple_of(mine + p * part, 8), part)]
        last.append(out.start(here, here, sibling))
    yield
    arrived(last)


def reduce_scratch(n):
    vm = lambda *shape: pltpu.VMEM((2,) + shape + (n,), jnp.float32)
    return [vm(1440), vm(3, 2, 3, 64), vm(3, 2, 64), vm(3, 128), vm(3, 3, 32), vm(3, 32), vm(3, 3, 8), vm(3, 128)]


def view(ref, p, places, half=None):
    row, size = 0, 1024
    for c in places:
        size = size // 4
        row = row + c * size
    if half is not None:
        size = size // 2
        row = row + half * size
    return ref.at[p, pl.ds(pl.multiple_of(row, 16), size)]


def gram_kernel(p_ref, g_ref, rs_ref, rb_ref, spread_ref, gram_ref, right_ref, rows_ref, rgram_ref,
                r0, r1, a, own_ref, b, r2, c, r3, f, r4, acc, send, recv):
    core, place = coords()
    x, y, z = place
    quads = []
    for step in range(1, 8):
        quads.append(((x + step // 2) % 4, (y // 2) * 2 + (y + step % 2) % 2, z))
    partners = all_partners(core, place)
    partners += [device_at(core, to) for step, to in enumerate(quads, 1) if step // 2 and step % 2]
    greet(partners)
    out = Sender(send, recv)
    given = p_ref.shape[1]
    first = out.start(p_ref.at[1 - core], r0, device_at(1 - core, place))
    acc[...] = jnp.zeros_like(acc)

    def right_body(i, carry):
        x = g_ref[core, pl.ds(pl.multiple_of(i * 480, 16), 480), :]
        high = x.astype(jnp.bfloat16)
        low = (x - high.astype(jnp.float32)).astype(jnp.bfloat16)
        acc[0] += lax.dot_general(high, high, CONTRACT_ROWS, preferred_element_type=jnp.float32)
        acc[1] += lax.dot_general(high, low, CONTRACT_ROWS, preferred_element_type=jnp.float32)
        return carry

    lax.fori_loop(0, 2, right_body, 0)
    first.wait_recv()
    add_rows(a, 0, [(r0, 0), (p_ref.at[core], 0)], given, 72)
    a[given:, :] = jnp.zeros((PADDED - given, a.shape[1]), jnp.float32)
    block = lambda to: pl.multiple_of((to[0] * 2 + to[1] % 2) * 48, 16)
    quarter = [out.start(a.at[pl.ds(block(to), 48)], r1.at[k], device_at(core, to)) for k, to in enumerate(quads)]
    lax.fori_loop(2, 4, right_body, 0)
    arrived(quarter)
    add_rows(own_ref, 0, [(a, block(place))] + [(r1.at[k], 0) for k in range(7)], 48, 48)
    own = own_ref[...]
    n = own.shape[1]
    spread3, spread2 = [], []
    for p in range(3):
        a1, a2, a3 = ORDERS[p]
        row = pl.multiple_of((place[a2] * 4 + place[a3]) * 16, 16)
        spread_ref[p, pl.ds(row, 16), :] = own_ref[pl.ds(16 * p, 16), :]
        here = spread_ref.at[p, pl.ds(row, 16)]
        spread3.append([out.start(here, here, device_at(core, to)) for to in peers(place, a3)])
    gram = lax.dot_general(own, own, CONTRACT_ROWS, precision=HIGHEST, preferred_element_type=jnp.float32)
    b[0, :, :] = gram[:128]
    b[1, :, :] = gram[128:256]
    b[2, :n - 256, :] = gram[256:]
    b[2, n - 256:, :] = jnp.zeros((PADDED - n, n), jnp.float32)
    level1, level2, level3, gather2, gather1 = [], [], [], [], []
    for p in range(3):
        axis = ORDERS[p][0]
        level1.append([
            out.start(b.at[p, pl.ds(pl.multiple_of(to[axis] * 32, 8), 32)], r2.at[p, k], device_at(core, to))
            for k, to in enumerate(peers(place, axis))
        ])
    lax.fori_loop(4, 5, right_body, 0)
    for p in range(3):
        arrived(level1[p])
        add_rows(c.at[p], 0, [(b.at[p], place[ORDERS[p][0]] * 32)] + [(r2.at[p, k], 0) for k in range(3)], 32, 32)
        axis = ORDERS[p][1]
        level2.append([
            out.start(c.at[p, pl.ds(pl.multiple_of(to[axis] * 8, 8), 8)], r3.at[p, k], device_at(core, to))
            for k, to in enumerate(peers(place, axis))
        ])
    for p in range(3):
        arrived(spread3[p])
        a2 = ORDERS[p][1]
        here = spread_ref.at[p, pl.ds(pl.multiple_of(place[a2] * 64, 16), 64)]
        spread2.append([out.start(here, here, device_at(core, to)) for to in peers(place, a2)])
    lax.fori_loop(5, 6, right_body, 0)
    cross = acc[1]
    right_ref[...] = BETA * rs_ref[core] + (1.0 - BETA) * (acc[0] + (cross + cross.T))
    for p in range(3):
        arrived(level2[p])
        add_rows(f.at[p], 0, [(c.at[p], place[ORDERS[p][1]] * 8)] + [(r3.at[p, k], 0) for k in range(3)], 8, 8)
        axis = ORDERS[p][2]
        level3.append([
            out.start(f.at[p], r4.at[p, k], device_at(core, to)) for k, to in enumerate(peers(place, axis))
        ])
    right_rows = jnp.dot(right_ref[...], rb_ref[core], precision=HIGHEST, preferred_element_type=jnp.float32)
    rows_ref[...] = right_rows
    for p in range(3):
        arrived(level3[p])
        axis = ORDERS[p][1]
        row = pl.multiple_of(p * 128 + place[ORDERS[p][0]] * 32 + place[axis] * 8, 8)
        add_rows(gram_ref, row, [(f.at[p], 0)] + [(r4.at[p, k], 0) for k in range(3)], 8, 8)
        here = gram_ref.at[pl.ds(row, 8)]
        gather2.append([out.start(here, here, device_at(core, to)) for to in peers(place, axis)])
    rgram_ref[...] = lax.dot_general(right_rows, right_rows, CONTRACT_ROWS, precision=HIGHEST,
                                     preferred_element_type=jnp.float32)
    for p in range(3):
        arrived(gather2[p])
        axis = ORDERS[p][0]
        here = gram_ref.at[pl.ds(pl.multiple_of(p * 128 + place[axis] * 32, 8), 32)]
        gather1.append([out.start(here, here, device_at(core, to)) for to in peers(place, axis)])
    for p in range(3):
        arrived(gather1[p])
        arrived(spread2[p])
    out.finish()


def gram_of_rows(partial, complete, right_stats, right_basis):
    n = partial.shape[-1]
    vm = lambda *s: pltpu.VMEM(s + (n,), jnp.float32)
    square = jax.ShapeDtypeStruct((n, n), jnp.float32)
    return pl.pallas_call(
        gram_kernel,
        out_shape=(jax.ShapeDtypeStruct((3, 256, n), jnp.float32), jax.ShapeDtypeStruct((PADDED, n), jnp.float32),
                   square, square, square),
        in_specs=[pl.BlockSpec(memory_space=pltpu.VMEM)] * 4,
        out_specs=(pl.BlockSpec(memory_space=pltpu.VMEM),) * 5,
        scratch_shapes=[vm(partial.shape[1]), vm(7, 48), vm(PADDED), vm(48), vm(3, 128), vm(3, 3, 32), vm(3, 32), vm(3, 3, 8),
                        vm(3, 8), vm(3, 3, 8), vm(2, n), pltpu.SemaphoreType.DMA((71,)), pltpu.SemaphoreType.DMA((71,))],
        compiler_params=kernel_params(1),
    )(partial, complete, right_stats, right_basis)


LANES = 256

def widened(x):
    return jnp.concatenate([x, jnp.zeros((x.shape[0], LANES - x.shape[1]), x.dtype)], axis=1)

def put_taps(x, dst, r):
    n = x.shape[0]
    x = widened(x)
    lanes = pl.ds(pl.multiple_of(r * LANES, LANES), LANES)
    for i, v in enumerate((pltpu.roll(x, 1, 1), x, pltpu.roll(x, LANES - 1, 1))):
        dst[pl.ds(i * n, n), lanes] = v.astype(jnp.bfloat16)

def grads_kernel(a_ref, v_ref, g_ref, w_ref, total_ref, o_ref, rims, wide_v, wide_a, wide_g, back, g_n, w_l, *rest):
    rows, n, cols = a_ref.shape
    span = rows * LANES
    scratch, (send, recv) = rest[:-2], rest[-2:]
    core, place = coords()
    me = lax.axis_index("space")
    up, down = (me + 7) % 8, (me + 1) % 8
    x, y, z = place
    greet(all_partners(core, place)
          + [device_at(core, (x, (y + 2) % 4, (z + 1 - 2 * (1 - y // 2)) % 4))])
    out = Sender(send, recv)
    copies = []
    for i, ref in enumerate((g_ref, a_ref)):
        for side, (first, to) in enumerate(((rows - 1, down), (0, up))):
            copies.append(out.start(ref.at[first], rims.at[i, side], {"dp": lax.axis_index("dp"), "space": to}))
    has = (me > 0, me < 7)
    stages = [
        reduce_layer(out, core, place, o_ref.at[layer], total_ref.at[layer], *[ref.at[layer] for ref in scratch])
        for layer in range(2)
    ]
    go = lambda layer: next(stages[layer], None)
    same = lambda x: x
    silu = lambda x: (x * jax.nn.sigmoid(x)).astype(jnp.bfloat16).astype(jnp.float32)

    def widen_rows(ref, dst, change, offset):
        def body(r, carry):
            put_taps(change(ref[r].astype(jnp.float32)), dst, r + offset)
            return carry

        lax.fori_loop(0, rows, body, 0)

    def widen_rims(i, dst):
        for side in range(2):
            copies[2 * i + side].wait_recv()
            put_taps(jnp.where(has[side], rims[i, side].astype(jnp.float32), 0.0), dst, side * (rows + 1))

    def tap_rows(layer, d, cells, first):
        o_ref[layer, pl.ds(pl.multiple_of(d * 3 * n, 8), 3 * n), :] = jnp.dot(
            cells, g_n[pl.ds(pl.multiple_of(first, LANES), span), :], preferred_element_type=jnp.float32
        )

    widen_rows(g_ref, wide_g, same, 1)
    g_n[pl.ds(LANES, span), :] = wide_g[n:2 * n, LANES:LANES + span].T
    widen_rows(v_ref, wide_v, silu, 0)
    tap_rows(1, 1, wide_v[...], LANES)
    widen_rows(a_ref, wide_a, same, 1)
    for d in range(3):
        for s in range(3):
            t = 3 * d + 2 - s
            w_l[d, :, s * n:(s + 1) * n] = w_ref[:, t * n:(t + 1) * n].T
    widen_rims(0, wide_g)
    for row in (0, rows + 1):
        g_n[pl.ds(row * LANES, LANES), :] = wide_g[n:2 * n, row * LANES:(row + 1) * LANES].T

    def outer_taps(i, carry):
        tap_rows(1, 2 * i, wide_v[...], (2 - 2 * i) * LANES)
        return carry

    lax.fori_loop(0, 2, outer_taps, 0)
    go(1)
    half = span // 2

    def back_body(i, carry):
        total = None
        for d in range(3):
            lanes = pl.ds(pl.multiple_of(i * half + (2 - d) * LANES, LANES), half)
            y = jnp.dot(w_l[d], wide_g[:, lanes], preferred_element_type=jnp.float32)
            total = y if total is None else total + y
        back[:, pl.ds(pl.multiple_of(i * half, LANES), half)] = total
        return carry

    lax.fori_loop(0, 2, back_body, 0)
    go(1)

    def slope_body(r, carry):
        v = v_ref[r].astype(jnp.float32)
        s = jax.nn.sigmoid(v)
        start = pl.multiple_of(r * LANES, LANES)
        g0 = back[:, pl.ds(start, LANES)] * widened(s * (1.0 + v * (1.0 - s)))
        g_n[pl.ds(pl.multiple_of(start + LANES, LANES), LANES), :] = g0.astype(jnp.bfloat16).T
        return carry

    lax.fori_loop(0, rows, slope_body, 0)
    widen_rims(1, wide_a)

    def first_taps(d, carry):
        tap_rows(0, d, wide_a[:, pl.ds(pl.multiple_of(d * LANES, LANES), span)], LANES)
        return carry

    lax.fori_loop(0, 1, first_taps, 0)
    go(1)
    lax.fori_loop(1, 2, first_taps, 0)
    lax.fori_loop(2, 3, first_taps, 0)
    go(0)
    for _ in range(8):
        go(1)
        go(0)
    for _ in range(5):
        go(0)
    out.finish()


def gradients(inputs, preacts, cotangent, weights):
    rows, cols, n = inputs.shape
    turned = [jnp.swapaxes(x, -1, -2) for x in (inputs, preacts, cotangent, weights)]
    b16 = jnp.bfloat16
    count = 4 + 2 * (3 + 18 + 9 * 4 + 18 + 3)
    return pl.pallas_call(
        grads_kernel,
        out_shape=jax.ShapeDtypeStruct((2, 9 * n, n), jnp.float32),
        in_specs=[pl.BlockSpec(memory_space=pltpu.VMEM)] * 4,
        out_specs=pl.BlockSpec(memory_space=pltpu.VMEM),
        scratch_shapes=[pltpu.VMEM((2, 9 * n, n), jnp.float32), pltpu.VMEM((2, 2, n, cols), b16),
                        pltpu.VMEM((3 * n, rows * LANES), b16), pltpu.VMEM((3 * n, (rows + 2) * LANES), b16),
                        pltpu.VMEM((3 * n, (rows + 2) * LANES), b16), pltpu.VMEM((n, rows * LANES), jnp.float32),
                        pltpu.VMEM(((rows + 2) * LANES, n), b16), pltpu.VMEM((3, n, 3 * n), b16),
                        *reduce_scratch(n), pltpu.SemaphoreType.DMA((count,)), pltpu.SemaphoreType.DMA((count,))],
        compiler_params=pltpu.CompilerParams(vmem_limit_bytes=60 * 1000 * 1000, collective_id=0, has_side_effects=True),
    )(*turned)


NB = 64


def diag_inverse(blocks):
    n = NB
    shape = (8, 2 * n)
    row = lax.broadcasted_iota(jnp.int32, (n, 2 * n), 0)
    col = lax.broadcasted_iota(jnp.int32, (n, 2 * n), 1)
    eye = jnp.where(row + n == col, 1.0, 0.0).astype(jnp.float32)
    sub = lax.broadcasted_iota(jnp.int32, shape, 0)
    tiles = []
    for b in blocks:
        x = jnp.concatenate([b, jnp.zeros((n, n), jnp.float32)], axis=1) + eye
        tiles.append([x[8 * t:8 * t + 8] for t in range(n // 8)])
    scales = [[None] * (n // 8) for _ in blocks]
    for tj in range(n // 8):
        steps = [[] for _ in blocks]
        for m in range(len(blocks)):
            x = tiles[m][tj]
            c = [jnp.broadcast_to(x[:, 8 * tj + k:8 * tj + k + 1], shape) for k in range(8)]
            scale = jnp.zeros(shape, jnp.float32)
            for k in range(8):
                rs = lax.rsqrt(jnp.broadcast_to(c[k][k:k + 1, :], shape))
                inv = rs * rs
                scale = jnp.where(sub == k, rs, scale)
                scaled = jnp.broadcast_to(x[k:k + 1, :], shape) * inv
                factors = []
                for kk in range(k + 1, 8):
                    factor = jnp.broadcast_to(c[kk][k:k + 1, :], shape) * inv
                    c[kk] = c[kk] - c[k] * factor
                    factors.append(factor)
                if k < 7:
                    x = x - jnp.where(sub > k, c[k], 0.0) * scaled
                steps[m].append((scaled, factors))
            tiles[m][tj] = x
            scales[m][tj] = scale
        for m in range(len(blocks)):
            for t in range(tj + 1, n // 8):
                x = tiles[m][t]
                c = [jnp.broadcast_to(x[:, 8 * tj + k:8 * tj + k + 1], shape) for k in range(8)]
                for k in range(8):
                    scaled, factors = steps[m][k]
                    for kk in range(k + 1, 8):
                        c[kk] = c[kk] - c[k] * factors[kk - k - 1]
                    x = x - c[k] * scaled
                tiles[m][t] = x
    out = []
    for m in range(len(blocks)):
        w = jnp.concatenate([tiles[m][t] * scales[m][t] for t in range(n // 8)], axis=0)
        out.append(w[:, n:])
    return out


def factor_step(m_ref, k):
    count, size, _ = m_ref.shape
    o = k * NB
    linv = diag_inverse([m_ref[m, o:o + NB, o:o + NB] for m in range(count)])
    for m in range(count):
        r = jnp.dot(linv[m], m_ref[m, o:o + NB, :], precision=HIGHEST, preferred_element_type=jnp.float32)
        pieces = ([r[:, :o]] if k else []) + [linv[m]] + ([r[:, o + NB:]] if o + NB < size else [])
        rz = jnp.concatenate(pieces, axis=1)
        if o + NB == size:
            m_ref[m, o:, :] = rz
            continue
        change = lax.dot_general(r[:, o + NB:], rz, CONTRACT_ROWS, precision=HIGHEST, preferred_element_type=jnp.float32)
        old = m_ref[m, o + NB:, :]
        col = lax.broadcasted_iota(jnp.int32, old.shape, 1)
        m_ref[m, o + NB:, :] = jnp.where((col >= o) & (col < o + NB), 0.0, old) - change
        col = lax.broadcasted_iota(jnp.int32, rz.shape, 1)
        m_ref[m, o:o + NB, :] = jnp.where(col < o + NB, rz, 0.0)


def factor_kernel(s_ref, gram_ref, right_ref, rows_ref, rgram_ref, o_ref, l_ref, y_ref, m_ref, send, recv):
    core, place = coords()
    n = rgram_ref.shape[0]
    greet(all_partners(core, place))
    sibling = device_at(1 - core, place)
    out = Sender(send, recv)
    mine = o_ref.at[core]
    y_ref[core, 0] = right_ref[...]
    last = [out.start(y_ref.at[core, 0], y_ref.at[core, 0], sibling)]
    gather1a, gather1b = {}, {}
    for p in range(3):
        axis = ORDERS[p][0]
        x = place[axis]
        mine[p, pl.ds(pl.multiple_of(x * 256, 16), 256), :] = s_ref[p]
        for half in range(2):
            near, far = ring_pairs(half)
            here = view(mine, p, (x,), half)
            gather1a[p, half] = out.start(here, here, device_at(core, moved_to(place, axis, far(x))))
            gather1b[p, half] = [out.start(here, here, device_at(core, moved_to(place, axis, near(x))))]
    m_ref[0] = gram_ref[:n, :]
    m_ref[1] = rgram_ref[...]
    steps = n // NB
    for k in range(2):
        factor_step(m_ref, k)
    for p in range(3):
        axis = ORDERS[p][0]
        x = place[axis]
        for half in range(2):
            near, far = ring_pairs(half)
            gather1a[p, half].wait_recv()
            here = view(mine, p, (far(x),), half)
            gather1b[p, half].append(out.start(here, here, device_at(core, moved_to(place, axis, near(x)))))
    for k in range(2, steps - 1):
        factor_step(m_ref, k)
    for p in range(3):
        for half in range(2):
            arrived(gather1b[p, half])
        last.append(out.start(mine.at[p], mine.at[p], sibling))
    factor_step(m_ref, steps - 1)
    l_ref[core] = m_ref[0]
    last.append(out.start(l_ref.at[core], l_ref.at[core], sibling))
    y_ref[core, 1] = math.sqrt(n) * lax.dot_general(
        rows_ref[...], m_ref[1], CONTRACT_COLS, precision=HIGHEST, preferred_element_type=jnp.float32
    )
    last.append(out.start(y_ref.at[core, 1], y_ref.at[core, 1], sibling))
    arrived(last)
    out.finish()


def factor(*pieces):
    n = pieces[0].shape[-1]
    return pl.pallas_call(
        factor_kernel,
        out_shape=tuple(jax.ShapeDtypeStruct((2,) + shape + (n,), jnp.float32) for shape in ((3, 1024), (n,), (2, n))),
        in_specs=[pl.BlockSpec(memory_space=pltpu.VMEM)] * 5,
        out_specs=(pl.BlockSpec(memory_space=pltpu.VMEM),) * 3,
        scratch_shapes=[pltpu.VMEM((2, n, n), jnp.float32), pltpu.SemaphoreType.DMA((24,)), pltpu.SemaphoreType.DMA((24,))],
        compiler_params=kernel_params(2),
    )(*pieces)


def basis_kernel(full_rows, in_ref, y_ref, o_ref, dense):
    layer = pl.program_id(0)
    share = full_rows // 8

    def place_rows(block, carry):
        z, y_high = block // 2, block % 2
        for pair in range(4):
            loaded = []
            for q in (2 * pair, 2 * pair + 1):
                place = (q // 2, y_high * 2 + q % 2, z)
                for p in range(3):
                    row = 48 * q + 16 * p
                    size = min(16, share - row)
                    if size <= 0:
                        continue
                    a1, a2, a3 = ORDERS[p]
                    src = pl.multiple_of(((place[a1] * 4 + place[a2]) * 4 + place[a3]) * 16, 16)
                    loaded.append((row, size, in_ref[layer, p, pl.ds(src, size), :]))
            for row, size, value in loaded:
                dense[pl.ds(pl.multiple_of(block * share + row, 8), size), :] = value
        return carry

    lax.fori_loop(0, 8, place_rows, 0)

    def halves(x):
        high = x.astype(jnp.bfloat16)
        return high, (x - high.astype(jnp.float32)).astype(jnp.bfloat16)

    times = lambda x, y: lax.dot_general(x, y, CONTRACT_COLS, preferred_element_type=jnp.float32)
    l_high, l_low = halves(y_ref[layer] * math.sqrt(full_rows))
    for start in range(0, full_rows, 768):
        size = min(768, full_rows - start)
        high, low = halves(dense[start:start + size, :])
        o_ref[0, :, start:start + size] = times(l_high, high) + (times(l_high, low) + times(l_low, high))


def basis_of(spread_rows, both, full_rows):
    n = spread_rows.shape[-1]
    return pl.pallas_call(
        functools.partial(basis_kernel, full_rows),
        grid=(2,),
        out_shape=jax.ShapeDtypeStruct((2, n, full_rows), jnp.float32),
        in_specs=[pl.BlockSpec(memory_space=pltpu.VMEM)] * 2,
        out_specs=pl.BlockSpec((1, n, full_rows), lambda i: (i, 0, 0)),
        scratch_shapes=[pltpu.VMEM((full_rows, n), jnp.float32)],
        compiler_params=kernel_params(),
    )(spread_rows, both)


def local(inputs, preacts, cotangent, weights, left_stats, left_basis, right_stats, right_basis):
    row_share = left_stats.shape[1]
    col_share = left_stats.shape[2]
    full_rows, channels = weights.shape[1:]
    dp_index = lax.axis_index("dp")
    space_index = lax.axis_index("space")
    complete = gradients(inputs[0, 0], preacts[0, 0, 0], cotangent[0, 0], weights[0])

    row_block = lax.dynamic_slice_in_dim(complete, space_index * row_share, row_share, 1)
    col_block = lax.dynamic_slice_in_dim(complete, dp_index * col_share, col_share, 1)
    left_new = BETA * left_stats + (1.0 - BETA) * lax.dot_general(
        row_block, col_block, (((2,), (2,)), ((0,), (0,))), precision=HIGHEST
    )
    partial = lax.dot_general(left_new, left_basis, (((2,), (1,)), ((0,), (0,))), precision=HIGHEST)
    spread_rows, inverses, both = factor(*gram_of_rows(partial, complete, right_stats, right_basis))
    basis_out = jnp.swapaxes(basis_of(spread_rows, inverses, full_rows), 1, 2)
    return left_new, basis_out, both[:, 0], both[:, 1]


def solution(mesh):
    placed = (
        P("dp", None, "space", None, None),
        P(None, "dp", None, "space", None, None),
        P("dp", None, "space", None, None),
        P(),
        P(None, "space", "dp"),
        P(None, "dp", None),
        P(),
        P(),
    )
    return jax.shard_map(
        local,
        mesh=mesh,
        in_specs=placed,
        out_specs=(P(None, "space", "dp"), P(), P(), P()),
        check_vma=False,
    )
```

```python
import functools
import math

import jax
import jax.numpy as jnp
from jax import lax
from jax.experimental import pallas as pl
from jax.experimental.pallas import tpu as pltpu
from jax.sharding import PartitionSpec as P

BETA = 0.95
HIGHEST = lax.Precision.HIGHEST
CONTRACT_ROWS = (((0,), (0,)), ((), ()))
CONTRACT_COLS = (((1,), (1,)), ((), ()))
MESH = pl.DeviceIdType.MESH
ORDERS = ((0, 1, 2), (1, 2, 0), (2, 0, 1))
PADDED = 384


def kernel_params(collective_id=None):
    extra = {} if collective_id is None else {"collective_id": collective_id, "has_side_effects": True}
    return pltpu.CompilerParams(vmem_limit_bytes=50 * 1024 * 1024, **extra)

def coords():
    dp, space = lax.axis_index("dp"), lax.axis_index("space")
    core, x, y = dp % 2, (dp // 2) % 4, (space % 2) * 2 + dp // 8
    return core, (x, y, space // 2)

def device_at(core, place):
    x, y, z = place
    return {"dp": ((y % 2) * 4 + x) * 2 + core, "space": z * 2 + y // 2}

def shifted_place(place, axis, step):
    moved = list(place)
    moved[axis] = (place[axis] + step) % 4
    return tuple(moved)

def greet(partners):
    barrier = pltpu.get_barrier_semaphore()
    for partner in partners:
        pl.semaphore_signal(barrier, inc=1, device_id=partner, device_id_type=pl.DeviceIdType.MESH)
    pl.semaphore_wait(barrier, len(partners))

def add_rows(dst, dst_row, terms, rows, step):
    def body(i, carry):
        total = None
        for ref, start in terms:
            first = pl.multiple_of(start + i * step, 8)
            value = ref[pl.ds(first, step), :]
            total = value if total is None else total + value
        dst[pl.ds(pl.multiple_of(dst_row + i * step, 8), step), :] = total
        return carry
    lax.fori_loop(0, rows // step, body, 0)


class Sender:
    def __init__(self, send, recv):
        self.send, self.recv, self.copies = send, recv, []

    def start(self, src, dst, to):
        n = len(self.copies)
        copy = pltpu.make_async_remote_copy(
            src_ref=src, dst_ref=dst, send_sem=self.send.at[n], recv_sem=self.recv.at[n],
            device_id=to, device_id_type=MESH,
        )
        copy.start()
        self.copies.append(copy)
        return copy

    def finish(self):
        for copy in self.copies:
            copy.wait_send()


def arrived(copies):
    for copy in copies:
        copy.wait_recv()


def all_partners(core, place):
    partners = [device_at(1 - core, place)]
    for axis in range(3):
        for step in (1, 2, 3):
            partners.append(device_at(core, shifted_place(place, axis, step)))
    return partners


def moved_to(place, axis, value):
    moved = list(place)
    moved[axis] = value
    return tuple(moved)


def ring_pairs(half):
    near = lambda x: x + 1 - 2 * (x % 2)
    far = lambda x: 3 - x
    return (near, far) if half == 0 else (far, near)


def peers(place, axis):
    return [shifted_place(place, axis, step) for step in (1, 2, 3)]


def reduce_layer(out, core, place, part_ref, o_ref, r0, r1, s1, b, r2, c, r3, f):
    part, chunk = 480, 120
    halves = ((0, 64), (64, 56))
    mine = core * 3 * part
    sibling = device_at(1 - core, place)
    theirs = (1 - core) * 3 * part
    first = [
        out.start(part_ref.at[pl.ds(pl.multiple_of(theirs + p * part, 8), part)], r0.at[pl.ds(p * part, part)], sibling)
        for p in range(3)
    ]
    yield
    level1a, level1b, level2, level3 = {}, {}, [], []

    def rows_at(p, j, half):
        return pl.multiple_of(p * part + j * chunk + halves[half][0], 8)

    for p in range(3):
        first[p].wait_recv()
        add_rows(r0, p * part, [(r0, p * part), (part_ref, mine + p * part)], part, 96)
        axis = ORDERS[p][0]
        for half in range(2):
            near, far = ring_pairs(half)
            to = near(place[axis])
            size = halves[half][1]
            level1a[p, half] = [
                out.start(r0.at[pl.ds(rows_at(p, j, half), size)], r1.at[p, half, slot, pl.ds(0, size)],
                          device_at(core, moved_to(place, axis, to)))
                for slot, j in ((1, far(to)), (0, to))
            ]
    yield
    for p in range(3):
        axis = ORDERS[p][0]
        for half in range(2):
            near, far = ring_pairs(half)
            to = far(place[axis])
            size = halves[half][1]
            level1a[p, half][0].wait_recv()
            add_rows(s1.at[p, half], 0, [(r0, rows_at(p, to, half)), (r1.at[p, half, 1], 0)], size, size)
            level1b[p, half] = out.start(s1.at[p, half, pl.ds(0, size)], r1.at[p, half, 2, pl.ds(0, size)],
                                         device_at(core, moved_to(place, axis, to)))
    yield
    for p in range(3):
        x = place[ORDERS[p][0]]
        for half in range(2):
            level1a[p, half][1].wait_recv()
            level1b[p, half].wait_recv()
            add_rows(b.at[p], halves[half][0],
                     [(r0, rows_at(p, x, half)), (r1.at[p, half, 0], 0), (r1.at[p, half, 2], 0)],
                     halves[half][1], halves[half][1])
        b[p, chunk:, :] = jnp.zeros((8, b.shape[2]), jnp.float32)
        axis = ORDERS[p][1]
        level2.append([
            out.start(b.at[p, pl.ds(pl.multiple_of(to[axis] * 32, 8), 32)], r2.at[p, k], device_at(core, to))
            for k, to in enumerate(peers(place, axis))
        ])
    yield
    for p in range(3):
        arrived(level2[p])
        add_rows(c.at[p], 0, [(b.at[p], place[ORDERS[p][1]] * 32)] + [(r2.at[p, k], 0) for k in range(3)], 32, 32)
        axis = ORDERS[p][2]
        level3.append([
            out.start(c.at[p, pl.ds(pl.multiple_of(to[axis] * 8, 8), 8)], r3.at[p, k], device_at(core, to))
            for k, to in enumerate(peers(place, axis))
        ])
    yield
    gather3, gather2, gather1a, gather1b, last = [], [], {}, {}, []
    for p in range(3):
        arrived(level3[p])
        axis = ORDERS[p][2]
        row = pl.multiple_of(place[ORDERS[p][1]] * 32 + place[axis] * 8, 8)
        add_rows(f.at[p], row, [(c.at[p], place[axis] * 8)] + [(r3.at[p, k], 0) for k in range(3)], 8, 8)
        here = f.at[p, pl.ds(row, 8)]
        gather3.append([out.start(here, here, device_at(core, to)) for to in peers(place, axis)])
    yield
    for p in range(3):
        arrived(gather3[p])
        axis = ORDERS[p][1]
        here = f.at[p, pl.ds(pl.multiple_of(place[axis] * 32, 8), 32)]
        gather2.append([out.start(here, here, device_at(core, to)) for to in peers(place, axis)])
    yield

    def gathered(p, j, half):
        return o_ref.at[pl.ds(pl.multiple_of(mine + rows_at(p, j, half), 8), halves[half][1])]

    for p in range(3):
        arrived(gather2[p])
        axis = ORDERS[p][0]
        x = place[axis]
        add_rows(o_ref, mine + rows_at(p, x, 0), [(f.at[p], 0)], chunk, 40)
        for half in range(2):
            near, far = ring_pairs(half)
            here = gathered(p, x, half)
            gather1a[p, half] = out.start(here, here, device_at(core, moved_to(place, axis, far(x))))
            gather1b[p, half] = [out.start(here, here, device_at(core, moved_to(place, axis, near(x))))]
    yield
    for p in range(3):
        axis = ORDERS[p][0]
        x = place[axis]
        for half in range(2):
            near, far = ring_pairs(half)
            gather1a[p, half].wait_recv()
            here = gathered(p, far(x), half)
            gather1b[p, half].append(out.start(here, here, device_at(core, moved_to(place, axis, near(x)))))
    yield
    for p in range(3):
        for half in range(2):
            arrived(gather1b[p, half])
        here = o_ref.at[pl.ds(pl.multiple_of(mine + p * part, 8), part)]
        last.append(out.start(here, here, sibling))
    yield
    arrived(last)


def reduce_scratch(n):
    vm = lambda *shape: pltpu.VMEM((2,) + shape + (n,), jnp.float32)
    return [vm(1440), vm(3, 2, 3, 64), vm(3, 2, 64), vm(3, 128), vm(3, 3, 32), vm(3, 32), vm(3, 3, 8), vm(3, 128)]


def view(ref, p, places, half=None):
    row, size = 0, 1024
    for c in places:
        size = size // 4
        row = row + c * size
    if half is not None:
        size = size // 2
        row = row + half * size
    return ref.at[p, pl.ds(pl.multiple_of(row, 16), size)]


def gram_kernel(p_ref, g_ref, rs_ref, rb_ref, spread_ref, gram_ref, right_ref, rows_ref, rgram_ref,
                r0, r1, a, own_ref, b, r2, c, r3, f, r4, acc, send, recv):
    core, place = coords()
    x, y, z = place
    quads = []
    for step in range(1, 8):
        quads.append(((x + step // 2) % 4, (y // 2) * 2 + (y + step % 2) % 2, z))
    partners = all_partners(core, place)
    partners += [device_at(core, to) for step, to in enumerate(quads, 1) if step // 2 and step % 2]
    greet(partners)
    out = Sender(send, recv)
    given = p_ref.shape[1]
    first = out.start(p_ref.at[1 - core], r0, device_at(1 - core, place))
    acc[...] = jnp.zeros_like(acc)

    def right_body(i, carry):
        x = g_ref[core, pl.ds(pl.multiple_of(i * 480, 16), 480), :]
        high = x.astype(jnp.bfloat16)
        low = (x - high.astype(jnp.float32)).astype(jnp.bfloat16)
        acc[0] += lax.dot_general(high, high, CONTRACT_ROWS, preferred_element_type=jnp.float32)
        acc[1] += lax.dot_general(high, low, CONTRACT_ROWS, preferred_element_type=jnp.float32)
        return carry

    lax.fori_loop(0, 2, right_body, 0)
    first.wait_recv()
    add_rows(a, 0, [(r0, 0), (p_ref.at[core], 0)], given, 72)
    a[given:, :] = jnp.zeros((PADDED - given, a.shape[1]), jnp.float32)
    block = lambda to: pl.multiple_of((to[0] * 2 + to[1] % 2) * 48, 16)
    quarter = [out.start(a.at[pl.ds(block(to), 48)], r1.at[k], device_at(core, to)) for k, to in enumerate(quads)]
    lax.fori_loop(2, 4, right_body, 0)
    arrived(quarter)
    add_rows(own_ref, 0, [(a, block(place))] + [(r1.at[k], 0) for k in range(7)], 48, 48)
    own = own_ref[...]
    n = own.shape[1]
    spread3, spread2 = [], []
    for p in range(3):
        a1, a2, a3 = ORDERS[p]
        row = pl.multiple_of((place[a2] * 4 + place[a3]) * 16, 16)
        spread_ref[p, pl.ds(row, 16), :] = own_ref[pl.ds(16 * p, 16), :]
        here = spread_ref.at[p, pl.ds(row, 16)]
        spread3.append([out.start(here, here, device_at(core, to)) for to in peers(place, a3)])
    gram = lax.dot_general(own, own, CONTRACT_ROWS, precision=HIGHEST, preferred_element_type=jnp.float32)
    b[0, :, :] = gram[:128]
    b[1, :, :] = gram[128:256]
    b[2, :n - 256, :] = gram[256:]
    b[2, n - 256:, :] = jnp.zeros((PADDED - n, n), jnp.float32)
    level1, level2, level3, gather2, gather1 = [], [], [], [], []
    for p in range(3):
        axis = ORDERS[p][0]
        level1.append([
            out.start(b.at[p, pl.ds(pl.multiple_of(to[axis] * 32, 8), 32)], r2.at[p, k], device_at(core, to))
            for k, to in enumerate(peers(place, axis))
        ])
    lax.fori_loop(4, 5, right_body, 0)
    for p in range(3):
        arrived(level1[p])
        add_rows(c.at[p], 0, [(b.at[p], place[ORDERS[p][0]] * 32)] + [(r2.at[p, k], 0) for k in range(3)], 32, 32)
        axis = ORDERS[p][1]
        level2.append([
            out.start(c.at[p, pl.ds(pl.multiple_of(to[axis] * 8, 8), 8)], r3.at[p, k], device_at(core, to))
            for k, to in enumerate(peers(place, axis))
        ])
    for p in range(3):
        arrived(spread3[p])
        a2 = ORDERS[p][1]
        here = spread_ref.at[p, pl.ds(pl.multiple_of(place[a2] * 64, 16), 64)]
        spread2.append([out.start(here, here, device_at(core, to)) for to in peers(place, a2)])
    lax.fori_loop(5, 6, right_body, 0)
    cross = acc[1]
    right_ref[...] = BETA * rs_ref[core] + (1.0 - BETA) * (acc[0] + (cross + cross.T))
    for p in range(3):
        arrived(level2[p])
        add_rows(f.at[p], 0, [(c.at[p], place[ORDERS[p][1]] * 8)] + [(r3.at[p, k], 0) for k in range(3)], 8, 8)
        axis = ORDERS[p][2]
        level3.append([
            out.start(f.at[p], r4.at[p, k], device_at(core, to)) for k, to in enumerate(peers(place, axis))
        ])
    right_rows = jnp.dot(right_ref[...], rb_ref[core], precision=HIGHEST, preferred_element_type=jnp.float32)
    rows_ref[...] = right_rows
    for p in range(3):
        arrived(level3[p])
        axis = ORDERS[p][1]
        row = pl.multiple_of(p * 128 + place[ORDERS[p][0]] * 32 + place[axis] * 8, 8)
        add_rows(gram_ref, row, [(f.at[p], 0)] + [(r4.at[p, k], 0) for k in range(3)], 8, 8)
        here = gram_ref.at[pl.ds(row, 8)]
        gather2.append([out.start(here, here, device_at(core, to)) for to in peers(place, axis)])
    rgram_ref[...] = lax.dot_general(right_rows, right_rows, CONTRACT_ROWS, precision=HIGHEST,
                                     preferred_element_type=jnp.float32)
    for p in range(3):
        arrived(gather2[p])
        axis = ORDERS[p][0]
        here = gram_ref.at[pl.ds(pl.multiple_of(p * 128 + place[axis] * 32, 8), 32)]
        gather1.append([out.start(here, here, device_at(core, to)) for to in peers(place, axis)])
    for p in range(3):
        arrived(gather1[p])
        arrived(spread2[p])
    out.finish()


def gram_of_rows(partial, complete, right_stats, right_basis):
    n = partial.shape[-1]
    vm = lambda *s: pltpu.VMEM(s + (n,), jnp.float32)
    square = jax.ShapeDtypeStruct((n, n), jnp.float32)
    return pl.pallas_call(
        gram_kernel,
        out_shape=(jax.ShapeDtypeStruct((3, 256, n), jnp.float32), jax.ShapeDtypeStruct((PADDED, n), jnp.float32),
                   square, square, square),
        in_specs=[pl.BlockSpec(memory_space=pltpu.VMEM)] * 4,
        out_specs=(pl.BlockSpec(memory_space=pltpu.VMEM),) * 5,
        scratch_shapes=[vm(partial.shape[1]), vm(7, 48), vm(PADDED), vm(48), vm(3, 128), vm(3, 3, 32), vm(3, 32), vm(3, 3, 8),
                        vm(3, 8), vm(3, 3, 8), vm(2, n), pltpu.SemaphoreType.DMA((71,)), pltpu.SemaphoreType.DMA((71,))],
        compiler_params=kernel_params(1),
    )(partial, complete, right_stats, right_basis)


LANES = 256

def widened(x):
    return jnp.concatenate([x, jnp.zeros((x.shape[0], LANES - x.shape[1]), x.dtype)], axis=1)

def put_taps(x, dst, r):
    n = x.shape[0]
    x = widened(x)
    lanes = pl.ds(pl.multiple_of(r * LANES, LANES), LANES)
    for i, v in enumerate((pltpu.roll(x, 1, 1), x, pltpu.roll(x, LANES - 1, 1))):
        dst[pl.ds(i * n, n), lanes] = v.astype(jnp.bfloat16)

def grads_kernel(a_ref, v_ref, g_ref, w_ref, total_ref, o_ref, rims, wide_v, wide_a, wide_g, back, g_n, w_l, *rest):
    rows, n, cols = a_ref.shape
    span = rows * LANES
    scratch, (send, recv) = rest[:-2], rest[-2:]
    core, place = coords()
    me = lax.axis_index("space")
    up, down = (me + 7) % 8, (me + 1) % 8
    x, y, z = place
    greet(all_partners(core, place)
          + [device_at(core, (x, (y + 2) % 4, (z + 1 - 2 * (1 - y // 2)) % 4))])
    out = Sender(send, recv)
    copies = []
    for i, ref in enumerate((g_ref, a_ref)):
        for side, (first, to) in enumerate(((rows - 1, down), (0, up))):
            copies.append(out.start(ref.at[first], rims.at[i, side], {"dp": lax.axis_index("dp"), "space": to}))
    has = (me > 0, me < 7)
    stages = [
        reduce_layer(out, core, place, o_ref.at[layer], total_ref.at[layer], *[ref.at[layer] for ref in scratch])
        for layer in range(2)
    ]
    go = lambda layer: next(stages[layer], None)
    same = lambda x: x
    silu = lambda x: (x * jax.nn.sigmoid(x)).astype(jnp.bfloat16).astype(jnp.float32)

    def widen_rows(ref, dst, change, offset):
        def body(r, carry):
            put_taps(change(ref[r].astype(jnp.float32)), dst, r + offset)
            return carry

        lax.fori_loop(0, rows, body, 0)

    def widen_rims(i, dst):
        for side in range(2):
            copies[2 * i + side].wait_recv()
            put_taps(jnp.where(has[side], rims[i, side].astype(jnp.float32), 0.0), dst, side * (rows + 1))

    def tap_rows(layer, d, cells, first):
        o_ref[layer, pl.ds(pl.multiple_of(d * 3 * n, 8), 3 * n), :] = jnp.dot(
            cells, g_n[pl.ds(pl.multiple_of(first, LANES), span), :], preferred_element_type=jnp.float32
        )

    widen_rows(g_ref, wide_g, same, 1)
    g_n[pl.ds(LANES, span), :] = wide_g[n:2 * n, LANES:LANES + span].T
    widen_rows(v_ref, wide_v, silu, 0)
    tap_rows(1, 1, wide_v[...], LANES)
    widen_rows(a_ref, wide_a, same, 1)
    for d in range(3):
        for s in range(3):
            t = 3 * d + 2 - s
            w_l[d, :, s * n:(s + 1) * n] = w_ref[:, t * n:(t + 1) * n].T
    widen_rims(0, wide_g)
    for row in (0, rows + 1):
        g_n[pl.ds(row * LANES, LANES), :] = wide_g[n:2 * n, row * LANES:(row + 1) * LANES].T

    def outer_taps(i, carry):
        tap_rows(1, 2 * i, wide_v[...], (2 - 2 * i) * LANES)
        return carry

    lax.fori_loop(0, 2, outer_taps, 0)
    go(1)
    half = span // 2

    def back_body(i, carry):
        total = None
        for d in range(3):
            lanes = pl.ds(pl.multiple_of(i * half + (2 - d) * LANES, LANES), half)
            y = jnp.dot(w_l[d], wide_g[:, lanes], preferred_element_type=jnp.float32)
            total = y if total is None else total + y
        back[:, pl.ds(pl.multiple_of(i * half, LANES), half)] = total
        return carry

    lax.fori_loop(0, 2, back_body, 0)
    go(1)

    def slope_body(r, carry):
        v = v_ref[r].astype(jnp.float32)
        s = jax.nn.sigmoid(v)
        start = pl.multiple_of(r * LANES, LANES)
        g0 = back[:, pl.ds(start, LANES)] * widened(s * (1.0 + v * (1.0 - s)))
        g_n[pl.ds(pl.multiple_of(start + LANES, LANES), LANES), :] = g0.astype(jnp.bfloat16).T
        return carry

    lax.fori_loop(0, rows, slope_body, 0)
    widen_rims(1, wide_a)

    def first_taps(d, carry):
        tap_rows(0, d, wide_a[:, pl.ds(pl.multiple_of(d * LANES, LANES), span)], LANES)
        return carry

    lax.fori_loop(0, 1, first_taps, 0)
    go(1)
    lax.fori_loop(1, 2, first_taps, 0)
    lax.fori_loop(2, 3, first_taps, 0)
    go(0)
    for _ in range(8):
        go(1)
        go(0)
    for _ in range(5):
        go(0)
    out.finish()


def gradients(inputs, preacts, cotangent, weights):
    rows, cols, n = inputs.shape
    turned = [jnp.swapaxes(x, -1, -2) for x in (inputs, preacts, cotangent, weights)]
    b16 = jnp.bfloat16
    count = 4 + 2 * (3 + 18 + 9 * 4 + 18 + 3)
    return pl.pallas_call(
        grads_kernel,
        out_shape=jax.ShapeDtypeStruct((2, 9 * n, n), jnp.float32),
        in_specs=[pl.BlockSpec(memory_space=pltpu.VMEM)] * 4,
        out_specs=pl.BlockSpec(memory_space=pltpu.VMEM),
        scratch_shapes=[pltpu.VMEM((2, 9 * n, n), jnp.float32), pltpu.VMEM((2, 2, n, cols), b16),
                        pltpu.VMEM((3 * n, rows * LANES), b16), pltpu.VMEM((3 * n, (rows + 2) * LANES), b16),
                        pltpu.VMEM((3 * n, (rows + 2) * LANES), b16), pltpu.VMEM((n, rows * LANES), jnp.float32),
                        pltpu.VMEM(((rows + 2) * LANES, n), b16), pltpu.VMEM((3, n, 3 * n), b16),
                        *reduce_scratch(n), pltpu.SemaphoreType.DMA((count,)), pltpu.SemaphoreType.DMA((count,))],
        compiler_params=pltpu.CompilerParams(vmem_limit_bytes=60 * 1000 * 1000, collective_id=0, has_side_effects=True),
    )(*turned)


NB = 64


def diag_inverse(blocks):
    n = NB
    shape = (8, 2 * n)
    row = lax.broadcasted_iota(jnp.int32, (n, 2 * n), 0)
    col = lax.broadcasted_iota(jnp.int32, (n, 2 * n), 1)
    eye = jnp.where(row + n == col, 1.0, 0.0).astype(jnp.float32)
    sub = lax.broadcasted_iota(jnp.int32, shape, 0)
    tiles = []
    for b in blocks:
        x = jnp.concatenate([b, jnp.zeros((n, n), jnp.float32)], axis=1) + eye
        tiles.append([x[8 * t:8 * t + 8] for t in range(n // 8)])
    scales = [[None] * (n // 8) for _ in blocks]
    for tj in range(n // 8):
        steps = [[] for _ in blocks]
        for m in range(len(blocks)):
            x = tiles[m][tj]
            c = [jnp.broadcast_to(x[:, 8 * tj + k:8 * tj + k + 1], shape) for k in range(8)]
            scale = jnp.zeros(shape, jnp.float32)
            for k in range(8):
                rs = lax.rsqrt(jnp.broadcast_to(c[k][k:k + 1, :], shape))
                inv = rs * rs
                scale = jnp.where(sub == k, rs, scale)
                scaled = jnp.broadcast_to(x[k:k + 1, :], shape) * inv
                factors = []
                for kk in range(k + 1, 8):
                    factor = jnp.broadcast_to(c[kk][k:k + 1, :], shape) * inv
                    c[kk] = c[kk] - c[k] * factor
                    factors.append(factor)
                if k < 7:
                    x = x - jnp.where(sub > k, c[k], 0.0) * scaled
                steps[m].append((scaled, factors))
            tiles[m][tj] = x
            scales[m][tj] = scale
        for m in range(len(blocks)):
            for t in range(tj + 1, n // 8):
                x = tiles[m][t]
                c = [jnp.broadcast_to(x[:, 8 * tj + k:8 * tj + k + 1], shape) for k in range(8)]
                for k in range(8):
                    scaled, factors = steps[m][k]
                    for kk in range(k + 1, 8):
                        c[kk] = c[kk] - c[k] * factors[kk - k - 1]
                    x = x - c[k] * scaled
                tiles[m][t] = x
    out = []
    for m in range(len(blocks)):
        w = jnp.concatenate([tiles[m][t] * scales[m][t] for t in range(n // 8)], axis=0)
        out.append(w[:, n:])
    return out


def factor_step(m_ref, k):
    count, size, _ = m_ref.shape
    o = k * NB
    linv = diag_inverse([m_ref[m, o:o + NB, o:o + NB] for m in range(count)])
    for m in range(count):
        r = jnp.dot(linv[m], m_ref[m, o:o + NB, :], precision=HIGHEST, preferred_element_type=jnp.float32)
        pieces = ([r[:, :o]] if k else []) + [linv[m]] + ([r[:, o + NB:]] if o + NB < size else [])
        rz = jnp.concatenate(pieces, axis=1)
        if o + NB == size:
            m_ref[m, o:, :] = rz
            continue
        change = lax.dot_general(r[:, o + NB:], rz, CONTRACT_ROWS, precision=HIGHEST, preferred_element_type=jnp.float32)
        old = m_ref[m, o + NB:, :]
        col = lax.broadcasted_iota(jnp.int32, old.shape, 1)
        m_ref[m, o + NB:, :] = jnp.where((col >= o) & (col < o + NB), 0.0, old) - change
        col = lax.broadcasted_iota(jnp.int32, rz.shape, 1)
        m_ref[m, o:o + NB, :] = jnp.where(col < o + NB, rz, 0.0)


def factor_kernel(s_ref, gram_ref, right_ref, rows_ref, rgram_ref, o_ref, l_ref, y_ref, m_ref, send, recv):
    core, place = coords()
    n = rgram_ref.shape[0]
    greet(all_partners(core, place))
    sibling = device_at(1 - core, place)
    out = Sender(send, recv)
    mine = o_ref.at[core]
    y_ref[core, 0] = right_ref[...]
    last = [out.start(y_ref.at[core, 0], y_ref.at[core, 0], sibling)]
    gather1a, gather1b = {}, {}
    for p in range(3):
        axis = ORDERS[p][0]
        x = place[axis]
        mine[p, pl.ds(pl.multiple_of(x * 256, 16), 256), :] = s_ref[p]
        for half in range(2):
            near, far = ring_pairs(half)
            here = view(mine, p, (x,), half)
            gather1a[p, half] = out.start(here, here, device_at(core, moved_to(place, axis, far(x))))
            gather1b[p, half] = [out.start(here, here, device_at(core, moved_to(place, axis, near(x))))]
    m_ref[0] = gram_ref[:n, :]
    m_ref[1] = rgram_ref[...]
    steps = n // NB
    for k in range(2):
        factor_step(m_ref, k)
    for p in range(3):
        axis = ORDERS[p][0]
        x = place[axis]
        for half in range(2):
            near, far = ring_pairs(half)
            gather1a[p, half].wait_recv()
            here = view(mine, p, (far(x),), half)
            gather1b[p, half].append(out.start(here, here, device_at(core, moved_to(place, axis, near(x)))))
    for k in range(2, steps - 1):
        factor_step(m_ref, k)
    for p in range(3):
        for half in range(2):
            arrived(gather1b[p, half])
        last.append(out.start(mine.at[p], mine.at[p], sibling))
    factor_step(m_ref, steps - 1)
    l_ref[core] = m_ref[0]
    last.append(out.start(l_ref.at[core], l_ref.at[core], sibling))
    y_ref[core, 1] = math.sqrt(n) * lax.dot_general(
        rows_ref[...], m_ref[1], CONTRACT_COLS, precision=HIGHEST, preferred_element_type=jnp.float32
    )
    last.append(out.start(y_ref.at[core, 1], y_ref.at[core, 1], sibling))
    arrived(last)
    out.finish()


def factor(*pieces):
    n = pieces[0].shape[-1]
    return pl.pallas_call(
        factor_kernel,
        out_shape=tuple(jax.ShapeDtypeStruct((2,) + shape + (n,), jnp.float32) for shape in ((3, 1024), (n,), (2, n))),
        in_specs=[pl.BlockSpec(memory_space=pltpu.VMEM)] * 5,
        out_specs=(pl.BlockSpec(memory_space=pltpu.VMEM),) * 3,
        scratch_shapes=[pltpu.VMEM((2, n, n), jnp.float32), pltpu.SemaphoreType.DMA((24,)), pltpu.SemaphoreType.DMA((24,))],
        compiler_params=kernel_params(2),
    )(*pieces)


def basis_kernel(full_rows, in_ref, y_ref, o_ref, dense):
    share = full_rows // 8

    def place_rows(block, carry):
        z, y_high = block // 2, block % 2
        for pair in range(4):
            loaded = []
            for q in (2 * pair, 2 * pair + 1):
                place = (q // 2, y_high * 2 + q % 2, z)
                for p in range(3):
                    row = 48 * q + 16 * p
                    size = min(16, share - row)
                    if size <= 0:
                        continue
                    a1, a2, a3 = ORDERS[p]
                    src = pl.multiple_of(((place[a1] * 4 + place[a2]) * 4 + place[a3]) * 16, 16)
                    loaded.append((row, size, in_ref[0, p, pl.ds(src, size), :]))
            for row, size, value in loaded:
                dense[pl.ds(pl.multiple_of(block * share + row, 8), size), :] = value
        return carry

    lax.fori_loop(0, 8, place_rows, 0)

    def halves(x):
        high = x.astype(jnp.bfloat16)
        return high, (x - high.astype(jnp.float32)).astype(jnp.bfloat16)

    times = lambda x, y: lax.dot_general(x, y, CONTRACT_COLS, preferred_element_type=jnp.float32)
    l_high, l_low = halves(y_ref[0] * math.sqrt(full_rows))
    for start in range(0, full_rows, 768):
        size = min(768, full_rows - start)
        high, low = halves(dense[start:start + size, :])
        o_ref[0, :, start:start + size] = times(l_high, high) + (times(l_high, low) + times(l_low, high))


def basis_of(spread_rows, both, full_rows):
    n = spread_rows.shape[-1]
    return pl.pallas_call(
        functools.partial(basis_kernel, full_rows),
        grid=(2,),
        out_shape=jax.ShapeDtypeStruct((2, n, full_rows), jnp.float32),
        in_specs=[pl.BlockSpec((1, 3, 1024, n), lambda i: (i, 0, 0, 0)), pl.BlockSpec((1, n, n), lambda i: (i, 0, 0))],
        out_specs=pl.BlockSpec((1, n, full_rows), lambda i: (i, 0, 0)),
        scratch_shapes=[pltpu.VMEM((full_rows, n), jnp.float32)],
        compiler_params=kernel_params(),
    )(spread_rows, both)


def local(inputs, preacts, cotangent, weights, left_stats, left_basis, right_stats, right_basis):
    row_share = left_stats.shape[1]
    col_share = left_stats.shape[2]
    full_rows, channels = weights.shape[1:]
    dp_index = lax.axis_index("dp")
    space_index = lax.axis_index("space")
    complete = gradients(inputs[0, 0], preacts[0, 0, 0], cotangent[0, 0], weights[0])

    row_block = lax.dynamic_slice_in_dim(complete, space_index * row_share, row_share, 1)
    col_block = lax.dynamic_slice_in_dim(complete, dp_index * col_share, col_share, 1)
    left_new = BETA * left_stats + (1.0 - BETA) * lax.dot_general(
        row_block, col_block, (((2,), (2,)), ((0,), (0,))), precision=HIGHEST
    )
    partial = lax.dot_general(left_new, left_basis, (((2,), (1,)), ((0,), (0,))), precision=HIGHEST)
    spread_rows, inverses, both = factor(*gram_of_rows(partial, complete, right_stats, right_basis))
    basis_out = jnp.swapaxes(basis_of(spread_rows, inverses, full_rows), 1, 2)
    return left_new, basis_out, both[:, 0], both[:, 1]


def solution(mesh):
    placed = (
        P("dp", None, "space", None, None),
        P(None, "dp", None, "space", None, None),
        P("dp", None, "space", None, None),
        P(),
        P(None, "space", "dp"),
        P(None, "dp", None),
        P(),
        P(),
    )
    return jax.shard_map(
        local,
        mesh=mesh,
        in_specs=placed,
        out_specs=(P(None, "space", "dp"), P(), P(), P()),
        check_vma=False,
    )
```
